512 devices in a mesh: sector: 64 (over x, y, core), chan: 8 (over z).
Axes of the slice: x: 4, y: 8, z: 8, core: 2. Of those that a mesh axis runs over, the one named last changes fastest.
Arguments:
- surface_functions: bfloat16 [128, 256, 4096], P('sector', 'chan'), may hold values from -6 to 6, as said below
- channel_rates: float32 [128, 256], P('sector'), may hold values from 0.5 to 12
- coupling: bfloat16 [128, 256, 256], P('sector'), may hold values from -1 to 6, as said below
Outputs:
- r_inner: float32 [256, 256], P('chan', 'sector')
- r_couple: float32 [256, 256], P('chan', 'sector')
- r_outer: float32 [256, 256], P('chan', 'sector')
The draws below stay inside these ranges and needn't reach their ends.
Inputs may be any that keep to these rules, and one draw needn't show every extreme that they name: `surface_functions`: the sum of a surface function shared by all sectors and a smaller part of each sector. `coupling`: each sector's matrix is symmetric, and each diagonal entry exceeds the sum of the magnitudes of the other entries of its row.
All inputs are finite; a program needn't handle non-finite values.
Results may differ from the reference program's by a relative error of at most 0.0003.
Values may be sent and summed in bfloat16 or wider, within the bound.
No kernel may reach another device: no remote copies, remote signals or barrier semaphores. Data moves between devices by JAX's collectives and lax.ppermute only.
A program may use at most 64 MiB of HBM per device.

```python
import math
import jax
import jax.numpy as jnp
from jax import lax

CH = 256
G = 4096
SECTORS = 128


def draw_surface_functions(key, part):
    key = jax.random.fold_in(key, 11)
    shared_key, sector_key = jax.random.split(key)
    shared_part = jax.random.normal(shared_key, (CH, G), jnp.float32)
    sector_part = 0.3 * jax.random.normal(sector_key, (SECTORS, CH, G), jnp.float32)
    return jnp.clip(shared_part[None] + sector_part, -6.0, 6.0).astype(jnp.bfloat16)


def draw_coupling(key, part):
    key = jax.random.fold_in(key, 23)
    matrix_key, diagonal_key = jax.random.split(key)
    matrix_draw = jax.random.uniform(matrix_key, (SECTORS, CH, CH), jnp.float32, -1.0, 1.0)
    symmetric_part = 0.75 / CH * (matrix_draw + jnp.swapaxes(matrix_draw, 1, 2))
    diag_vals = jax.random.uniform(diagonal_key, (SECTORS, CH), jnp.float32, 1.6, 4.0)
    identity = jnp.eye(CH, dtype=jnp.float32)
    return (symmetric_part * (1.0 - identity) + diag_vals[:, :, None] * identity).astype(jnp.bfloat16)


def block_levels(key, shape, pieces, low, high):
    level, own = 1.0, jax.random.fold_in(key, 6)
    for position, shards_of in pieces:
        draws = jnp.exp(jax.random.uniform(jax.random.fold_in(own, position), (shards_of,), jnp.float32, low / len(pieces), high / len(pieces)))
        level = level * jnp.repeat(draws, shape[position] // shards_of).reshape([-1 if axis == position else 1 for axis in range(len(shape))])
    return level


def setup_inputs(seed: int = 0) -> dict:
    seeds = jax.random.split(jax.random.key(seed), 4)
    surface_functions = draw_surface_functions(jax.random.fold_in(seeds[3], 71), 0)
    channel_rates = jnp.clip(jnp.exp(math.log(12.0) - 3.1780538 * jax.random.uniform(seeds[1], (SECTORS, CH), jnp.float32) ** block_levels(seeds[1], (SECTORS, CH), ((0, 64),), -0.2, 0.2)), 0.5, 12.0)
    coupling = draw_coupling(jax.random.fold_in(seeds[3], 71), 0)
    return dict(surface_functions=surface_functions, channel_rates=channel_rates, coupling=coupling)


def sector_blocks(margin_now, rates_row, coupling_row, sector_step):
    cot_term = rates_row / jnp.tanh(rates_row * sector_step)
    csc_term = rates_row / jnp.sinh(rates_row * sector_step)
    inner_block = jnp.diag(cot_term) + 0.5 * sector_step * coupling_row.astype(jnp.float32)
    half_done = jnp.dot(margin_now, inner_block, precision=lax.Precision.HIGHEST)
    block_a = jnp.dot(half_done, margin_now.T, precision=lax.Precision.HIGHEST)
    block_b = margin_now * csc_term[None, :]
    return (block_a, block_b, inner_block)

def merge_blocks(left_part, right_part):
    a_left, b_left, c_left = left_part
    a_right, b_right, c_right = right_part
    factor = jnp.linalg.cholesky(c_left + a_right)
    solved_a = jax.scipy.linalg.cho_solve((factor, True), b_left.T)
    solved_b = jax.scipy.linalg.cho_solve((factor, True), b_right)
    new_a = a_left - jnp.dot(b_left, solved_a, precision=lax.Precision.HIGHEST)
    new_b = jnp.dot(b_left, solved_b, precision=lax.Precision.HIGHEST)
    new_c = c_right - jnp.dot(b_right.T, solved_b, precision=lax.Precision.HIGHEST)
    return (new_a, new_b, new_c)

def reference(surface_functions, channel_rates, coupling):
    sector_step = 1.0 / SECTORS
    identity = jnp.eye(CH, dtype=jnp.float32)
    opening = sector_blocks(identity, channel_rates[0], coupling[0], sector_step)

    def advance(running, sector_idx):
        margin_now = jnp.dot(surface_functions[sector_idx - 1].astype(jnp.float32), surface_functions[sector_idx].T.astype(jnp.float32), preferred_element_type=jnp.float32) / G
        blocks = sector_blocks(margin_now, channel_rates[sector_idx], coupling[sector_idx], sector_step)
        return (merge_blocks(running, blocks), None)
    combined, _ = lax.scan(advance, opening, jnp.arange(1, SECTORS, dtype=jnp.int32))
    return (combined[0], combined[1], combined[2])
```

```python
import functools

import jax
import jax.numpy as jnp
from jax import lax
from jax.experimental import pallas as pl
from jax.experimental.pallas import tpu as pltpu
from jax.sharding import PartitionSpec as P

F32 = jnp.float32
BF16 = jnp.bfloat16
NN = (((1,), (0,)), ((), ()))
NT = (((1,), (1,)), ((), ()))
TN = (((0,), (0,)), ((), ()))
SQUARINGS = 7
TOLERANCE = 1e-5
PARAMS = pltpu.CompilerParams(vmem_limit_bytes=32 * 2**20)
VMEM = pl.BlockSpec(memory_space=pltpu.VMEM)
SMEM = pl.BlockSpec(memory_space=pltpu.SMEM)


def parts(x):
    high = x.astype(BF16)
    rest = x - high.astype(F32)
    middle = rest.astype(BF16)
    return high, middle, (rest - middle.astype(F32)).astype(BF16)


def dot1(a, b, dims=NN):
    return lax.dot_general(a, b, dims, preferred_element_type=F32)


def dot3(a, b, dims=NN):
    return dot1(a[0], b[0], dims) + (dot1(a[0], b[1], dims) + dot1(a[1], b[0], dims))


def dot6(a, b, dims=NN):
    low = dot1(a[0], b[2], dims) + dot1(a[1], b[1], dims) + dot1(a[2], b[0], dims)
    return dot1(a[0], b[0], dims) + ((dot1(a[0], b[1], dims) + dot1(a[1], b[0], dims)) + low)


def grid_of(n):
    return (
        lax.broadcasted_iota(jnp.int32, (n, n), 0),
        lax.broadcasted_iota(jnp.int32, (n, n), 1),
    )


def unit(n):
    row, column = grid_of(n)
    return jnp.where(row == column, F32(1), F32(0))


def invert(d_ref, x_ref):
    n = d_ref.shape[0]
    d = d_ref[...]
    bound = jnp.max(jnp.sum(jnp.abs(d), axis=0, keepdims=True), axis=1, keepdims=True)
    alpha = 1.9 / bound
    e = unit(n) - alpha * d
    x = unit(n) + e
    for _ in range(SQUARINGS):
        rounded = e.astype(BF16)
        e = dot1(rounded, rounded)
        x = x + dot1(x.astype(BF16), e.astype(BF16))
    x_ref[...] = alpha * x
    split = parts(d_ref[...])

    def going(state):
        return jnp.logical_and(state[0] < 8, jnp.logical_not(state[1] < TOLERANCE))

    def refine(state):
        x_parts = parts(x_ref[...])
        residual = unit(n) - dot6(split, x_parts)
        x_ref[...] = x_ref[...] + dot3(x_parts, parts(residual))
        return state[0] + 1, jnp.sum(residual * residual)

    _, left = lax.while_loop(going, refine, (0, F32(1)))

    @pl.when(jnp.logical_not(left < TOLERANCE))
    def _():
        x_ref[...] = alpha * unit(n)

        def still(state):
            return jnp.logical_and(state[0] < 60, jnp.logical_not(state[1] < TOLERANCE**2))

        def careful(state):
            before = x_ref[...]
            residual = unit(n) - jnp.dot(d_ref[...], before, precision=lax.Precision.HIGHEST)
            x_ref[...] = before + jnp.dot(before, residual, precision=lax.Precision.HIGHEST)
            return state[0] + 1, jnp.sum(residual * residual)

        lax.while_loop(still, careful, (0, F32(1)))


def combine(left, right, x_ref, out_ref):
    b1, b2, x = parts(left(1)), parts(right(1)), parts(x_ref[...])
    w1, w2 = parts(dot6(b1, x)), parts(dot6(x, b2))
    new_a = left(0) - dot6(w1, b1, NT)
    new_b = dot6(w1, b2)
    new_c = right(2) - dot6(b2, w2, TN)
    out_ref[0] = new_a
    out_ref[1] = new_b
    out_ref[2] = new_c


def pack(core, out_ref, send_ref):
    n = out_ref.shape[-1]
    row, column = grid_of(n)
    last = out_ref[2]
    both = jnp.where(row >= column, out_ref[0], last)
    send_ref[0:n] = jnp.where(core == 0, both, out_ref[1])
    diagonal = jnp.sum(jnp.where(row == column, last, F32(0)), axis=0, keepdims=True)
    send_ref[n : n + 8] = jnp.broadcast_to(diagonal, (8, n))


def leaf_kernel(flags_ref, margin_ref, cot_ref, csc_ref, coupling_ref, out_ref, d_ref, x_ref, a_ref, b_ref, c_ref):
    n = d_ref.shape[0]
    row, column = grid_of(n)
    half_step = 0.5 / (2 * flags_ref[1]).astype(F32)

    def sector(s):
        margin = margin_ref[:, s].reshape(n, n)
        if s == 0:
            margin = jnp.where(flags_ref[0] == 0, unit(n), margin)
        inner = jnp.where(row == column, cot_ref[s : s + 1, :], F32(0)) + half_step * coupling_ref[s].astype(F32)
        m = parts(margin)
        a_ref[s] = dot6(parts(dot6(m, parts(inner))), m, NT)
        b_ref[s] = margin * csc_ref[s : s + 1, :]
        c_ref[s] = inner

    sector(1)
    sector(0)
    d_ref[...] = c_ref[0] + a_ref[1]
    invert(d_ref, x_ref)
    blocks = (a_ref, b_ref, c_ref)
    combine(lambda i: blocks[i][0], lambda i: blocks[i][1], x_ref, out_ref)


def leaf(flags, margin, cot, csc, coupling):
    n = coupling.shape[-1]
    return pl.pallas_call(
        leaf_kernel,
        out_shape=jax.ShapeDtypeStruct((3, n, n), F32),
        in_specs=[SMEM, VMEM, VMEM, VMEM, VMEM],
        out_specs=VMEM,
        scratch_shapes=[pltpu.VMEM((n, n), F32)] * 2 + [pltpu.VMEM((2, n, n), F32)] * 3,
        compiler_params=PARAMS,
        name="leaf",
    )(flags, margin, cot, csc, coupling)


def merge_refs(upper, own_ref, other_ref, out_ref, d_ref, x_ref):
    d_ref[...] = jnp.where(upper, other_ref[2] + own_ref[0], own_ref[2] + other_ref[0])
    invert(d_ref, x_ref)
    combine(
        lambda i: jnp.where(upper, other_ref[i], own_ref[i]),
        lambda i: jnp.where(upper, own_ref[i], other_ref[i]),
        x_ref,
        out_ref,
    )


def core_kernel(flags_ref, own_ref, other_ref, out_ref, send_ref, d_ref, x_ref):
    core = flags_ref[2]
    merge_refs(core == 1, own_ref, other_ref, out_ref, d_ref, x_ref)
    pack(core, out_ref, send_ref)


def core_merge(flags, own, other):
    n = own.shape[-1]
    return pl.pallas_call(
        core_kernel,
        out_shape=(jax.ShapeDtypeStruct((3, n, n), F32), jax.ShapeDtypeStruct((n + 8, n), F32)),
        in_specs=[SMEM, VMEM, VMEM],
        out_specs=(VMEM, VMEM),
        scratch_shapes=[pltpu.VMEM((n, n), F32)] * 2,
        compiler_params=PARAMS,
        name="core_merge",
    )(flags, own, other)


def chip_kernel(level, flags_ref, own_ref, came_ref, swapped_ref, out_ref, send_ref, d_ref, x_ref, other_ref):
    n = d_ref.shape[0]
    core = flags_ref[2]
    active = flags_ref[4 + 2 * level] == 1

    @pl.when(active)
    def _():
        row, column = grid_of(n)
        both = jnp.where(core == 0, came_ref[0:n], swapped_ref[0:n])
        diagonal = jnp.where(core == 0, came_ref[n : n + 1], swapped_ref[n : n + 1])
        turned = both.T
        other_ref[0] = jnp.where(row >= column, both, turned)
        other_ref[1] = jnp.where(core == 0, swapped_ref[0:n], came_ref[0:n])
        other_ref[2] = jnp.where(row == column, diagonal, jnp.where(row < column, both, turned))
        merge_refs(flags_ref[5 + 2 * level] == 1, own_ref, other_ref, out_ref, d_ref, x_ref)
        pack(core, out_ref, send_ref)

    @pl.when(jnp.logical_not(active))
    def _():
        out_ref[...] = own_ref[...]
        send_ref[...] = jnp.zeros_like(send_ref)


def chip_merge(level, flags, own, came, swapped):
    n = own.shape[-1]
    return pl.pallas_call(
        functools.partial(chip_kernel, level),
        out_shape=(jax.ShapeDtypeStruct((3, n, n), F32), jax.ShapeDtypeStruct((n + 8, n), F32)),
        in_specs=[SMEM, VMEM, VMEM, VMEM],
        out_specs=(VMEM, VMEM),
        scratch_shapes=[pltpu.VMEM((n, n), F32)] * 2 + [pltpu.VMEM((3, n, n), F32)],
        compiler_params=PARAMS,
        name="chip_merge",
    )(flags, own, came, swapped)


def margin_kernel(own_ref, before_ref, out_ref):
    shards, _, rows, depth = own_ref.shape
    n = shards * rows
    first = own_ref[:, 0].reshape(n, depth)
    second = own_ref[:, 1].reshape(n, depth)
    out_ref[:, 1] = dot1(first, second, NT).reshape(shards, rows, n)
    out_ref[:, 0] = dot1(before_ref[...].reshape(n, depth), first, NT).reshape(shards, rows, n)


def margin_parts(own, before):
    shards, sectors, rows, _ = own.shape
    return pl.pallas_call(
        margin_kernel,
        out_shape=jax.ShapeDtypeStruct((shards, sectors, rows, shards * rows), F32),
        in_specs=[VMEM, VMEM],
        out_specs=VMEM,
        compiler_params=PARAMS,
        name="margin_parts",
    )(own, before)


def exchange(array):
    return lax.all_to_all(array, "chan", split_axis=0, concat_axis=0, tiled=True)


YS = 8
ENDS = (0, 3, 4, 7)


def place(position):
    return position // (2 * YS), position // 2 % YS, position % 2


def spot(x, y, core):
    return (x * YS + y) * 2 + core


def levels(xs):
    result = [
        (lambda x, y: (x, y ^ 1), range(YS), ("y", 0)),
        (lambda x, y: (x, y ^ 2), ENDS, ("y", 1)),
        (lambda x, y: (x, YS - 1 - y), ENDS, ("y", 2)),
    ]
    for bit in range(xs.bit_length() - 1):
        mask = 2 ** (bit + 1) - 1
        result.append((lambda x, y, mask=mask: (x ^ mask, y), ENDS, ("x", bit)))
    return result


def per_device(surface_functions, channel_rates, coupling):
    sectors, rows, points = surface_functions.shape
    n = channel_rates.shape[1]
    shards = lax.axis_size("chan")
    count = lax.axis_size("sector")
    position = lax.axis_index("sector")
    plan = levels(count // (2 * YS))
    x, y, core = place(position)
    at_end = (y == ENDS[0]) | (y == ENDS[1]) | (y == ENDS[2]) | (y == ENDS[3])
    words = [position, jnp.int32(count), core, jnp.int32(0)]
    for _, takers, (axis, bit) in plan:
        words.append(jnp.int32(1) if len(takers) == YS else at_end.astype(jnp.int32))
        words.append((x if axis == "x" else y) >> bit & 1)
    flags = jnp.stack([jnp.asarray(word, jnp.int32) for word in words])

    step = 1.0 / (sectors * count)
    cot = channel_rates / jnp.tanh(channel_rates * step)
    csc = channel_rates / jnp.sinh(channel_rates * step)

    cut = surface_functions.reshape(sectors, rows, shards, points // shards)
    own = exchange(jnp.transpose(cut, (2, 0, 1, 3)))
    before = lax.ppermute(own[:, sectors - 1], "sector", [(i, i + 1) for i in range(count - 1)])
    partial = exchange(margin_parts(own, before))
    summed = jnp.sum(partial, axis=0) / points
    margin = exchange(jnp.broadcast_to(summed[None], (shards, sectors, rows, n)))

    packed = leaf(flags, margin, cot, csc, coupling)
    cores = [(i, i ^ 1) for i in range(count)]
    packed, send = core_merge(flags, packed, lax.ppermute(packed, "sector", cores))
    for level, (partner, takers, _) in enumerate(plan):
        pairs = []
        for i in range(count):
            xi, yi, ci = place(i)
            if yi in takers:
                pairs.append((spot(*partner(xi, yi), ci), i))
        came = lax.ppermute(send, "sector", pairs)
        swapped = lax.ppermute(came, "sector", cores)
        packed, send = chip_merge(level, flags, packed, came, swapped)

    wide = n // count
    mine = lax.dynamic_slice_in_dim(packed, lax.axis_index("chan") * rows, rows, 1)
    next_door = spot(x, y ^ 1, core)
    for_next = lax.dynamic_slice_in_dim(mine, next_door * wide, wide, 2)
    pairs = []
    for i in range(count):
        xi, yi, ci = place(i)
        if yi not in ENDS:
            pairs.append((spot(xi, yi ^ 1, ci), i))
    brought = lax.ppermute(for_next, "sector", pairs)
    result = jnp.where(at_end, lax.dynamic_slice_in_dim(mine, position * wide, wide, 2), brought)
    return (result[0], result[1], result[2])


def solution(mesh):
    placed = (P("sector", "chan", None), P("sector", None), P("sector", None, None))
    return jax.shard_map(
        per_device,
        mesh=mesh,
        in_specs=placed,
        out_specs=(P("chan", "sector"), P("chan", "sector"), P("chan", "sector")),
        check_vma=False,
    )
```

```python
import functools

import jax
import jax.numpy as jnp
from jax import lax
from jax.experimental import pallas as pl
from jax.experimental.pallas import tpu as pltpu
from jax.sharding import PartitionSpec as P

F32 = jnp.float32
BF16 = jnp.bfloat16
NN = (((1,), (0,)), ((), ()))
NT = (((1,), (1,)), ((), ()))
TN = (((0,), (0,)), ((), ()))
TOLERANCE = 1e-6
SQUARINGS = (4, 4, 5, 5, 6, 7, 8)
PARAMS = pltpu.CompilerParams(vmem_limit_bytes=32 * 2**20)
VMEM = pl.BlockSpec(memory_space=pltpu.VMEM)
SMEM = pl.BlockSpec(memory_space=pltpu.SMEM)


def parts(x):
    high = x.astype(BF16)
    rest = x - high.astype(F32)
    middle = rest.astype(BF16)
    return high, middle, (rest - middle.astype(F32)).astype(BF16)


def dot1(a, b, dims=NN):
    return lax.dot_general(a, b, dims, preferred_element_type=F32)


def dot3(a, b, dims=NN):
    return dot1(a[0], b[0], dims) + (dot1(a[0], b[1], dims) + dot1(a[1], b[0], dims))


def dot6(a, b, dims=NN):
    low = dot1(a[0], b[2], dims) + dot1(a[1], b[1], dims) + dot1(a[2], b[0], dims)
    return dot1(a[0], b[0], dims) + ((dot1(a[0], b[1], dims) + dot1(a[1], b[0], dims)) + low)


def grid_of(n):
    return (
        lax.broadcasted_iota(jnp.int32, (n, n), 0),
        lax.broadcasted_iota(jnp.int32, (n, n), 1),
    )


def unit(n):
    row, column = grid_of(n)
    return jnp.where(row == column, F32(1), F32(0))


def step_size(d):
    return 1.9 / jnp.max(jnp.sum(jnp.abs(d), axis=0, keepdims=True), axis=1, keepdims=True)


def first_inverse(d, squarings):
    n = d.shape[0]
    one = unit(n)
    alpha = step_size(d)
    e = one - alpha * d
    c = jnp.sum(jnp.sum(e * one, axis=0, keepdims=True), axis=1, keepdims=True) / n
    f = e - c * one
    p, y = 1 + c, f
    for _ in range(squarings):
        rounded = f.astype(BF16)
        f = 2 * c * f + dot1(rounded, rounded)
        c = c * c
        y = p * f + (1 + c) * y + dot1(y.astype(BF16), f.astype(BF16))
        p = p * (1 + c)
    return alpha * (p * one + y)


def newton(d_parts, x, dot):
    x_parts = parts(x)
    residual = unit(x.shape[0]) - dot(d_parts, x_parts)
    return x + dot1(x_parts[0], residual.astype(BF16)), residual


def inverse(d, squarings):
    d_parts = parts(d)
    x, _ = newton(d_parts, first_inverse(d, squarings), dot3)
    x, residual = newton(d_parts, x, dot6)
    return x, jnp.sum(residual * residual)


def finish_inverse(d_ref, x_ref, left):
    def going(state):
        return jnp.logical_and(state[0] < 8, jnp.logical_not(state[1] < TOLERANCE))

    def refine(state):
        x, residual = newton(parts(d_ref[...]), x_ref[...], dot6)
        x_ref[...] = x
        return state[0] + 1, jnp.sum(residual * residual)

    _, left = lax.while_loop(going, refine, (0, left))

    @pl.when(jnp.logical_not(left < TOLERANCE))
    def _():
        x_ref[...] = step_size(d_ref[...]) * unit(d_ref.shape[0])

        def still(state):
            return jnp.logical_and(state[0] < 60, jnp.logical_not(state[1] < TOLERANCE**2))

        def careful(state):
            before = x_ref[...]
            residual = unit(d_ref.shape[0]) - jnp.dot(d_ref[...], before, precision=lax.Precision.HIGHEST)
            x_ref[...] = before + jnp.dot(before, residual, precision=lax.Precision.HIGHEST)
            return state[0] + 1, jnp.sum(residual * residual)

        lax.while_loop(still, careful, (0, F32(1)))


def combine(left, right, x, out_ref):
    b1, b2, x = parts(left(1)), parts(right(1)), parts(x)
    w1, w2 = parts(dot6(b1, x)), parts(dot6(x, b2))
    out_ref[0] = left(0) - dot6(w1, b1, NT)
    out_ref[1] = dot6(w1, b2)
    out_ref[2] = right(2) - dot6(b2, w2, TN)


def merge_blocks(d, left, right, depth, out_ref, d_ref, x_ref, after):
    x, size = inverse(d, SQUARINGS[min(depth, len(SQUARINGS) - 1)])
    d_ref[...] = d
    x_ref[...] = x
    combine(left, right, x, out_ref)
    after()

    @pl.when(jnp.logical_not(size < TOLERANCE))
    def _():
        finish_inverse(d_ref, x_ref, size)
        combine(left, right, x_ref[...], out_ref)
        after()


def pack(core, out_ref, send_ref):
    n = out_ref.shape[-1]
    row, column = grid_of(n)
    last = out_ref[2]
    both = jnp.where(row >= column, out_ref[0], last)
    send_ref[0:n] = jnp.where(core == 0, both, out_ref[1])
    diagonal = jnp.sum(jnp.where(row == column, last, F32(0)), axis=0, keepdims=True)
    send_ref[n : n + 8] = jnp.broadcast_to(diagonal, (8, n))


def leaf_kernel(flags_ref, margin_ref, cot_ref, csc_ref, coupling_ref, out_ref, d_ref, x_ref, a_ref, b_ref, c_ref):
    n = d_ref.shape[0]
    row, column = grid_of(n)
    half_step = 0.5 / (2 * flags_ref[1]).astype(F32)

    def sector(s):
        margin = margin_ref[:, s].reshape(n, n)
        if s == 0:
            margin = jnp.where(flags_ref[0] == 0, unit(n), margin)
        inner = jnp.where(row == column, cot_ref[s : s + 1, :], F32(0)) + half_step * coupling_ref[s].astype(F32)
        m = parts(margin)
        a_ref[s] = dot6(parts(dot6(m, parts(inner))), m, NT)
        b_ref[s] = margin * csc_ref[s : s + 1, :]
        c_ref[s] = inner

    sector(1)
    sector(0)
    blocks = (a_ref, b_ref, c_ref)
    merge_blocks(
        c_ref[0] + a_ref[1],
        lambda i: blocks[i][0],
        lambda i: blocks[i][1],
        0, out_ref, d_ref, x_ref, lambda: None,
    )


def leaf(flags, margin, cot, csc, coupling):
    n = coupling.shape[-1]
    return pl.pallas_call(
        leaf_kernel,
        out_shape=jax.ShapeDtypeStruct((3, n, n), F32),
        in_specs=[SMEM, VMEM, VMEM, VMEM, VMEM],
        out_specs=VMEM,
        scratch_shapes=[pltpu.VMEM((n, n), F32)] * 2 + [pltpu.VMEM((2, n, n), F32)] * 3,
        compiler_params=PARAMS,
        name="leaf",
    )(flags, margin, cot, csc, coupling)


def merge_refs(upper, own_ref, other_ref, depth, out_ref, d_ref, x_ref, after):
    merge_blocks(
        jnp.where(upper, other_ref[2] + own_ref[0], own_ref[2] + other_ref[0]),
        lambda i: jnp.where(upper, other_ref[i], own_ref[i]),
        lambda i: jnp.where(upper, own_ref[i], other_ref[i]),
        depth, out_ref, d_ref, x_ref, after,
    )


def core_kernel(flags_ref, own_ref, other_ref, out_ref, send_ref, d_ref, x_ref):
    core = flags_ref[2]
    merge_refs(core == 1, own_ref, other_ref, 1, out_ref, d_ref, x_ref, lambda: pack(core, out_ref, send_ref))


def core_merge(flags, own, other):
    n = own.shape[-1]
    return pl.pallas_call(
        core_kernel,
        out_shape=(jax.ShapeDtypeStruct((3, n, n), F32), jax.ShapeDtypeStruct((n + 8, n), F32)),
        in_specs=[SMEM, VMEM, VMEM],
        out_specs=(VMEM, VMEM),
        scratch_shapes=[pltpu.VMEM((n, n), F32)] * 2,
        compiler_params=PARAMS,
        name="core_merge",
    )(flags, own, other)


def unpack(core, came_ref, swapped_ref, other_ref):
    n = other_ref.shape[-1]
    row, column = grid_of(n)
    both = jnp.where(core == 0, came_ref[0:n], swapped_ref[0:n])
    diagonal = jnp.where(core == 0, came_ref[n : n + 1], swapped_ref[n : n + 1])
    turned = both.T
    other_ref[0] = jnp.where(row >= column, both, turned)
    other_ref[1] = jnp.where(core == 0, swapped_ref[0:n], came_ref[0:n])
    other_ref[2] = jnp.where(row == column, diagonal, jnp.where(row < column, both, turned))


def chip_kernel(level, flags_ref, own_ref, came_ref, swapped_ref, out_ref, send_ref, d_ref, x_ref, other_ref):
    core = flags_ref[2]
    active = flags_ref[4 + 2 * level] == 1

    @pl.when(active)
    def _():
        unpack(core, came_ref, swapped_ref, other_ref)
        merge_refs(
            flags_ref[5 + 2 * level] == 1, own_ref, other_ref, level + 2, out_ref, d_ref, x_ref,
            lambda: pack(core, out_ref, send_ref),
        )

    @pl.when(jnp.logical_not(active))
    def _():
        out_ref[...] = own_ref[...]
        send_ref[...] = jnp.zeros_like(send_ref)


def chip_merge(level, flags, own, came, swapped):
    n = own.shape[-1]
    return pl.pallas_call(
        functools.partial(chip_kernel, level),
        out_shape=(jax.ShapeDtypeStruct((3, n, n), F32), jax.ShapeDtypeStruct((n + 8, n), F32)),
        in_specs=[SMEM, VMEM, VMEM, VMEM],
        out_specs=(VMEM, VMEM),
        scratch_shapes=[pltpu.VMEM((n, n), F32)] * 2 + [pltpu.VMEM((3, n, n), F32)],
        compiler_params=PARAMS,
        name="chip_merge",
    )(flags, own, came, swapped)


def last_kernel(level, flags_ref, own_ref, came_ref, swapped_ref, mine_ref, next_ref, d_ref, x_ref, other_ref, out_ref):
    n = d_ref.shape[0]
    core = flags_ref[2]
    wide, rows = mine_ref.shape[1:]
    active = flags_ref[4 + 2 * level] == 1

    def piece(chip, to_ref):
        chip_rows = pl.ds(pl.multiple_of(chip * (2 * wide), 2 * wide), 2 * wide)
        for i in range(3):
            source = other_ref if i == 1 else out_ref
            both = source[0 if i == 1 else i, chip_rows, :]
            moved = pltpu.roll(both, (n - flags_ref[3] * rows) % n, axis=1)[:, :rows]
            to_ref[i] = jnp.where(core == 0, moved[:wide], moved[wide:])

    @pl.when(active)
    def _():
        unpack(core, came_ref, swapped_ref, other_ref)
        merge_refs(
            flags_ref[5 + 2 * level] == 1, own_ref, other_ref, level + 2, out_ref, d_ref, x_ref, lambda: None
        )
        other_ref[0] = out_ref[1].T
        chip = flags_ref[0] // 2
        piece(chip, mine_ref)
        piece(chip + 1 - 2 * (chip % 2), next_ref)

    @pl.when(jnp.logical_not(active))
    def _():
        mine_ref[...] = jnp.zeros_like(mine_ref)
        next_ref[...] = jnp.zeros_like(next_ref)


def last_merge(level, flags, own, came, swapped, wide, rows):
    n = own.shape[-1]
    return pl.pallas_call(
        functools.partial(last_kernel, level),
        out_shape=(jax.ShapeDtypeStruct((3, wide, rows), F32),) * 2,
        in_specs=[SMEM, VMEM, VMEM, VMEM],
        out_specs=(VMEM, VMEM),
        scratch_shapes=[pltpu.VMEM((n, n), F32)] * 2 + [pltpu.VMEM((3, n, n), F32)] * 2,
        compiler_params=PARAMS,
        name="last_merge",
    )(flags, own, came, swapped)


def pick_kernel(flags_ref, mine_ref, brought_ref, a_ref, b_ref, c_ref):
    for i, ref in enumerate((a_ref, b_ref, c_ref)):
        ref[...] = jnp.where(flags_ref[0] == 1, mine_ref[i], brought_ref[i])


def pick(flag, mine, brought):
    return pl.pallas_call(
        pick_kernel,
        out_shape=(jax.ShapeDtypeStruct(mine.shape[1:], F32),) * 3,
        in_specs=[SMEM, VMEM, VMEM],
        out_specs=(VMEM,) * 3,
        name="pick",
    )(flag, mine, brought)


def margin_kernel(own_ref, before_ref, out_ref):
    shards, _, rows, depth = own_ref.shape
    n = shards * rows
    first = own_ref[:, 0].reshape(n, depth)
    second = own_ref[:, 1].reshape(n, depth)
    out_ref[:, 1] = dot1(first, second, NT).reshape(shards, rows, n)
    out_ref[:, 0] = dot1(before_ref[...].reshape(n, depth), first, NT).reshape(shards, rows, n)


def margin_parts(own, before):
    shards, sectors, rows, _ = own.shape
    return pl.pallas_call(
        margin_kernel,
        out_shape=jax.ShapeDtypeStruct((shards, sectors, rows, shards * rows), F32),
        in_specs=[VMEM, VMEM],
        out_specs=VMEM,
        compiler_params=PARAMS,
        name="margin_parts",
    )(own, before)


def total_kernel(points, partial_ref, out_ref):
    total = partial_ref[0]
    for shard in range(1, partial_ref.shape[0]):
        total = total + partial_ref[shard]
    total = total / points
    for shard in range(partial_ref.shape[0]):
        out_ref[shard] = total


def total_for_all(partial, points):
    return pl.pallas_call(
        functools.partial(total_kernel, points),
        out_shape=jax.ShapeDtypeStruct(partial.shape, F32),
        in_specs=[VMEM],
        out_specs=VMEM,
        compiler_params=PARAMS,
        name="total_for_all",
    )(partial)


def exchange(array):
    return lax.all_to_all(array, "chan", split_axis=0, concat_axis=0, tiled=True)


YS = 8
ENDS = (0, 3, 4, 7)


def place(position):
    return position // (2 * YS), position // 2 % YS, position % 2


def spot(x, y, core):
    return (x * YS + y) * 2 + core


def levels(xs):
    result = [
        (lambda x, y: (x, y ^ 1), range(YS), ("y", 0)),
        (lambda x, y: (x, y ^ 2), ENDS, ("y", 1)),
        (lambda x, y: (x, YS - 1 - y), ENDS, ("y", 2)),
    ]
    for bit in range(xs.bit_length() - 1):
        mask = 2 ** (bit + 1) - 1
        result.append((lambda x, y, mask=mask: (x ^ mask, y), ENDS, ("x", bit)))
    return result


def per_device(surface_functions, channel_rates, coupling):
    sectors, rows, points = surface_functions.shape
    n = channel_rates.shape[1]
    shards = lax.axis_size("chan")
    count = lax.axis_size("sector")
    position = lax.axis_index("sector")
    plan = levels(count // (2 * YS))
    x, y, core = place(position)
    at_end = (y == ENDS[0]) | (y == ENDS[1]) | (y == ENDS[2]) | (y == ENDS[3])
    words = [position, jnp.int32(count), core, lax.axis_index("chan")]
    for _, takers, (axis, bit) in plan:
        words.append(jnp.int32(1) if len(takers) == YS else at_end.astype(jnp.int32))
        words.append((x if axis == "x" else y) >> bit & 1)
    flags = jnp.stack([jnp.asarray(word, jnp.int32) for word in words])

    step = 1.0 / (sectors * count)
    cot = channel_rates / jnp.tanh(channel_rates * step)
    csc = channel_rates / jnp.sinh(channel_rates * step)

    cut = surface_functions.reshape(sectors, rows, shards, points // shards)
    own = exchange(jnp.transpose(cut, (2, 0, 1, 3)))
    before = lax.ppermute(own[:, sectors - 1], "sector", [(i, i + 1) for i in range(count - 1)])
    partial = exchange(margin_parts(own, before))
    margin = exchange(total_for_all(partial, points))

    packed = leaf(flags, margin, cot, csc, coupling)
    cores = [(i, i ^ 1) for i in range(count)]
    packed, send = core_merge(flags, packed, lax.ppermute(packed, "sector", cores))
    wide = n // count
    for level, (partner, takers, _) in enumerate(plan):
        pairs = []
        for i in range(count):
            xi, yi, ci = place(i)
            if yi in takers:
                pairs.append((spot(*partner(xi, yi), ci), i))
        came = lax.ppermute(send, "sector", pairs)
        swapped = lax.ppermute(came, "sector", cores)
        if level < len(plan) - 1:
            packed, send = chip_merge(level, flags, packed, came, swapped)
        else:
            mine, for_next = last_merge(level, flags, packed, came, swapped, wide, rows)
    pairs = []
    for i in range(count):
        xi, yi, ci = place(i)
        if yi not in ENDS:
            pairs.append((spot(xi, yi ^ 1, ci), i))
    brought = lax.ppermute(for_next, "sector", pairs)
    return tuple(block.T for block in pick(at_end.astype(jnp.int32)[None], mine, brought))


def solution(mesh):
    placed = (P("sector", "chan", None), P("sector", None), P("sector", None, None))
    return jax.shard_map(
        per_device,
        mesh=mesh,
        in_specs=placed,
        out_specs=(P("chan", "sector"), P("chan", "sector"), P("chan", "sector")),
        check_vma=False,
    )
```

```python
import functools

import jax
import jax.numpy as jnp
from jax import lax
from jax.experimental import pallas as pl
from jax.experimental.pallas import tpu as pltpu
from jax.sharding import PartitionSpec as P

F32 = jnp.float32
BF16 = jnp.bfloat16
NN = (((1,), (0,)), ((), ()))
NT = (((1,), (1,)), ((), ()))
TN = (((0,), (0,)), ((), ()))
TOLERANCE = 4e-6
SQUARINGS = (4, 4, 5, 6, 7, 8, 8)
PARAMS = pltpu.CompilerParams(vmem_limit_bytes=32 * 2**20)
VMEM = pl.BlockSpec(memory_space=pltpu.VMEM)
SMEM = pl.BlockSpec(memory_space=pltpu.SMEM)


def parts(x):
    high = x.astype(BF16)
    rest = x - high.astype(F32)
    middle = rest.astype(BF16)
    return high, middle, (rest - middle.astype(F32)).astype(BF16)


def dot1(a, b, dims=NN):
    return lax.dot_general(a, b, dims, preferred_element_type=F32)


def dot3(a, b, dims=NN):
    return dot1(a[0], b[0], dims) + (dot1(a[0], b[1], dims) + dot1(a[1], b[0], dims))


def dot6(a, b, dims=NN):
    low = dot1(a[0], b[2], dims) + dot1(a[1], b[1], dims) + dot1(a[2], b[0], dims)
    return dot1(a[0], b[0], dims) + ((dot1(a[0], b[1], dims) + dot1(a[1], b[0], dims)) + low)


def grid_of(n):
    return (
        lax.broadcasted_iota(jnp.int32, (n, n), 0),
        lax.broadcasted_iota(jnp.int32, (n, n), 1),
    )


def unit(n):
    row, column = grid_of(n)
    return jnp.where(row == column, F32(1), F32(0))


def step_size(d):
    return 1.9 / jnp.max(jnp.sum(jnp.abs(d), axis=0, keepdims=True), axis=1, keepdims=True)


def first_inverse(d, squarings):
    n = d.shape[0]
    one = unit(n)
    alpha = step_size(d)
    e = one - alpha * d
    c = jnp.sum(jnp.sum(e * one, axis=0, keepdims=True), axis=1, keepdims=True) / n
    f = e - c * one
    p, y = 1 + c, f
    for _ in range(squarings):
        rounded = f.astype(BF16)
        f = 2 * c * f + dot1(rounded, rounded)
        c = c * c
        y = p * f + (1 + c) * y + dot1(y.astype(BF16), f.astype(BF16))
        p = p * (1 + c)
    return alpha * (p * one + y)


def newton(d_parts, x, dot):
    x_parts = parts(x)
    residual = unit(x.shape[0]) - dot(d_parts, x_parts)
    return x + dot1(x_parts[0], residual.astype(BF16)), residual


def inverse(d, squarings):
    d_parts = parts(d)
    x, _ = newton(d_parts, first_inverse(d, squarings), dot3)
    x, residual = newton(d_parts, x, dot6)
    return x, jnp.sum(residual * residual)


def finish_inverse(d_ref, x_ref, left):
    def going(state):
        return jnp.logical_and(state[0] < 8, jnp.logical_not(state[1] < TOLERANCE))

    def refine(state):
        x, residual = newton(parts(d_ref[...]), x_ref[...], dot6)
        x_ref[...] = x
        return state[0] + 1, jnp.sum(residual * residual)

    _, left = lax.while_loop(going, refine, (0, left))

    @pl.when(jnp.logical_not(left < TOLERANCE))
    def _():
        x_ref[...] = step_size(d_ref[...]) * unit(d_ref.shape[0])

        def still(state):
            return jnp.logical_and(state[0] < 60, jnp.logical_not(state[1] < TOLERANCE**2))

        def careful(state):
            before = x_ref[...]
            residual = unit(d_ref.shape[0]) - jnp.dot(d_ref[...], before, precision=lax.Precision.HIGHEST)
            x_ref[...] = before + jnp.dot(before, residual, precision=lax.Precision.HIGHEST)
            return state[0] + 1, jnp.sum(residual * residual)

        lax.while_loop(still, careful, (0, F32(1)))


def combine(left, right, x, out_ref):
    b1, b2, x = parts(left(1)), parts(right(1)), parts(x)
    w1, w2 = parts(dot6(b1, x)), parts(dot6(x, b2))
    out_ref[0] = left(0) - dot6(w1, b1, NT)
    out_ref[1] = dot6(w1, b2)
    out_ref[2] = right(2) - dot6(b2, w2, TN)


def merge_blocks(d, left, right, depth, out_ref, d_ref, x_ref, after):
    x, size = inverse(d, SQUARINGS[min(depth, len(SQUARINGS) - 1)])
    d_ref[...] = d
    x_ref[...] = x
    combine(left, right, x, out_ref)
    after()

    @pl.when(jnp.logical_not(size < TOLERANCE))
    def _():
        finish_inverse(d_ref, x_ref, size)
        combine(left, right, x_ref[...], out_ref)
        after()


def pack(core, out_ref, send_ref):
    n = out_ref.shape[-1]
    row, column = grid_of(n)
    last = out_ref[2]
    both = jnp.where(row >= column, out_ref[0], last)
    send_ref[0:n] = jnp.where(core == 0, both, out_ref[1])
    diagonal = jnp.sum(jnp.where(row == column, last, F32(0)), axis=0, keepdims=True)
    send_ref[n : n + 8] = jnp.broadcast_to(diagonal, (8, n))


def leaf_kernel(flags_ref, margin_ref, cot_ref, csc_ref, coupling_ref, out_ref, d_ref, x_ref, a_ref, b_ref, c_ref):
    n = d_ref.shape[0]
    row, column = grid_of(n)
    half_step = 0.5 / (2 * flags_ref[1]).astype(F32)

    def sector(s):
        margin = margin_ref[:, s].reshape(n, n)
        if s == 0:
            margin = jnp.where(flags_ref[0] == 0, unit(n), margin)
        inner = jnp.where(row == column, cot_ref[s : s + 1, :], F32(0)) + half_step * coupling_ref[s].astype(F32)
        m = parts(margin)
        a_ref[s] = dot6(parts(dot6(m, parts(inner))), m, NT)
        b_ref[s] = margin * csc_ref[s : s + 1, :]
        c_ref[s] = inner

    sector(1)
    sector(0)
    blocks = (a_ref, b_ref, c_ref)
    merge_blocks(
        c_ref[0] + a_ref[1],
        lambda i: blocks[i][0],
        lambda i: blocks[i][1],
        0, out_ref, d_ref, x_ref, lambda: None,
    )


def leaf(flags, margin, cot, csc, coupling):
    n = coupling.shape[-1]
    return pl.pallas_call(
        leaf_kernel,
        out_shape=jax.ShapeDtypeStruct((3, n, n), F32),
        in_specs=[SMEM, VMEM, VMEM, VMEM, VMEM],
        out_specs=VMEM,
        scratch_shapes=[pltpu.VMEM((n, n), F32)] * 2 + [pltpu.VMEM((2, n, n), F32)] * 3,
        compiler_params=PARAMS,
        name="leaf",
    )(flags, margin, cot, csc, coupling)


def merge_refs(upper, own_ref, other_ref, depth, out_ref, d_ref, x_ref, after):
    merge_blocks(
        jnp.where(upper, other_ref[2] + own_ref[0], own_ref[2] + other_ref[0]),
        lambda i: jnp.where(upper, other_ref[i], own_ref[i]),
        lambda i: jnp.where(upper, own_ref[i], other_ref[i]),
        depth, out_ref, d_ref, x_ref, after,
    )


def core_kernel(flags_ref, own_ref, other_ref, out_ref, send_ref, d_ref, x_ref):
    core = flags_ref[2]
    merge_refs(core == 1, own_ref, other_ref, 1, out_ref, d_ref, x_ref, lambda: pack(core, out_ref, send_ref))


def core_merge(flags, own, other):
    n = own.shape[-1]
    return pl.pallas_call(
        core_kernel,
        out_shape=(jax.ShapeDtypeStruct((3, n, n), F32), jax.ShapeDtypeStruct((n + 8, n), F32)),
        in_specs=[SMEM, VMEM, VMEM],
        out_specs=(VMEM, VMEM),
        scratch_shapes=[pltpu.VMEM((n, n), F32)] * 2,
        compiler_params=PARAMS,
        name="core_merge",
    )(flags, own, other)


def unpack(core, came_ref, swapped_ref, other_ref):
    n = other_ref.shape[-1]
    row, column = grid_of(n)
    both = jnp.where(core == 0, came_ref[0:n], swapped_ref[0:n])
    diagonal = jnp.where(core == 0, came_ref[n : n + 1], swapped_ref[n : n + 1])
    turned = both.T
    other_ref[0] = jnp.where(row >= column, both, turned)
    other_ref[1] = jnp.where(core == 0, swapped_ref[0:n], came_ref[0:n])
    other_ref[2] = jnp.where(row == column, diagonal, jnp.where(row < column, both, turned))


def chip_kernel(level, flags_ref, own_ref, came_ref, swapped_ref, out_ref, send_ref, d_ref, x_ref, other_ref):
    core = flags_ref[2]
    active = flags_ref[4 + 2 * level] == 1

    @pl.when(active)
    def _():
        unpack(core, came_ref, swapped_ref, other_ref)
        merge_refs(
            flags_ref[5 + 2 * level] == 1, own_ref, other_ref, level + 2, out_ref, d_ref, x_ref,
            lambda: pack(core, out_ref, send_ref),
        )

    @pl.when(jnp.logical_not(active))
    def _():
        out_ref[...] = own_ref[...]
        send_ref[...] = jnp.zeros_like(send_ref)


def chip_merge(level, flags, own, came, swapped):
    n = own.shape[-1]
    return pl.pallas_call(
        functools.partial(chip_kernel, level),
        out_shape=(jax.ShapeDtypeStruct((3, n, n), F32), jax.ShapeDtypeStruct((n + 8, n), F32)),
        in_specs=[SMEM, VMEM, VMEM, VMEM],
        out_specs=(VMEM, VMEM),
        scratch_shapes=[pltpu.VMEM((n, n), F32)] * 2 + [pltpu.VMEM((3, n, n), F32)],
        compiler_params=PARAMS,
        name="chip_merge",
    )(flags, own, came, swapped)


def last_kernel(level, flags_ref, own_ref, came_ref, swapped_ref, mine_ref, next_ref, d_ref, x_ref, other_ref, out_ref):
    n = d_ref.shape[0]
    core = flags_ref[2]
    wide, rows = mine_ref.shape[1:]
    active = flags_ref[4 + 2 * level] == 1

    def piece(chip, to_ref):
        chip_rows = pl.ds(pl.multiple_of(chip * (2 * wide), 2 * wide), 2 * wide)
        for i in range(3):
            source = other_ref if i == 1 else out_ref
            both = source[0 if i == 1 else i, chip_rows, :]
            moved = pltpu.roll(both, (n - flags_ref[3] * rows) % n, axis=1)[:, :rows]
            to_ref[i] = jnp.where(core == 0, moved[:wide], moved[wide:])

    @pl.when(active)
    def _():
        unpack(core, came_ref, swapped_ref, other_ref)
        merge_refs(
            flags_ref[5 + 2 * level] == 1, own_ref, other_ref, level + 2, out_ref, d_ref, x_ref, lambda: None
        )
        other_ref[0] = out_ref[1].T
        chip = flags_ref[0] // 2
        piece(chip, mine_ref)
        piece(chip + 1 - 2 * (chip % 2), next_ref)

    @pl.when(jnp.logical_not(active))
    def _():
        mine_ref[...] = jnp.zeros_like(mine_ref)
        next_ref[...] = jnp.zeros_like(next_ref)


def last_merge(level, flags, own, came, swapped, wide, rows):
    n = own.shape[-1]
    return pl.pallas_call(
        functools.partial(last_kernel, level),
        out_shape=(jax.ShapeDtypeStruct((3, wide, rows), F32),) * 2,
        in_specs=[SMEM, VMEM, VMEM, VMEM],
        out_specs=(VMEM, VMEM),
        scratch_shapes=[pltpu.VMEM((n, n), F32)] * 2 + [pltpu.VMEM((3, n, n), F32)] * 2,
        compiler_params=PARAMS,
        name="last_merge",
    )(flags, own, came, swapped)


def pick_kernel(flags_ref, mine_ref, brought_ref, a_ref, b_ref, c_ref):
    for i, ref in enumerate((a_ref, b_ref, c_ref)):
        ref[...] = jnp.where(flags_ref[0] == 1, mine_ref[i], brought_ref[i])


def pick(flag, mine, brought):
    return pl.pallas_call(
        pick_kernel,
        out_shape=(jax.ShapeDtypeStruct(mine.shape[1:], F32),) * 3,
        in_specs=[SMEM, VMEM, VMEM],
        out_specs=(VMEM,) * 3,
        name="pick",
    )(flag, mine, brought)


def margin_kernel(own_ref, before_ref, out_ref):
    shards, _, rows, depth = own_ref.shape
    n = shards * rows
    first = own_ref[:, 0].reshape(n, depth)
    second = own_ref[:, 1].reshape(n, depth)
    out_ref[:, 1] = dot1(first, second, NT).reshape(shards, rows, n)
    out_ref[:, 0] = dot1(before_ref[...].reshape(n, depth), first, NT).reshape(shards, rows, n)


def margin_parts(own, before):
    shards, sectors, rows, _ = own.shape
    return pl.pallas_call(
        margin_kernel,
        out_shape=jax.ShapeDtypeStruct((shards, sectors, rows, shards * rows), F32),
        in_specs=[VMEM, VMEM],
        out_specs=VMEM,
        compiler_params=PARAMS,
        name="margin_parts",
    )(own, before)


def total_kernel(points, partial_ref, out_ref):
    total = partial_ref[0]
    for shard in range(1, partial_ref.shape[0]):
        total = total + partial_ref[shard]
    total = total / points
    for shard in range(partial_ref.shape[0]):
        out_ref[shard] = total


def total_for_all(partial, points):
    return pl.pallas_call(
        functools.partial(total_kernel, points),
        out_shape=jax.ShapeDtypeStruct(partial.shape, F32),
        in_specs=[VMEM],
        out_specs=VMEM,
        compiler_params=PARAMS,
        name="total_for_all",
    )(partial)


def exchange(array):
    return lax.all_to_all(array, "chan", split_axis=0, concat_axis=0, tiled=True)


YS = 8
ENDS = (0, 3, 4, 7)


def place(position):
    return position // (2 * YS), position // 2 % YS, position % 2


def spot(x, y, core):
    return (x * YS + y) * 2 + core


def levels(xs):
    result = [
        (lambda x, y: (x, y ^ 1), range(YS), ("y", 0)),
        (lambda x, y: (x, y ^ 2), ENDS, ("y", 1)),
        (lambda x, y: (x, YS - 1 - y), ENDS, ("y", 2)),
    ]
    for bit in range(xs.bit_length() - 1):
        mask = 2 ** (bit + 1) - 1
        result.append((lambda x, y, mask=mask: (x ^ mask, y), ENDS, ("x", bit)))
    return result


def per_device(surface_functions, channel_rates, coupling):
    sectors, rows, points = surface_functions.shape
    n = channel_rates.shape[1]
    shards = lax.axis_size("chan")
    count = lax.axis_size("sector")
    position = lax.axis_index("sector")
    plan = levels(count // (2 * YS))
    x, y, core = place(position)
    at_end = (y == ENDS[0]) | (y == ENDS[1]) | (y == ENDS[2]) | (y == ENDS[3])
    words = [position, jnp.int32(count), core, lax.axis_index("chan")]
    for _, takers, (axis, bit) in plan:
        words.append(jnp.int32(1) if len(takers) == YS else at_end.astype(jnp.int32))
        words.append((x if axis == "x" else y) >> bit & 1)
    flags = jnp.stack([jnp.asarray(word, jnp.int32) for word in words])

    step = 1.0 / (sectors * count)
    cot = channel_rates / jnp.tanh(channel_rates * step)
    csc = channel_rates / jnp.sinh(channel_rates * step)

    cut = surface_functions.reshape(sectors, rows, shards, points // shards)
    own = exchange(jnp.transpose(cut, (2, 0, 1, 3)))
    before = lax.ppermute(own[:, sectors - 1], "sector", [(i, i + 1) for i in range(count - 1)])
    partial = exchange(margin_parts(own, before))
    ready = total_for_all(partial, points)
    ready, flags, cot, csc = lax.optimization_barrier((ready, flags, cot, csc))
    margin = exchange(ready)

    packed = leaf(flags, margin, cot, csc, coupling)
    cores = [(i, i ^ 1) for i in range(count)]
    packed, send = core_merge(flags, packed, lax.ppermute(packed, "sector", cores))
    wide = n // count
    for level, (partner, takers, _) in enumerate(plan):
        pairs = []
        for i in range(count):
            xi, yi, ci = place(i)
            if yi in takers:
                pairs.append((spot(*partner(xi, yi), ci), i))
        came = lax.ppermute(send, "sector", pairs)
        swapped = lax.ppermute(came, "sector", cores)
        if level < len(plan) - 1:
            packed, send = chip_merge(level, flags, packed, came, swapped)
        else:
            mine, for_next = last_merge(level, flags, packed, came, swapped, wide, rows)
    pairs = []
    for i in range(count):
        xi, yi, ci = place(i)
        if yi not in ENDS:
            pairs.append((spot(xi, yi ^ 1, ci), i))
    brought = lax.ppermute(for_next, "sector", pairs)
    return tuple(block.T for block in pick(at_end.astype(jnp.int32)[None], mine, brought))


def solution(mesh):
    placed = (P("sector", "chan", None), P("sector", None), P("sector", None, None))
    return jax.shard_map(
        per_device,
        mesh=mesh,
        in_specs=placed,
        out_specs=(P("chan", "sector"), P("chan", "sector"), P("chan", "sector")),
        check_vma=False,
    )
```

```python
import functools

import jax
import jax.numpy as jnp
from jax import lax
from jax.experimental import pallas as pl
from jax.experimental.pallas import tpu as pltpu
from jax.sharding import PartitionSpec as P

F32 = jnp.float32
BF16 = jnp.bfloat16
NN = (((1,), (0,)), ((), ()))
NT = (((1,), (1,)), ((), ()))
TN = (((0,), (0,)), ((), ()))
TOLERANCE = 1e-5
STEPS = 8
SQUARINGS = (4, 4, 5, 6, 7, 8, 8)
PARAMS = pltpu.CompilerParams(vmem_limit_bytes=32 * 2**20)
VMEM = pl.BlockSpec(memory_space=pltpu.VMEM)
SMEM = pl.BlockSpec(memory_space=pltpu.SMEM)


def parts(x):
    high = x.astype(BF16)
    rest = x - high.astype(F32)
    middle = rest.astype(BF16)
    return high, middle, (rest - middle.astype(F32)).astype(BF16)


def dot1(a, b, dims=NN):
    return lax.dot_general(a, b, dims, preferred_element_type=F32)


def dot3(a, b, dims=NN):
    return dot1(a[0], b[0], dims) + (dot1(a[0], b[1], dims) + dot1(a[1], b[0], dims))


def dot6(a, b, dims=NN):
    low = dot1(a[0], b[2], dims) + dot1(a[1], b[1], dims) + dot1(a[2], b[0], dims)
    return dot1(a[0], b[0], dims) + ((dot1(a[0], b[1], dims) + dot1(a[1], b[0], dims)) + low)


def grid_of(n):
    return (
        lax.broadcasted_iota(jnp.int32, (n, n), 0),
        lax.broadcasted_iota(jnp.int32, (n, n), 1),
    )


def unit(n):
    row, column = grid_of(n)
    return jnp.where(row == column, F32(1), F32(0))


def step_size(d):
    return 1.9 / jnp.max(jnp.sum(jnp.abs(d), axis=0, keepdims=True), axis=1, keepdims=True)


def first_inverse(d, squarings):
    n = d.shape[0]
    one = unit(n)
    alpha = step_size(d)
    e = one - alpha * d
    c = jnp.sum(jnp.sum(e * one, axis=0, keepdims=True), axis=1, keepdims=True) / n
    f = e - c * one
    p, y = 1 + c, f
    for _ in range(squarings):
        rounded = f.astype(BF16)
        f = 2 * c * f + dot1(rounded, rounded)
        c = c * c
        y = p * f + (1 + c) * y + dot1(y.astype(BF16), f.astype(BF16))
        p = p * (1 + c)
    return alpha * (p * one + y)


def newton(d_parts, x, dot):
    x_parts = parts(x)
    residual = unit(x.shape[0]) - dot(d_parts, x_parts)
    return x + dot3(x_parts, parts(residual)), residual


def combine(left, right, x, out_ref):
    b1, b2, x = parts(left(1)), parts(right(1)), parts(x)
    w1, w2 = parts(dot6(b1, x)), parts(dot6(x, b2))
    out_ref[0] = left(0) - dot6(w1, b1, NT)
    out_ref[1] = dot6(w1, b2)
    out_ref[2] = right(2) - dot6(b2, w2, TN)


def merge_blocks(d, left, right, depth, out_ref, d_ref, x_ref, after):
    d_ref[...] = d
    x_ref[...], _ = newton(parts(d), first_inverse(d, SQUARINGS[min(depth, len(SQUARINGS) - 1)]), dot3)

    def going(state):
        return jnp.logical_and(state[0] < 9 * STEPS, jnp.logical_not(state[1] < TOLERANCE))

    def again(state):
        @pl.when(state[0] == STEPS)
        def _():
            x_ref[...] = step_size(d_ref[...]) * unit(d_ref.shape[0])

        x, residual = newton(parts(d_ref[...]), x_ref[...], dot6)
        x_ref[...] = x
        combine(left, right, x, out_ref)
        after()
        return state[0] + 1, jnp.sum(residual * residual)

    lax.while_loop(going, again, (0, F32(1)))


def pack(core, out_ref, send_ref):
    n = out_ref.shape[-1]
    row, column = grid_of(n)
    last = out_ref[2]
    both = jnp.where(row >= column, out_ref[0], last)
    send_ref[0:n] = jnp.where(core == 0, both, out_ref[1])
    diagonal = jnp.sum(jnp.where(row == column, last, F32(0)), axis=0, keepdims=True)
    send_ref[n : n + 8] = jnp.broadcast_to(diagonal, (8, n))


def leaf_kernel(flags_ref, margin_ref, cot_ref, csc_ref, coupling_ref, out_ref, d_ref, x_ref, a_ref, b_ref, c_ref):
    n = d_ref.shape[0]
    row, column = grid_of(n)
    half_step = 0.5 / (2 * flags_ref[1]).astype(F32)

    def sector(s):
        margin = margin_ref[:, s].reshape(n, n)
        if s == 0:
            margin = jnp.where(flags_ref[0] == 0, unit(n), margin)
        inner = jnp.where(row == column, cot_ref[s : s + 1, :], F32(0)) + half_step * coupling_ref[s].astype(F32)
        m = parts(margin)
        a_ref[s] = dot6(parts(dot6(m, parts(inner))), m, NT)
        b_ref[s] = margin * csc_ref[s : s + 1, :]
        c_ref[s] = inner

    sector(1)
    sector(0)
    blocks = (a_ref, b_ref, c_ref)
    merge_blocks(
        c_ref[0] + a_ref[1],
        lambda i: blocks[i][0],
        lambda i: blocks[i][1],
        0, out_ref, d_ref, x_ref, lambda: None,
    )


def leaf(flags, margin, cot, csc, coupling):
    n = coupling.shape[-1]
    return pl.pallas_call(
        leaf_kernel,
        out_shape=jax.ShapeDtypeStruct((3, n, n), F32),
        in_specs=[SMEM, VMEM, VMEM, VMEM, VMEM],
        out_specs=VMEM,
        scratch_shapes=[pltpu.VMEM((n, n), F32)] * 2 + [pltpu.VMEM((2, n, n), F32)] * 3,
        compiler_params=PARAMS,
        name="leaf",
    )(flags, margin, cot, csc, coupling)


def merge_refs(upper, own_ref, other_ref, depth, out_ref, d_ref, x_ref, after):
    merge_blocks(
        jnp.where(upper, other_ref[2] + own_ref[0], own_ref[2] + other_ref[0]),
        lambda i: jnp.where(upper, other_ref[i], own_ref[i]),
        lambda i: jnp.where(upper, own_ref[i], other_ref[i]),
        depth, out_ref, d_ref, x_ref, after,
    )


def core_kernel(flags_ref, own_ref, other_ref, out_ref, send_ref, d_ref, x_ref):
    core = flags_ref[2]
    merge_refs(core == 1, own_ref, other_ref, 1, out_ref, d_ref, x_ref, lambda: pack(core, out_ref, send_ref))


def core_merge(flags, own, other):
    n = own.shape[-1]
    return pl.pallas_call(
        core_kernel,
        out_shape=(jax.ShapeDtypeStruct((3, n, n), F32), jax.ShapeDtypeStruct((n + 8, n), F32)),
        in_specs=[SMEM, VMEM, VMEM],
        out_specs=(VMEM, VMEM),
        scratch_shapes=[pltpu.VMEM((n, n), F32)] * 2,
        compiler_params=PARAMS,
        name="core_merge",
    )(flags, own, other)


def unpack(core, came_ref, swapped_ref, other_ref):
    n = other_ref.shape[-1]
    row, column = grid_of(n)
    both = jnp.where(core == 0, came_ref[0:n], swapped_ref[0:n])
    diagonal = jnp.where(core == 0, came_ref[n : n + 1], swapped_ref[n : n + 1])
    turned = both.T
    other_ref[0] = jnp.where(row >= column, both, turned)
    other_ref[1] = jnp.where(core == 0, swapped_ref[0:n], came_ref[0:n])
    other_ref[2] = jnp.where(row == column, diagonal, jnp.where(row < column, both, turned))


def chip_kernel(level, flags_ref, own_ref, came_ref, swapped_ref, out_ref, send_ref, d_ref, x_ref, other_ref):
    core = flags_ref[2]
    active = flags_ref[4 + 2 * level] == 1

    @pl.when(active)
    def _():
        unpack(core, came_ref, swapped_ref, other_ref)
        merge_refs(
            flags_ref[5 + 2 * level] == 1, own_ref, other_ref, level + 2, out_ref, d_ref, x_ref,
            lambda: pack(core, out_ref, send_ref),
        )

    @pl.when(jnp.logical_not(active))
    def _():
        out_ref[...] = own_ref[...]
        send_ref[...] = jnp.zeros_like(send_ref)


def chip_merge(level, flags, own, came, swapped):
    n = own.shape[-1]
    return pl.pallas_call(
        functools.partial(chip_kernel, level),
        out_shape=(jax.ShapeDtypeStruct((3, n, n), F32), jax.ShapeDtypeStruct((n + 8, n), F32)),
        in_specs=[SMEM, VMEM, VMEM, VMEM],
        out_specs=(VMEM, VMEM),
        scratch_shapes=[pltpu.VMEM((n, n), F32)] * 2 + [pltpu.VMEM((3, n, n), F32)],
        compiler_params=PARAMS,
        name="chip_merge",
    )(flags, own, came, swapped)


def last_kernel(level, flags_ref, own_ref, came_ref, swapped_ref, mine_ref, next_ref, d_ref, x_ref, other_ref, out_ref):
    n = d_ref.shape[0]
    core = flags_ref[2]
    wide, rows = mine_ref.shape[1:]
    active = flags_ref[4 + 2 * level] == 1

    def piece(chip, to_ref):
        chip_rows = pl.ds(pl.multiple_of(chip * (2 * wide), 2 * wide), 2 * wide)
        for i in range(3):
            source = other_ref if i == 1 else out_ref
            both = source[0 if i == 1 else i, chip_rows, :]
            moved = pltpu.roll(both, (n - flags_ref[3] * rows) % n, axis=1)[:, :rows]
            to_ref[i] = jnp.where(core == 0, moved[:wide], moved[wide:])

    @pl.when(active)
    def _():
        unpack(core, came_ref, swapped_ref, other_ref)
        merge_refs(
            flags_ref[5 + 2 * level] == 1, own_ref, other_ref, level + 2, out_ref, d_ref, x_ref, lambda: None
        )
        other_ref[0] = out_ref[1].T
        chip = flags_ref[0] // 2
        piece(chip, mine_ref)
        piece(chip + 1 - 2 * (chip % 2), next_ref)

    @pl.when(jnp.logical_not(active))
    def _():
        mine_ref[...] = jnp.zeros_like(mine_ref)
        next_ref[...] = jnp.zeros_like(next_ref)


def last_merge(level, flags, own, came, swapped, wide, rows):
    n = own.shape[-1]
    return pl.pallas_call(
        functools.partial(last_kernel, level),
        out_shape=(jax.ShapeDtypeStruct((3, wide, rows), F32),) * 2,
        in_specs=[SMEM, VMEM, VMEM, VMEM],
        out_specs=(VMEM, VMEM),
        scratch_shapes=[pltpu.VMEM((n, n), F32)] * 2 + [pltpu.VMEM((3, n, n), F32)] * 2,
        compiler_params=PARAMS,
        name="last_merge",
    )(flags, own, came, swapped)


def pick_kernel(flags_ref, mine_ref, brought_ref, a_ref, b_ref, c_ref):
    for i, ref in enumerate((a_ref, b_ref, c_ref)):
        ref[...] = jnp.where(flags_ref[0] == 1, mine_ref[i], brought_ref[i])


def pick(flag, mine, brought):
    return pl.pallas_call(
        pick_kernel,
        out_shape=(jax.ShapeDtypeStruct(mine.shape[1:], F32),) * 3,
        in_specs=[SMEM, VMEM, VMEM],
        out_specs=(VMEM,) * 3,
        name="pick",
    )(flag, mine, brought)


def margin_kernel(own_ref, before_ref, out_ref):
    shards, _, rows, depth = own_ref.shape
    n = shards * rows
    first = own_ref[:, 0].reshape(n, depth)
    second = own_ref[:, 1].reshape(n, depth)
    out_ref[:, 1] = dot1(first, second, NT).reshape(shards, rows, n)
    out_ref[:, 0] = dot1(before_ref[...].reshape(n, depth), first, NT).reshape(shards, rows, n)


def margin_parts(own, before):
    shards, sectors, rows, _ = own.shape
    return pl.pallas_call(
        margin_kernel,
        out_shape=jax.ShapeDtypeStruct((shards, sectors, rows, shards * rows), F32),
        in_specs=[VMEM, VMEM],
        out_specs=VMEM,
        compiler_params=PARAMS,
        name="margin_parts",
    )(own, before)


def total_kernel(points, partial_ref, out_ref):
    total = partial_ref[0]
    for shard in range(1, partial_ref.shape[0]):
        total = total + partial_ref[shard]
    total = total / points
    for shard in range(partial_ref.shape[0]):
        out_ref[shard] = total


def total_for_all(partial, points):
    return pl.pallas_call(
        functools.partial(total_kernel, points),
        out_shape=jax.ShapeDtypeStruct(partial.shape, F32),
        in_specs=[VMEM],
        out_specs=VMEM,
        compiler_params=PARAMS,
        name="total_for_all",
    )(partial)


def exchange(array):
    return lax.all_to_all(array, "chan", split_axis=0, concat_axis=0, tiled=True)


YS = 8
ENDS = (0, 3, 4, 7)


def place(position):
    return position // (2 * YS), position // 2 % YS, position % 2


def spot(x, y, core):
    return (x * YS + y) * 2 + core


def levels(xs):
    result = [
        (lambda x, y: (x, y ^ 1), range(YS), ("y", 0)),
        (lambda x, y: (x, y ^ 2), ENDS, ("y", 1)),
        (lambda x, y: (x, YS - 1 - y), ENDS, ("y", 2)),
    ]
    for bit in range(xs.bit_length() - 1):
        mask = 2 ** (bit + 1) - 1
        result.append((lambda x, y, mask=mask: (x ^ mask, y), ENDS, ("x", bit)))
    return result


def per_device(surface_functions, channel_rates, coupling):
    sectors, rows, points = surface_functions.shape
    n = channel_rates.shape[1]
    shards = lax.axis_size("chan")
    count = lax.axis_size("sector")
    position = lax.axis_index("sector")
    plan = levels(count // (2 * YS))
    x, y, core = place(position)
    at_end = (y == ENDS[0]) | (y == ENDS[1]) | (y == ENDS[2]) | (y == ENDS[3])
    words = [position, jnp.int32(count), core, lax.axis_index("chan")]
    for _, takers, (axis, bit) in plan:
        words.append(jnp.int32(1) if len(takers) == YS else at_end.astype(jnp.int32))
        words.append((x if axis == "x" else y) >> bit & 1)
    flags = jnp.stack([jnp.asarray(word, jnp.int32) for word in words])

    step = 1.0 / (sectors * count)
    cot = channel_rates / jnp.tanh(channel_rates * step)
    csc = channel_rates / jnp.sinh(channel_rates * step)

    cut = surface_functions.reshape(sectors, rows, shards, points // shards)
    own = exchange(jnp.transpose(cut, (2, 0, 1, 3)))
    before = lax.ppermute(own[:, sectors - 1], "sector", [(i, i + 1) for i in range(count - 1)])
    partial = exchange(margin_parts(own, before))
    ready = total_for_all(partial, points)
    ready, flags, cot, csc = lax.optimization_barrier((ready, flags, cot, csc))
    margin = exchange(ready)

    packed = leaf(flags, margin, cot, csc, coupling)
    cores = [(i, i ^ 1) for i in range(count)]
    packed, send = core_merge(flags, packed, lax.ppermute(packed, "sector", cores))
    wide = n // count
    for level, (partner, takers, _) in enumerate(plan):
        pairs = []
        for i in range(count):
            xi, yi, ci = place(i)
            if yi in takers:
                pairs.append((spot(*partner(xi, yi), ci), i))
        came = lax.ppermute(send, "sector", pairs)
        swapped = lax.ppermute(came, "sector", cores)
        if level < len(plan) - 1:
            packed, send = chip_merge(level, flags, packed, came, swapped)
        else:
            mine, for_next = last_merge(level, flags, packed, came, swapped, wide, rows)
    pairs = []
    for i in range(count):
        xi, yi, ci = place(i)
        if yi not in ENDS:
            pairs.append((spot(xi, yi ^ 1, ci), i))
    brought = lax.ppermute(for_next, "sector", pairs)
    return tuple(block.T for block in pick(at_end.astype(jnp.int32)[None], mine, brought))


def solution(mesh):
    placed = (P("sector", "chan", None), P("sector", None), P("sector", None, None))
    return jax.shard_map(
        per_device,
        mesh=mesh,
        in_specs=placed,
        out_specs=(P("chan", "sector"), P("chan", "sector"), P("chan", "sector")),
        check_vma=False,
    )
```

```python
import functools

import jax
import jax.numpy as jnp
from jax import lax
from jax.experimental import pallas as pl
from jax.experimental.pallas import tpu as pltpu
from jax.sharding import PartitionSpec as P

F32 = jnp.float32
BF16 = jnp.bfloat16
NN = (((1,), (0,)), ((), ()))
NT = (((1,), (1,)), ((), ()))
TN = (((0,), (0,)), ((), ()))
TOLERANCE = 1e-5
STEPS = 8
SQUARINGS = (4, 4, 5, 6, 7, 8, 8)
PARAMS = pltpu.CompilerParams(vmem_limit_bytes=32 * 2**20)
VMEM = pl.BlockSpec(memory_space=pltpu.VMEM)
SMEM = pl.BlockSpec(memory_space=pltpu.SMEM)


def parts(x):
    high = x.astype(BF16)
    rest = x - high.astype(F32)
    middle = rest.astype(BF16)
    return high, middle, (rest - middle.astype(F32)).astype(BF16)


def dot1(a, b, dims=NN):
    return lax.dot_general(a, b, dims, preferred_element_type=F32)


def dot3(a, b, dims=NN):
    return dot1(a[0], b[0], dims) + (dot1(a[0], b[1], dims) + dot1(a[1], b[0], dims))


def dot6(a, b, dims=NN):
    low = dot1(a[0], b[2], dims) + dot1(a[1], b[1], dims) + dot1(a[2], b[0], dims)
    return dot1(a[0], b[0], dims) + ((dot1(a[0], b[1], dims) + dot1(a[1], b[0], dims)) + low)


def grid_of(n):
    return (
        lax.broadcasted_iota(jnp.int32, (n, n), 0),
        lax.broadcasted_iota(jnp.int32, (n, n), 1),
    )


def unit(n):
    row, column = grid_of(n)
    return jnp.where(row == column, F32(1), F32(0))


def step_size(d):
    return 1.9 / jnp.max(jnp.sum(jnp.abs(d), axis=0, keepdims=True), axis=1, keepdims=True)


def first_inverse(d, squarings):
    n = d.shape[0]
    one = unit(n)
    alpha = step_size(d)
    e = one - alpha * d
    c = jnp.sum(jnp.sum(e * one, axis=0, keepdims=True), axis=1, keepdims=True) / n
    f = e - c * one
    p, y = 1 + c, f
    for _ in range(squarings):
        rounded = f.astype(BF16)
        f = 2 * c * f + dot1(rounded, rounded)
        c = c * c
        y = p * f + (1 + c) * y + dot1(y.astype(BF16), f.astype(BF16))
        p = p * (1 + c)
    return alpha * (p * one + y)


def newton(d_parts, x, dot):
    x_parts = parts(x)
    residual = unit(x.shape[0]) - dot(d_parts, x_parts)
    return x + dot3(x_parts, parts(residual)), residual


def combine(left, right, x, out_ref):
    b1, b2, x = parts(left(1)), parts(right(1)), parts(x)
    w1, w2 = parts(dot6(b1, x)), parts(dot6(x, b2))
    out_ref[0] = left(0) - dot6(w1, b1, NT)
    out_ref[1] = dot6(w1, b2)
    out_ref[2] = right(2) - dot6(b2, w2, TN)


def merge_blocks(d, left, right, depth, out_ref, d_ref, x_ref, after):
    d_ref[...] = d
    x_ref[...], _ = newton(parts(d), first_inverse(d, SQUARINGS[min(depth, len(SQUARINGS) - 1)]), dot3)

    def going(state):
        return jnp.logical_and(state[0] < 9 * STEPS, jnp.logical_not(state[1] < TOLERANCE))

    def again(state):
        @pl.when(state[0] == STEPS)
        def _():
            x_ref[...] = step_size(d_ref[...]) * unit(d_ref.shape[0])

        x, residual = newton(parts(d_ref[...]), x_ref[...], dot6)
        x_ref[...] = x
        combine(left, right, x, out_ref)
        after()
        return state[0] + 1, jnp.sum(residual * residual)

    lax.while_loop(going, again, (0, F32(1)))


def pack(core, out_ref, send_ref):
    n = out_ref.shape[-1]
    row, column = grid_of(n)
    last = out_ref[2]
    both = jnp.where(row >= column, out_ref[0], last)
    send_ref[0:n] = jnp.where(core == 0, both, out_ref[1])
    diagonal = jnp.sum(jnp.where(row == column, last, F32(0)), axis=0, keepdims=True)
    send_ref[n : n + 8] = jnp.broadcast_to(diagonal, (8, n))


def leaf_kernel(flags_ref, margin_ref, cot_ref, csc_ref, coupling_ref, out_ref, d_ref, x_ref, a_ref, b_ref, c_ref):
    n = d_ref.shape[0]
    row, column = grid_of(n)
    half_step = 0.5 / (2 * flags_ref[1]).astype(F32)

    def sector(s):
        margin = margin_ref[:, s].reshape(n, n)
        if s == 0:
            margin = jnp.where(flags_ref[0] == 0, unit(n), margin)
        inner = jnp.where(row == column, cot_ref[s : s + 1, :], F32(0)) + half_step * coupling_ref[s].astype(F32)
        m = parts(margin)
        a_ref[s] = dot6(parts(dot6(m, parts(inner))), m, NT)
        b_ref[s] = margin * csc_ref[s : s + 1, :]
        c_ref[s] = inner

    sector(1)
    sector(0)
    blocks = (a_ref, b_ref, c_ref)
    merge_blocks(
        c_ref[0] + a_ref[1],
        lambda i: blocks[i][0],
        lambda i: blocks[i][1],
        0, out_ref, d_ref, x_ref, lambda: None,
    )


def leaf(flags, margin, cot, csc, coupling):
    n = coupling.shape[-1]
    return pl.pallas_call(
        leaf_kernel,
        out_shape=jax.ShapeDtypeStruct((3, n, n), F32),
        in_specs=[SMEM, VMEM, VMEM, VMEM, VMEM],
        out_specs=VMEM,
        scratch_shapes=[pltpu.VMEM((n, n), F32)] * 2 + [pltpu.VMEM((2, n, n), F32)] * 3,
        compiler_params=PARAMS,
        name="leaf",
    )(flags, margin, cot, csc, coupling)


def merge_refs(upper, own_ref, other_ref, depth, out_ref, d_ref, x_ref, after):
    merge_blocks(
        jnp.where(upper, other_ref[2] + own_ref[0], own_ref[2] + other_ref[0]),
        lambda i: jnp.where(upper, other_ref[i], own_ref[i]),
        lambda i: jnp.where(upper, own_ref[i], other_ref[i]),
        depth, out_ref, d_ref, x_ref, after,
    )


def core_kernel(flags_ref, own_ref, other_ref, out_ref, send_ref, d_ref, x_ref):
    core = flags_ref[2]
    merge_refs(core == 1, own_ref, other_ref, 1, out_ref, d_ref, x_ref, lambda: pack(core, out_ref, send_ref))


def core_merge(flags, own, other):
    n = own.shape[-1]
    return pl.pallas_call(
        core_kernel,
        out_shape=(jax.ShapeDtypeStruct((3, n, n), F32), jax.ShapeDtypeStruct((n + 8, n), F32)),
        in_specs=[SMEM, VMEM, VMEM],
        out_specs=(VMEM, VMEM),
        scratch_shapes=[pltpu.VMEM((n, n), F32)] * 2,
        compiler_params=PARAMS,
        name="core_merge",
    )(flags, own, other)


def unpack(core, came_ref, swapped_ref, other_ref):
    n = other_ref.shape[-1]
    row, column = grid_of(n)
    both = jnp.where(core == 0, came_ref[0:n], swapped_ref[0:n])
    diagonal = jnp.where(core == 0, came_ref[n : n + 1], swapped_ref[n : n + 1])
    turned = both.T
    other_ref[0] = jnp.where(row >= column, both, turned)
    other_ref[1] = jnp.where(core == 0, swapped_ref[0:n], came_ref[0:n])
    other_ref[2] = jnp.where(row == column, diagonal, jnp.where(row < column, both, turned))


def chip_kernel(level, flags_ref, own_ref, came_ref, swapped_ref, out_ref, send_ref, d_ref, x_ref, other_ref):
    core = flags_ref[2]
    active = flags_ref[4 + 2 * level] == 1

    @pl.when(active)
    def _():
        unpack(core, came_ref, swapped_ref, other_ref)
        merge_refs(
            flags_ref[5 + 2 * level] == 1, own_ref, other_ref, level + 2, out_ref, d_ref, x_ref,
            lambda: pack(core, out_ref, send_ref),
        )

    @pl.when(jnp.logical_not(active))
    def _():
        out_ref[...] = own_ref[...]
        send_ref[...] = jnp.zeros_like(send_ref)


def chip_merge(level, flags, own, came, swapped):
    n = own.shape[-1]
    return pl.pallas_call(
        functools.partial(chip_kernel, level),
        out_shape=(jax.ShapeDtypeStruct((3, n, n), F32), jax.ShapeDtypeStruct((n + 8, n), F32)),
        in_specs=[SMEM, VMEM, VMEM, VMEM],
        out_specs=(VMEM, VMEM),
        scratch_shapes=[pltpu.VMEM((n, n), F32)] * 2 + [pltpu.VMEM((3, n, n), F32)],
        compiler_params=PARAMS,
        name="chip_merge",
    )(flags, own, came, swapped)


def pair_kernel(level, flags_ref, came_ref, swapped_ref, came2_ref, swapped2_ref, out_ref, d_ref, x_ref, one_ref, other_ref):
    core = flags_ref[2]
    active = flags_ref[4 + 2 * level] == 1

    @pl.when(active)
    def _():
        unpack(core, came_ref, swapped_ref, one_ref)
        unpack(core, came2_ref, swapped2_ref, other_ref)
        merge_refs(
            flags_ref[5 + 2 * level] == 1, one_ref, other_ref, level + 2, out_ref, d_ref, x_ref, lambda: None
        )


def pair_merge(level, flags, one, other):
    n = one[0].shape[-1]
    return pl.pallas_call(
        functools.partial(pair_kernel, level),
        out_shape=jax.ShapeDtypeStruct((3, n, n), F32),
        in_specs=[SMEM] + [VMEM] * 4,
        out_specs=VMEM,
        scratch_shapes=[pltpu.VMEM((n, n), F32)] * 2 + [pltpu.VMEM((3, n, n), F32)] * 2,
        compiler_params=PARAMS,
        name="pair_merge",
    )(flags, *one, *other)


def last_kernel(level, flags_ref, own_ref, other_ref, mine_ref, next_ref, d_ref, x_ref, turned_ref, out_ref):
    n = d_ref.shape[0]
    core = flags_ref[2]
    wide, rows = mine_ref.shape[1:]
    active = flags_ref[4 + 2 * level] == 1

    def piece(chip, to_ref):
        chip_rows = pl.ds(pl.multiple_of(chip * (2 * wide), 2 * wide), 2 * wide)
        for i in range(3):
            both = turned_ref[chip_rows, :] if i == 1 else out_ref[i, chip_rows, :]
            moved = pltpu.roll(both, (n - flags_ref[3] * rows) % n, axis=1)[:, :rows]
            to_ref[i] = jnp.where(core == 0, moved[:wide], moved[wide:])

    @pl.when(active)
    def _():
        merge_refs(
            flags_ref[5 + 2 * level] == 1, own_ref, other_ref, level + 2, out_ref, d_ref, x_ref, lambda: None
        )
        turned_ref[...] = out_ref[1].T
        chip = flags_ref[0] // 2
        piece(chip, mine_ref)
        piece(chip + 1 - 2 * (chip % 2), next_ref)

    @pl.when(jnp.logical_not(active))
    def _():
        mine_ref[...] = jnp.zeros_like(mine_ref)
        next_ref[...] = jnp.zeros_like(next_ref)


def last_merge(level, flags, own, other, wide, rows):
    n = own.shape[-1]
    return pl.pallas_call(
        functools.partial(last_kernel, level),
        out_shape=(jax.ShapeDtypeStruct((3, wide, rows), F32),) * 2,
        in_specs=[SMEM, VMEM, VMEM],
        out_specs=(VMEM, VMEM),
        scratch_shapes=[pltpu.VMEM((n, n), F32)] * 3 + [pltpu.VMEM((3, n, n), F32)],
        compiler_params=PARAMS,
        name="last_merge",
    )(flags, own, other)


def pick_kernel(level, flags_ref, mine_ref, brought_ref, a_ref, b_ref, c_ref):
    for i, ref in enumerate((a_ref, b_ref, c_ref)):
        ref[...] = jnp.where(flags_ref[4 + 2 * level] == 1, mine_ref[i], brought_ref[i])


def pick(level, flags, mine, brought):
    return pl.pallas_call(
        functools.partial(pick_kernel, level),
        out_shape=(jax.ShapeDtypeStruct(mine.shape[1:], F32),) * 3,
        in_specs=[SMEM, VMEM, VMEM],
        out_specs=(VMEM,) * 3,
        name="pick",
    )(flags, mine, brought)


def margin_kernel(own_ref, before_ref, out_ref):
    shards, _, rows, depth = own_ref.shape
    n = shards * rows
    first = own_ref[:, 0].reshape(n, depth)
    second = own_ref[:, 1].reshape(n, depth)
    out_ref[:, 1] = dot1(first, second, NT).reshape(shards, rows, n)
    out_ref[:, 0] = dot1(before_ref[...].reshape(n, depth), first, NT).reshape(shards, rows, n)


def margin_parts(own, before):
    shards, sectors, rows, _ = own.shape
    return pl.pallas_call(
        margin_kernel,
        out_shape=jax.ShapeDtypeStruct((shards, sectors, rows, shards * rows), F32),
        in_specs=[VMEM, VMEM],
        out_specs=VMEM,
        compiler_params=PARAMS,
        name="margin_parts",
    )(own, before)


def total_kernel(points, partial_ref, out_ref):
    total = partial_ref[0]
    for shard in range(1, partial_ref.shape[0]):
        total = total + partial_ref[shard]
    total = total / points
    for shard in range(partial_ref.shape[0]):
        out_ref[shard] = total


def total_for_all(partial, points):
    return pl.pallas_call(
        functools.partial(total_kernel, points),
        out_shape=jax.ShapeDtypeStruct(partial.shape, F32),
        in_specs=[VMEM],
        out_specs=VMEM,
        compiler_params=PARAMS,
        name="total_for_all",
    )(partial)


def exchange(array):
    return lax.all_to_all(array, "chan", split_axis=0, concat_axis=0, tiled=True)


YS = 8
ENDS = (0, 3, 4, 7)


def place(position):
    return position // (2 * YS), position // 2 % YS, position % 2


def spot(x, y, core):
    return (x * YS + y) * 2 + core


def levels(xs):
    result = [
        (lambda x, y: (x, y ^ 1), range(YS), ("y", 0)),
        (lambda x, y: (x, y ^ 2), ENDS, ("y", 1)),
        (lambda x, y: (x, YS - 1 - y), ENDS, ("y", 2)),
    ]
    for bit in range(xs.bit_length() - 1):
        mask = 2 ** (bit + 1) - 1
        result.append((lambda x, y, mask=mask: (x ^ mask, y), ENDS, ("x", bit)))
    return result


def per_device(surface_functions, channel_rates, coupling):
    sectors, rows, points = surface_functions.shape
    n = channel_rates.shape[1]
    shards = lax.axis_size("chan")
    count = lax.axis_size("sector")
    position = lax.axis_index("sector")
    plan = levels(count // (2 * YS))
    x, y, core = place(position)
    at_end = (y == ENDS[0]) | (y == ENDS[1]) | (y == ENDS[2]) | (y == ENDS[3])
    words = [position, jnp.int32(count), core, lax.axis_index("chan")]
    for _, takers, (axis, bit) in plan:
        words.append(jnp.int32(1) if len(takers) == YS else at_end.astype(jnp.int32))
        words.append((x if axis == "x" else y) >> bit & 1)
    flags = jnp.stack([jnp.asarray(word, jnp.int32) for word in words])

    step = 1.0 / (sectors * count)
    cot = channel_rates / jnp.tanh(channel_rates * step)
    csc = channel_rates / jnp.sinh(channel_rates * step)

    cut = surface_functions.reshape(sectors, rows, shards, points // shards)
    own = exchange(jnp.transpose(cut, (2, 0, 1, 3)))
    before = lax.ppermute(own[:, sectors - 1], "sector", [(i, i + 1) for i in range(count - 1)])
    partial = exchange(margin_parts(own, before))
    ready = total_for_all(partial, points)
    ready, flags, cot, csc = lax.optimization_barrier((ready, flags, cot, csc))
    margin = exchange(ready)

    packed = leaf(flags, margin, cot, csc, coupling)
    cores = [(i, i ^ 1) for i in range(count)]
    packed, send = core_merge(flags, packed, lax.ppermute(packed, "sector", cores))
    def fetched(partner, takers):
        pairs = []
        for i in range(count):
            xi, yi, ci = place(i)
            if yi in takers:
                pairs.append((spot(*partner(xi, yi), ci), i))
        return lax.ppermute(send, "sector", pairs)

    def both(came):
        return came, lax.ppermute(came, "sector", cores)

    for level, (partner, takers, _) in enumerate(plan[:3]):
        packed, send = chip_merge(level, flags, packed, *both(fetched(partner, takers)))
    across = fetched(lambda x, y: (x ^ 2, y), ENDS)
    near = fetched(lambda x, y: (x ^ 1, y), ENDS)
    far = fetched(lambda x, y: (x ^ 3, y), ENDS)
    packed, _ = chip_merge(3, flags, packed, *both(near))
    other = pair_merge(3, flags, both(across), both(far))
    mine, for_next = last_merge(4, flags, packed, other, n // count, rows)
    pairs = []
    for i in range(count):
        xi, yi, ci = place(i)
        if yi not in ENDS:
            pairs.append((spot(xi, yi ^ 1, ci), i))
    brought = lax.ppermute(for_next, "sector", pairs)
    return tuple(block.T for block in pick(4, flags, mine, brought))


def solution(mesh):
    placed = (P("sector", "chan", None), P("sector", None), P("sector", None, None))
    return jax.shard_map(
        per_device,
        mesh=mesh,
        in_specs=placed,
        out_specs=(P("chan", "sector"), P("chan", "sector"), P("chan", "sector")),
        check_vma=False,
    )
```

```python
import functools

import jax
import jax.numpy as jnp
from jax import lax
from jax.experimental import pallas as pl
from jax.experimental.pallas import tpu as pltpu
from jax.sharding import PartitionSpec as P

F32 = jnp.float32
BF16 = jnp.bfloat16
NN = (((1,), (0,)), ((), ()))
NT = (((1,), (1,)), ((), ()))
TN = (((0,), (0,)), ((), ()))
TOLERANCE = 1e-5
STEPS = 8
SQUARINGS = (4, 4, 5, 6, 7, 8, 8)
PARAMS = pltpu.CompilerParams(vmem_limit_bytes=32 * 2**20)
VMEM = pl.BlockSpec(memory_space=pltpu.VMEM)
SMEM = pl.BlockSpec(memory_space=pltpu.SMEM)


def parts(x):
    high = x.astype(BF16)
    rest = x - high.astype(F32)
    middle = rest.astype(BF16)
    return high, middle, (rest - middle.astype(F32)).astype(BF16)


def dot1(a, b, dims=NN):
    return lax.dot_general(a, b, dims, preferred_element_type=F32)


def dot3(a, b, dims=NN):
    return dot1(a[0], b[0], dims) + (dot1(a[0], b[1], dims) + dot1(a[1], b[0], dims))


def dot6(a, b, dims=NN):
    low = dot1(a[0], b[2], dims) + dot1(a[1], b[1], dims) + dot1(a[2], b[0], dims)
    return dot1(a[0], b[0], dims) + ((dot1(a[0], b[1], dims) + dot1(a[1], b[0], dims)) + low)


def grid_of(n):
    return (
        lax.broadcasted_iota(jnp.int32, (n, n), 0),
        lax.broadcasted_iota(jnp.int32, (n, n), 1),
    )


def unit(n):
    row, column = grid_of(n)
    return jnp.where(row == column, F32(1), F32(0))


def step_size(d):
    return 1.9 / jnp.max(jnp.sum(jnp.abs(d), axis=0, keepdims=True), axis=1, keepdims=True)


def first_inverse(d, squarings):
    n = d.shape[0]
    one = unit(n)
    alpha = step_size(d)
    e = one - alpha * d
    c = jnp.sum(jnp.sum(e * one, axis=0, keepdims=True), axis=1, keepdims=True) / n
    f = e - c * one
    p, y = 1 + c, f
    for _ in range(squarings):
        rounded = f.astype(BF16)
        f = 2 * c * f + dot1(rounded, rounded)
        c = c * c
        y = p * f + (1 + c) * y + dot1(y.astype(BF16), f.astype(BF16))
        p = p * (1 + c)
    return alpha * (p * one + y)


def newton(d_parts, x, dot):
    x_parts = parts(x)
    residual = unit(x.shape[0]) - dot(d_parts, x_parts)
    return x + dot3(x_parts, parts(residual)), residual


def combine(left, right, x, out_ref):
    b1, b2, x = parts(left(1)), parts(right(1)), parts(x)
    w1, w2 = parts(dot6(b1, x)), parts(dot6(x, b2))
    out_ref[0] = left(0) - dot6(w1, b1, NT)
    out_ref[1] = dot6(w1, b2)
    out_ref[2] = right(2) - dot6(b2, w2, TN)


def merge_blocks(d, left, right, depth, out_ref, d_ref, x_ref, after):
    d_ref[...] = d
    x_ref[...], _ = newton(parts(d), first_inverse(d, SQUARINGS[min(depth, len(SQUARINGS) - 1)]), dot3)

    def going(state):
        return jnp.logical_and(state[0] < 9 * STEPS, jnp.logical_not(state[1] < TOLERANCE))

    def again(state):
        @pl.when(state[0] == STEPS)
        def _():
            x_ref[...] = step_size(d_ref[...]) * unit(d_ref.shape[0])

        x, residual = newton(parts(d_ref[...]), x_ref[...], dot6)
        x_ref[...] = x
        combine(left, right, x, out_ref)
        after()
        return state[0] + 1, jnp.sum(residual * residual)

    lax.while_loop(going, again, (0, F32(1)))


def pack(core, out_ref, send_ref):
    n = out_ref.shape[-1]
    row, column = grid_of(n)
    last = out_ref[2]
    both = jnp.where(row >= column, out_ref[0], last)
    send_ref[0:n] = jnp.where(core == 0, both, out_ref[1])
    diagonal = jnp.sum(jnp.where(row == column, last, F32(0)), axis=0, keepdims=True)
    send_ref[n : n + 8] = jnp.broadcast_to(diagonal, (8, n))


def leaf_kernel(flags_ref, margin_ref, cot_ref, csc_ref, coupling_ref, out_ref, d_ref, x_ref, a_ref, b_ref, c_ref):
    n = d_ref.shape[0]
    row, column = grid_of(n)
    half_step = 0.5 / (2 * flags_ref[1]).astype(F32)

    def sector(s):
        margin = margin_ref[:, s].reshape(n, n)
        if s == 0:
            margin = jnp.where(flags_ref[0] == 0, unit(n), margin)
        inner = jnp.where(row == column, cot_ref[s : s + 1, :], F32(0)) + half_step * coupling_ref[s].astype(F32)
        m = parts(margin)
        a_ref[s] = dot6(parts(dot6(m, parts(inner))), m, NT)
        b_ref[s] = margin * csc_ref[s : s + 1, :]
        c_ref[s] = inner

    sector(1)
    sector(0)
    blocks = (a_ref, b_ref, c_ref)
    merge_blocks(
        c_ref[0] + a_ref[1],
        lambda i: blocks[i][0],
        lambda i: blocks[i][1],
        0, out_ref, d_ref, x_ref, lambda: None,
    )


def leaf(flags, margin, cot, csc, coupling):
    n = coupling.shape[-1]
    return pl.pallas_call(
        leaf_kernel,
        out_shape=jax.ShapeDtypeStruct((3, n, n), F32),
        in_specs=[SMEM, VMEM, VMEM, VMEM, VMEM],
        out_specs=VMEM,
        scratch_shapes=[pltpu.VMEM((n, n), F32)] * 2 + [pltpu.VMEM((2, n, n), F32)] * 3,
        compiler_params=PARAMS,
        name="leaf",
    )(flags, margin, cot, csc, coupling)


def merge_refs(upper, own_ref, other_ref, depth, out_ref, d_ref, x_ref, after):
    merge_blocks(
        jnp.where(upper, other_ref[2] + own_ref[0], own_ref[2] + other_ref[0]),
        lambda i: jnp.where(upper, other_ref[i], own_ref[i]),
        lambda i: jnp.where(upper, own_ref[i], other_ref[i]),
        depth, out_ref, d_ref, x_ref, after,
    )


def core_kernel(flags_ref, own_ref, other_ref, out_ref, send_ref, d_ref, x_ref):
    core = flags_ref[2]
    merge_refs(core == 1, own_ref, other_ref, 1, out_ref, d_ref, x_ref, lambda: pack(core, out_ref, send_ref))


def core_merge(flags, own, other):
    n = own.shape[-1]
    return pl.pallas_call(
        core_kernel,
        out_shape=(jax.ShapeDtypeStruct((3, n, n), F32), jax.ShapeDtypeStruct((n + 8, n), F32)),
        in_specs=[SMEM, VMEM, VMEM],
        out_specs=(VMEM, VMEM),
        scratch_shapes=[pltpu.VMEM((n, n), F32)] * 2,
        compiler_params=PARAMS,
        name="core_merge",
    )(flags, own, other)


def unpack(core, came_ref, swapped_ref, other_ref):
    n = other_ref.shape[-1]
    row, column = grid_of(n)
    both = jnp.where(core == 0, came_ref[0:n], swapped_ref[0:n])
    diagonal = jnp.where(core == 0, came_ref[n : n + 1], swapped_ref[n : n + 1])
    turned = both.T
    other_ref[0] = jnp.where(row >= column, both, turned)
    other_ref[1] = jnp.where(core == 0, swapped_ref[0:n], came_ref[0:n])
    other_ref[2] = jnp.where(row == column, diagonal, jnp.where(row < column, both, turned))


def chip_kernel(level, flags_ref, own_ref, came_ref, swapped_ref, out_ref, send_ref, d_ref, x_ref, other_ref):
    core = flags_ref[2]
    active = flags_ref[4 + 2 * level] == 1

    @pl.when(active)
    def _():
        unpack(core, came_ref, swapped_ref, other_ref)
        merge_refs(
            flags_ref[5 + 2 * level] == 1, own_ref, other_ref, level + 2, out_ref, d_ref, x_ref,
            lambda: pack(core, out_ref, send_ref),
        )

    @pl.when(jnp.logical_not(active))
    def _():
        out_ref[...] = own_ref[...]
        send_ref[...] = jnp.zeros_like(send_ref)


def chip_merge(level, flags, own, came, swapped):
    n = own.shape[-1]
    return pl.pallas_call(
        functools.partial(chip_kernel, level),
        out_shape=(jax.ShapeDtypeStruct((3, n, n), F32), jax.ShapeDtypeStruct((n + 8, n), F32)),
        in_specs=[SMEM, VMEM, VMEM, VMEM],
        out_specs=(VMEM, VMEM),
        scratch_shapes=[pltpu.VMEM((n, n), F32)] * 2 + [pltpu.VMEM((3, n, n), F32)],
        compiler_params=PARAMS,
        name="chip_merge",
    )(flags, own, came, swapped)


def last_kernel(level, flags_ref, own_ref, came_ref, swapped_ref, mine_ref, next_ref, d_ref, x_ref, other_ref, out_ref):
    n = d_ref.shape[0]
    core = flags_ref[2]
    wide, rows = mine_ref.shape[1:]
    active = flags_ref[4 + 2 * level] == 1

    def piece(chip, to_ref):
        chip_rows = pl.ds(pl.multiple_of(chip * (2 * wide), 2 * wide), 2 * wide)
        for i in range(3):
            source = other_ref if i == 1 else out_ref
            both = source[0 if i == 1 else i, chip_rows, :]
            moved = pltpu.roll(both, (n - flags_ref[3] * rows) % n, axis=1)[:, :rows]
            to_ref[i] = jnp.where(core == 0, moved[:wide], moved[wide:])

    @pl.when(active)
    def _():
        unpack(core, came_ref, swapped_ref, other_ref)
        merge_refs(
            flags_ref[5 + 2 * level] == 1, own_ref, other_ref, level + 2, out_ref, d_ref, x_ref, lambda: None
        )
        other_ref[0] = out_ref[1].T
        chip = flags_ref[0] // 2
        piece(chip, mine_ref)
        piece(chip + 1 - 2 * (chip % 2), next_ref)

    @pl.when(jnp.logical_not(active))
    def _():
        mine_ref[...] = jnp.zeros_like(mine_ref)
        next_ref[...] = jnp.zeros_like(next_ref)


def last_merge(level, flags, own, came, swapped, wide, rows):
    n = own.shape[-1]
    return pl.pallas_call(
        functools.partial(last_kernel, level),
        out_shape=(jax.ShapeDtypeStruct((3, wide, rows), F32),) * 2,
        in_specs=[SMEM, VMEM, VMEM, VMEM],
        out_specs=(VMEM, VMEM),
        scratch_shapes=[pltpu.VMEM((n, n), F32)] * 2 + [pltpu.VMEM((3, n, n), F32)] * 2,
        compiler_params=PARAMS,
        name="last_merge",
    )(flags, own, came, swapped)


def pick_kernel(level, flags_ref, mine_ref, brought_ref, a_ref, b_ref, c_ref):
    for i, ref in enumerate((a_ref, b_ref, c_ref)):
        ref[...] = jnp.where(flags_ref[4 + 2 * level] == 1, mine_ref[i], brought_ref[i])


def pick(level, flags, mine, brought):
    return pl.pallas_call(
        functools.partial(pick_kernel, level),
        out_shape=(jax.ShapeDtypeStruct(mine.shape[1:], F32),) * 3,
        in_specs=[SMEM, VMEM, VMEM],
        out_specs=(VMEM,) * 3,
        compiler_params=pltpu.CompilerParams(vmem_limit_bytes=2**20),
        name="pick",
    )(flags, mine, brought)


def margin_kernel(own_ref, before_ref, out_ref):
    shards, _, rows, depth = own_ref.shape
    n = shards * rows
    first = own_ref[:, 0].reshape(n, depth)
    second = own_ref[:, 1].reshape(n, depth)
    out_ref[:, 1] = dot1(first, second, NT).reshape(shards, rows, n)
    out_ref[:, 0] = dot1(before_ref[...].reshape(n, depth), first, NT).reshape(shards, rows, n)


def margin_parts(own, before):
    shards, sectors, rows, _ = own.shape
    return pl.pallas_call(
        margin_kernel,
        out_shape=jax.ShapeDtypeStruct((shards, sectors, rows, shards * rows), F32),
        in_specs=[VMEM, VMEM],
        out_specs=VMEM,
        compiler_params=PARAMS,
        name="margin_parts",
    )(own, before)


def total_kernel(points, partial_ref, out_ref):
    total = partial_ref[0]
    for shard in range(1, partial_ref.shape[0]):
        total = total + partial_ref[shard]
    total = total / points
    for shard in range(partial_ref.shape[0]):
        out_ref[shard] = total


def total_for_all(partial, points):
    return pl.pallas_call(
        functools.partial(total_kernel, points),
        out_shape=jax.ShapeDtypeStruct(partial.shape, F32),
        in_specs=[VMEM],
        out_specs=VMEM,
        compiler_params=PARAMS,
        name="total_for_all",
    )(partial)


def exchange(array):
    return lax.all_to_all(array, "chan", split_axis=0, concat_axis=0, tiled=True)


YS = 8
ENDS = (0, 3, 4, 7)


def place(position):
    return position // (2 * YS), position // 2 % YS, position % 2


def spot(x, y, core):
    return (x * YS + y) * 2 + core


def levels(xs):
    result = [
        (lambda x, y: (x, y ^ 1), range(YS), ("y", 0)),
        (lambda x, y: (x, y ^ 2), ENDS, ("y", 1)),
        (lambda x, y: (x, YS - 1 - y), ENDS, ("y", 2)),
    ]
    for bit in range(xs.bit_length() - 1):
        mask = 2 ** (bit + 1) - 1
        result.append((lambda x, y, mask=mask: (x ^ mask, y), ENDS, ("x", bit)))
    return result


def per_device(surface_functions, channel_rates, coupling):
    sectors, rows, points = surface_functions.shape
    n = channel_rates.shape[1]
    shards = lax.axis_size("chan")
    count = lax.axis_size("sector")
    position = lax.axis_index("sector")
    plan = levels(count // (2 * YS))
    x, y, core = place(position)
    at_end = (y == ENDS[0]) | (y == ENDS[1]) | (y == ENDS[2]) | (y == ENDS[3])
    words = [position, jnp.int32(count), core, lax.axis_index("chan")]
    for _, takers, (axis, bit) in plan:
        words.append(jnp.int32(1) if len(takers) == YS else at_end.astype(jnp.int32))
        words.append((x if axis == "x" else y) >> bit & 1)
    flags = jnp.stack([jnp.asarray(word, jnp.int32) for word in words])

    step = 1.0 / (sectors * count)
    cot = channel_rates / jnp.tanh(channel_rates * step)
    csc = channel_rates / jnp.sinh(channel_rates * step)

    cut = surface_functions.reshape(sectors, rows, shards, points // shards)
    cut, flags, cot, csc = lax.optimization_barrier((jnp.transpose(cut, (2, 0, 1, 3)), flags, cot, csc))
    own = exchange(cut)
    before = lax.ppermute(own[:, sectors - 1], "sector", [(i, i + 1) for i in range(count - 1)])
    partial = exchange(margin_parts(own, before))
    margin = exchange(total_for_all(partial, points))

    packed = leaf(flags, margin, cot, csc, coupling)
    cores = [(i, i ^ 1) for i in range(count)]
    packed, send = core_merge(flags, packed, lax.ppermute(packed, "sector", cores))
    wide = n // count
    for level, (partner, takers, _) in enumerate(plan):
        pairs = []
        for i in range(count):
            xi, yi, ci = place(i)
            if yi in takers:
                pairs.append((spot(*partner(xi, yi), ci), i))
        came = lax.ppermute(send, "sector", pairs)
        swapped = lax.ppermute(came, "sector", cores)
        if level < len(plan) - 1:
            packed, send = chip_merge(level, flags, packed, came, swapped)
        else:
            mine, for_next = last_merge(level, flags, packed, came, swapped, wide, rows)
    pairs = []
    for i in range(count):
        xi, yi, ci = place(i)
        if yi not in ENDS:
            pairs.append((spot(xi, yi ^ 1, ci), i))
    brought = lax.ppermute(for_next, "sector", pairs)
    return tuple(block.T for block in pick(len(plan) - 1, flags, mine, brought))


def solution(mesh):
    placed = (P("sector", "chan", None), P("sector", None), P("sector", None, None))
    return jax.shard_map(
        per_device,
        mesh=mesh,
        in_specs=placed,
        out_specs=(P("chan", "sector"), P("chan", "sector"), P("chan", "sector")),
        check_vma=False,
    )
```

```python
import functools

import jax
import jax.numpy as jnp
from jax import lax
from jax.experimental import pallas as pl
from jax.experimental.pallas import tpu as pltpu
from jax.sharding import PartitionSpec as P

F32 = jnp.float32
BF16 = jnp.bfloat16
NN = (((1,), (0,)), ((), ()))
NT = (((1,), (1,)), ((), ()))
TN = (((0,), (0,)), ((), ()))
TOLERANCE = 1e-5
STEPS = 8
SQUARINGS = (3, 3, 4, 5, 6, 7, 7)
WORK = pl.CostEstimate(flops=10**9, bytes_accessed=2 * 10**6, transcendentals=0)
PARAMS = pltpu.CompilerParams(vmem_limit_bytes=32 * 2**20)
VMEM = pl.BlockSpec(memory_space=pltpu.VMEM)
SMEM = pl.BlockSpec(memory_space=pltpu.SMEM)


def parts(x):
    high = x.astype(BF16)
    rest = x - high.astype(F32)
    middle = rest.astype(BF16)
    return high, middle, (rest - middle.astype(F32)).astype(BF16)


def dot1(a, b, dims=NN):
    return lax.dot_general(a, b, dims, preferred_element_type=F32)


def dot3(a, b, dims=NN):
    return dot1(a[0], b[0], dims) + (dot1(a[0], b[1], dims) + dot1(a[1], b[0], dims))


def dot6(a, b, dims=NN):
    low = dot1(a[0], b[2], dims) + dot1(a[1], b[1], dims) + dot1(a[2], b[0], dims)
    return dot1(a[0], b[0], dims) + ((dot1(a[0], b[1], dims) + dot1(a[1], b[0], dims)) + low)


def grid_of(n):
    return (
        lax.broadcasted_iota(jnp.int32, (n, n), 0),
        lax.broadcasted_iota(jnp.int32, (n, n), 1),
    )


def unit(n):
    row, column = grid_of(n)
    return jnp.where(row == column, F32(1), F32(0))


def step_size(d):
    return 1.9 / jnp.max(jnp.sum(jnp.abs(d), axis=0, keepdims=True), axis=1, keepdims=True)


def first_inverse(d, squarings):
    n = d.shape[0]
    one = unit(n)
    alpha = step_size(d)
    e = one - alpha * d
    c = jnp.sum(jnp.sum(e * one, axis=0, keepdims=True), axis=1, keepdims=True) / n
    f = e - c * one
    p, y = 1 + c, f
    for _ in range(squarings):
        rounded = f.astype(BF16)
        f = 2 * c * f + dot1(rounded, rounded)
        c = c * c
        y = p * f + (1 + c) * y + dot1(y.astype(BF16), f.astype(BF16))
        p = p * (1 + c)
    return alpha * (p * one + y)


def newton(d_parts, x, dot):
    x_parts = parts(x)
    residual = unit(x.shape[0]) - dot(d_parts, x_parts)
    return x + (dot1(x_parts[0], residual.astype(BF16)) if dot is dot3 else dot3(x_parts, parts(residual))), residual


def combine(left, right, x, out_ref):
    b1, b2, x = parts(left(1)), parts(right(1)), parts(x)
    w1, w2 = parts(dot6(b1, x)), parts(dot6(x, b2))
    out_ref[0] = left(0) - dot6(w1, b1, NT)
    out_ref[1] = dot6(w1, b2)
    out_ref[2] = right(2) - dot6(b2, w2, TN)


def merge_blocks(d, left, right, depth, out_ref, d_ref, x_ref, after):
    d_ref[...] = d
    x_ref[...], _ = newton(parts(d), first_inverse(d, SQUARINGS[min(depth, len(SQUARINGS) - 1)]), dot3)

    def going(state):
        return jnp.logical_and(state[0] < 9 * STEPS, jnp.logical_not(state[1] < TOLERANCE))

    def again(state):
        @pl.when(state[0] == STEPS)
        def _():
            x_ref[...] = step_size(d_ref[...]) * unit(d_ref.shape[0])

        x, residual = newton(parts(d_ref[...]), x_ref[...], dot6)
        x_ref[...] = x
        combine(left, right, x, out_ref)
        after()
        return state[0] + 1, jnp.sum(residual * residual)

    lax.while_loop(going, again, (0, F32(1)))


def pack(core, out_ref, send_ref):
    n = out_ref.shape[-1]
    row, column = grid_of(n)
    last = out_ref[2]
    both = jnp.where(row >= column, out_ref[0], last)
    send_ref[0:n] = jnp.where(core == 0, both, out_ref[1])
    diagonal = jnp.sum(jnp.where(row == column, last, F32(0)), axis=0, keepdims=True)
    send_ref[n : n + 8] = jnp.broadcast_to(diagonal, (8, n))


def leaf_kernel(flags_ref, margin_ref, cot_ref, csc_ref, coupling_ref, out_ref, d_ref, x_ref, a_ref, b_ref, c_ref):
    n = d_ref.shape[0]
    row, column = grid_of(n)
    half_step = 0.5 / (2 * flags_ref[1]).astype(F32)

    def sector(s):
        margin = margin_ref[:, s].reshape(n, n)
        if s == 0:
            margin = jnp.where(flags_ref[0] == 0, unit(n), margin)
        inner = jnp.where(row == column, cot_ref[s : s + 1, :], F32(0)) + half_step * coupling_ref[s].astype(F32)
        m = parts(margin)
        a_ref[s] = dot6(parts(dot6(m, parts(inner))), m, NT)
        b_ref[s] = margin * csc_ref[s : s + 1, :]
        c_ref[s] = inner

    sector(1)
    sector(0)
    blocks = (a_ref, b_ref, c_ref)
    merge_blocks(
        c_ref[0] + a_ref[1],
        lambda i: blocks[i][0],
        lambda i: blocks[i][1],
        0, out_ref, d_ref, x_ref, lambda: None,
    )


def leaf(flags, margin, cot, csc, coupling):
    n = coupling.shape[-1]
    return pl.pallas_call(
        leaf_kernel,
        out_shape=jax.ShapeDtypeStruct((3, n, n), F32),
        in_specs=[SMEM, VMEM, VMEM, VMEM, VMEM],
        out_specs=VMEM,
        scratch_shapes=[pltpu.VMEM((n, n), F32)] * 2 + [pltpu.VMEM((2, n, n), F32)] * 3,
        compiler_params=PARAMS,
        name="leaf",
    )(flags, margin, cot, csc, coupling)


def merge_refs(upper, own_ref, other_ref, depth, out_ref, d_ref, x_ref, after):
    merge_blocks(
        jnp.where(upper, other_ref[2] + own_ref[0], own_ref[2] + other_ref[0]),
        lambda i: jnp.where(upper, other_ref[i], own_ref[i]),
        lambda i: jnp.where(upper, own_ref[i], other_ref[i]),
        depth, out_ref, d_ref, x_ref, after,
    )


def core_kernel(flags_ref, own_ref, other_ref, out_ref, send_ref, d_ref, x_ref):
    core = flags_ref[2]
    merge_refs(core == 1, own_ref, other_ref, 1, out_ref, d_ref, x_ref, lambda: pack(core, out_ref, send_ref))


def core_merge(flags, own, other):
    n = own.shape[-1]
    return pl.pallas_call(
        core_kernel,
        out_shape=(jax.ShapeDtypeStruct((3, n, n), F32), jax.ShapeDtypeStruct((n + 8, n), F32)),
        in_specs=[SMEM, VMEM, VMEM],
        out_specs=(VMEM, VMEM),
        scratch_shapes=[pltpu.VMEM((n, n), F32)] * 2,
        compiler_params=PARAMS,
        name="core_merge",
    )(flags, own, other)


def unpack(core, came_ref, swapped_ref, other_ref):
    n = other_ref.shape[-1]
    row, column = grid_of(n)
    both = jnp.where(core == 0, came_ref[0:n], swapped_ref[0:n])
    diagonal = jnp.where(core == 0, came_ref[n : n + 1], swapped_ref[n : n + 1])
    turned = both.T
    other_ref[0] = jnp.where(row >= column, both, turned)
    other_ref[1] = jnp.where(core == 0, swapped_ref[0:n], came_ref[0:n])
    other_ref[2] = jnp.where(row == column, diagonal, jnp.where(row < column, both, turned))


def chip_kernel(level, flags_ref, own_ref, came_ref, swapped_ref, out_ref, send_ref, d_ref, x_ref, other_ref):
    core = flags_ref[2]
    active = flags_ref[4 + 2 * level] == 1

    @pl.when(active)
    def _():
        unpack(core, came_ref, swapped_ref, other_ref)
        merge_refs(
            flags_ref[5 + 2 * level] == 1, own_ref, other_ref, level + 2, out_ref, d_ref, x_ref,
            lambda: pack(core, out_ref, send_ref),
        )

    @pl.when(jnp.logical_not(active))
    def _():
        out_ref[...] = own_ref[...]
        send_ref[...] = jnp.zeros_like(send_ref)


def chip_merge(level, flags, own, came, swapped):
    n = own.shape[-1]
    return pl.pallas_call(
        functools.partial(chip_kernel, level),
        out_shape=(jax.ShapeDtypeStruct((3, n, n), F32), jax.ShapeDtypeStruct((n + 8, n), F32)),
        in_specs=[SMEM, VMEM, VMEM, VMEM],
        out_specs=(VMEM, VMEM),
        scratch_shapes=[pltpu.VMEM((n, n), F32)] * 2 + [pltpu.VMEM((3, n, n), F32)],
        compiler_params=PARAMS,
        name="chip_merge",
    )(flags, own, came, swapped)


def last_kernel(level, flags_ref, own_ref, came_ref, swapped_ref, mine_ref, next_ref, d_ref, x_ref, other_ref, out_ref):
    n = d_ref.shape[0]
    core = flags_ref[2]
    wide, rows = mine_ref.shape[1:]
    active = flags_ref[4 + 2 * level] == 1

    def piece(chip, to_ref):
        chip_rows = pl.ds(pl.multiple_of(chip * (2 * wide), 2 * wide), 2 * wide)
        for i in range(3):
            source = other_ref if i == 1 else out_ref
            both = source[0 if i == 1 else i, chip_rows, :]
            moved = pltpu.roll(both, (n - flags_ref[3] * rows) % n, axis=1)[:, :rows]
            to_ref[i] = jnp.where(core == 0, moved[:wide], moved[wide:])

    @pl.when(active)
    def _():
        unpack(core, came_ref, swapped_ref, other_ref)
        merge_refs(
            flags_ref[5 + 2 * level] == 1, own_ref, other_ref, level + 2, out_ref, d_ref, x_ref, lambda: None
        )
        other_ref[0] = out_ref[1].T
        chip = flags_ref[0] // 2
        piece(chip, mine_ref)
        piece(chip + 1 - 2 * (chip % 2), next_ref)

    @pl.when(jnp.logical_not(active))
    def _():
        mine_ref[...] = jnp.zeros_like(mine_ref)
        next_ref[...] = jnp.zeros_like(next_ref)


def last_merge(level, flags, own, came, swapped, wide, rows):
    n = own.shape[-1]
    return pl.pallas_call(
        functools.partial(last_kernel, level),
        out_shape=(jax.ShapeDtypeStruct((3, wide, rows), F32),) * 2,
        in_specs=[SMEM, VMEM, VMEM, VMEM],
        out_specs=(VMEM, VMEM),
        scratch_shapes=[pltpu.VMEM((n, n), F32)] * 2 + [pltpu.VMEM((3, n, n), F32)] * 2,
        compiler_params=PARAMS,
        name="last_merge",
    )(flags, own, came, swapped)


def pick_kernel(level, flags_ref, mine_ref, brought_ref, a_ref, b_ref, c_ref):
    for i, ref in enumerate((a_ref, b_ref, c_ref)):
        ref[...] = jnp.where(flags_ref[4 + 2 * level] == 1, mine_ref[i], brought_ref[i])


def pick(level, flags, mine, brought):
    return pl.pallas_call(
        functools.partial(pick_kernel, level),
        out_shape=(jax.ShapeDtypeStruct(mine.shape[1:], F32),) * 3,
        in_specs=[SMEM, VMEM, VMEM],
        out_specs=(VMEM,) * 3,
        compiler_params=pltpu.CompilerParams(vmem_limit_bytes=2**20),
        name="pick",
    )(flags, mine, brought)


def inner_kernel(own_ref, out_ref):
    shards, _, rows, depth = own_ref.shape
    n = shards * rows
    first = own_ref[:, 0].reshape(n, depth)
    second = own_ref[:, 1].reshape(n, depth)
    out_ref[...] = dot1(first, second, NT).reshape(shards, rows, n)


def margin_kernel(own_ref, before_ref, inner_ref, out_ref):
    shards, _, rows, depth = own_ref.shape
    n = shards * rows
    first = own_ref[:, 0].reshape(n, depth)
    out_ref[:, 0] = dot1(before_ref[...].reshape(n, depth), first, NT).reshape(shards, rows, n)
    out_ref[:, 1] = inner_ref[...]


def inner_parts(own):
    shards, _, rows, _ = own.shape
    return pl.pallas_call(
        inner_kernel,
        out_shape=jax.ShapeDtypeStruct((shards, rows, shards * rows), F32),
        in_specs=[VMEM],
        out_specs=VMEM,
        compiler_params=PARAMS,
        cost_estimate=WORK,
        name="inner_parts",
    )(own)


def margin_parts(own, before, inner):
    shards, sectors, rows, _ = own.shape
    return pl.pallas_call(
        margin_kernel,
        out_shape=jax.ShapeDtypeStruct((shards, sectors, rows, shards * rows), F32),
        in_specs=[VMEM, VMEM, VMEM],
        out_specs=VMEM,
        compiler_params=PARAMS,
        name="margin_parts",
    )(own, before, inner)


def total_kernel(points, partial_ref, out_ref):
    total = partial_ref[0]
    for shard in range(1, partial_ref.shape[0]):
        total = total + partial_ref[shard]
    total = total / points
    for shard in range(partial_ref.shape[0]):
        out_ref[shard] = total


def total_for_all(partial, points):
    return pl.pallas_call(
        functools.partial(total_kernel, points),
        out_shape=jax.ShapeDtypeStruct(partial.shape, F32),
        in_specs=[VMEM],
        out_specs=VMEM,
        compiler_params=PARAMS,
        name="total_for_all",
    )(partial)


def exchange(array):
    return lax.all_to_all(array, "chan", split_axis=0, concat_axis=0, tiled=True)


YS = 8
ENDS = (0, 3, 4, 7)


def place(position):
    return position // (2 * YS), position // 2 % YS, position % 2


def spot(x, y, core):
    return (x * YS + y) * 2 + core


def levels(xs):
    result = [
        (lambda x, y: (x, y ^ 1), range(YS), ("y", 0)),
        (lambda x, y: (x, y ^ 2), ENDS, ("y", 1)),
        (lambda x, y: (x, YS - 1 - y), ENDS, ("y", 2)),
    ]
    for bit in range(xs.bit_length() - 1):
        mask = 2 ** (bit + 1) - 1
        result.append((lambda x, y, mask=mask: (x ^ mask, y), ENDS, ("x", bit)))
    return result


def per_device(surface_functions, channel_rates, coupling):
    sectors, rows, points = surface_functions.shape
    n = channel_rates.shape[1]
    shards = lax.axis_size("chan")
    count = lax.axis_size("sector")
    position = lax.axis_index("sector")
    plan = levels(count // (2 * YS))
    x, y, core = place(position)
    at_end = (y == ENDS[0]) | (y == ENDS[1]) | (y == ENDS[2]) | (y == ENDS[3])
    words = [position, jnp.int32(count), core, lax.axis_index("chan")]
    for _, takers, (axis, bit) in plan:
        words.append(jnp.int32(1) if len(takers) == YS else at_end.astype(jnp.int32))
        words.append((x if axis == "x" else y) >> bit & 1)
    flags = jnp.stack([jnp.asarray(word, jnp.int32) for word in words])

    step = 1.0 / (sectors * count)
    cot = channel_rates / jnp.tanh(channel_rates * step)
    csc = channel_rates / jnp.sinh(channel_rates * step)

    cut = surface_functions.reshape(sectors, rows, shards, points // shards)
    own = exchange(jnp.transpose(cut, (2, 0, 1, 3)))
    before = lax.ppermute(own[:, sectors - 1], "sector", [(i, i + 1) for i in range(count - 1)])
    inner, cot, csc, flags, before = lax.optimization_barrier((inner_parts(own), cot, csc, flags, before))
    partial = exchange(margin_parts(own, before, inner))
    margin = exchange(total_for_all(partial, points))

    packed = leaf(flags, margin, cot, csc, coupling)
    cores = [(i, i ^ 1) for i in range(count)]
    packed, send = core_merge(flags, packed, lax.ppermute(packed, "sector", cores))
    wide = n // count
    for level, (partner, takers, _) in enumerate(plan):
        pairs = []
        for i in range(count):
            xi, yi, ci = place(i)
            if yi in takers:
                pairs.append((spot(*partner(xi, yi), ci), i))
        came = lax.ppermute(send, "sector", pairs)
        swapped = lax.ppermute(came, "sector", cores)
        if level < len(plan) - 1:
            packed, send = chip_merge(level, flags, packed, came, swapped)
        else:
            mine, for_next = last_merge(level, flags, packed, came, swapped, wide, rows)
    pairs = []
    for i in range(count):
        xi, yi, ci = place(i)
        if yi not in ENDS:
            pairs.append((spot(xi, yi ^ 1, ci), i))
    brought = lax.ppermute(for_next, "sector", pairs)
    return tuple(block.T for block in pick(len(plan) - 1, flags, mine, brought))


def solution(mesh):
    placed = (P("sector", "chan", None), P("sector", None), P("sector", None, None))
    return jax.shard_map(
        per_device,
        mesh=mesh,
        in_specs=placed,
        out_specs=(P("chan", "sector"), P("chan", "sector"), P("chan", "sector")),
        check_vma=False,
    )
```

```python
import functools

import jax
import jax.numpy as jnp
from jax import lax
from jax.experimental import pallas as pl
from jax.experimental.pallas import tpu as pltpu
from jax.sharding import PartitionSpec as P

F32 = jnp.float32
BF16 = jnp.bfloat16
NN = (((1,), (0,)), ((), ()))
NT = (((1,), (1,)), ((), ()))
TN = (((0,), (0,)), ((), ()))
TOLERANCE = 1e-5
STEPS = 8
SQUARINGS = (3, 3, 4, 5, 6, 7, 7)
WORK = pl.CostEstimate(flops=10**9, bytes_accessed=2 * 10**6, transcendentals=0)
PARAMS = pltpu.CompilerParams(vmem_limit_bytes=32 * 2**20)
VMEM = pl.BlockSpec(memory_space=pltpu.VMEM)
SMEM = pl.BlockSpec(memory_space=pltpu.SMEM)


def parts(x):
    high = x.astype(BF16)
    rest = x - high.astype(F32)
    middle = rest.astype(BF16)
    return high, middle, (rest - middle.astype(F32)).astype(BF16)


def dot1(a, b, dims=NN):
    return lax.dot_general(a, b, dims, preferred_element_type=F32)


def dot3(a, b, dims=NN):
    return dot1(a[0], b[0], dims) + (dot1(a[0], b[1], dims) + dot1(a[1], b[0], dims))


def dot6(a, b, dims=NN):
    low = dot1(a[0], b[2], dims) + dot1(a[1], b[1], dims) + dot1(a[2], b[0], dims)
    return dot1(a[0], b[0], dims) + ((dot1(a[0], b[1], dims) + dot1(a[1], b[0], dims)) + low)


def grid_of(n):
    return (
        lax.broadcasted_iota(jnp.int32, (n, n), 0),
        lax.broadcasted_iota(jnp.int32, (n, n), 1),
    )


def unit(n):
    row, column = grid_of(n)
    return jnp.where(row == column, F32(1), F32(0))


def step_size(d):
    return 1.9 / jnp.max(jnp.sum(jnp.abs(d), axis=0, keepdims=True), axis=1, keepdims=True)


def first_inverse(d, squarings):
    n = d.shape[0]
    one = unit(n)
    alpha = step_size(d)
    e = one - alpha * d
    c = jnp.sum(jnp.sum(e * one, axis=0, keepdims=True), axis=1, keepdims=True) / n
    f = e - c * one
    p, y = 1 + c, f
    for _ in range(squarings):
        rounded = f.astype(BF16)
        f = 2 * c * f + dot1(rounded, rounded)
        c = c * c
        y = p * f + (1 + c) * y + dot1(y.astype(BF16), f.astype(BF16))
        p = p * (1 + c)
    return alpha * (p * one + y)


def newton(d_parts, x, dot):
    x_parts = parts(x)
    residual = unit(x.shape[0]) - dot(d_parts, x_parts)
    return x + (dot1(x_parts[0], residual.astype(BF16)) if dot is dot3 else dot3(x_parts, parts(residual))), residual


def combine(left, right, x, out_ref):
    b1, b2, x = parts(left(1)), parts(right(1)), parts(x)
    w1, w2 = parts(dot6(b1, x)), parts(dot6(x, b2))
    out_ref[0] = left(0) - dot6(w1, b1, NT)
    out_ref[1] = dot6(w1, b2)
    out_ref[2] = right(2) - dot6(b2, w2, TN)


def merge_blocks(d, depth, d_ref, x_ref, finish):
    d_ref[...] = d
    x_ref[...], _ = newton(parts(d), first_inverse(d, SQUARINGS[min(depth, len(SQUARINGS) - 1)]), dot3)

    def going(state):
        return jnp.logical_and(state[0] < 9 * STEPS, jnp.logical_not(state[1] < TOLERANCE))

    def again(state):
        @pl.when(state[0] == STEPS)
        def _():
            x_ref[...] = step_size(d_ref[...]) * unit(d_ref.shape[0])

        x, residual = newton(parts(d_ref[...]), x_ref[...], dot6)
        x_ref[...] = x
        finish(x)
        return state[0] + 1, jnp.sum(residual * residual)

    lax.while_loop(going, again, (0, F32(1)))


def pack(core, out_ref, send_ref):
    n = out_ref.shape[-1]
    row, column = grid_of(n)
    last = out_ref[2]
    both = jnp.where(row >= column, out_ref[0], last)
    send_ref[0:n] = jnp.where(core == 0, both, out_ref[1])
    diagonal = jnp.sum(jnp.where(row == column, last, F32(0)), axis=0, keepdims=True)
    send_ref[n : n + 8] = jnp.broadcast_to(diagonal, (8, n))


def leaf_kernel(flags_ref, margin_ref, cot_ref, csc_ref, coupling_ref, out_ref, d_ref, x_ref, a_ref, b_ref, c_ref):
    n = d_ref.shape[0]
    row, column = grid_of(n)
    half_step = 0.5 / (2 * flags_ref[1]).astype(F32)

    def sector(s):
        margin = margin_ref[:, s].reshape(n, n)
        if s == 0:
            margin = jnp.where(flags_ref[0] == 0, unit(n), margin)
        inner = jnp.where(row == column, cot_ref[s : s + 1, :], F32(0)) + half_step * coupling_ref[s].astype(F32)
        m = parts(margin)
        a_ref[s] = dot6(parts(dot6(m, parts(inner))), m, NT)
        b_ref[s] = margin * csc_ref[s : s + 1, :]
        c_ref[s] = inner

    sector(1)
    sector(0)
    blocks = (a_ref, b_ref, c_ref)
    merge_blocks(
        c_ref[0] + a_ref[1], 0, d_ref, x_ref,
        lambda x: combine(lambda i: blocks[i][0], lambda i: blocks[i][1], x, out_ref),
    )


def leaf(flags, margin, cot, csc, coupling):
    n = coupling.shape[-1]
    return pl.pallas_call(
        leaf_kernel,
        out_shape=jax.ShapeDtypeStruct((3, n, n), F32),
        in_specs=[SMEM, VMEM, VMEM, VMEM, VMEM],
        out_specs=VMEM,
        scratch_shapes=[pltpu.VMEM((n, n), F32)] * 2 + [pltpu.VMEM((2, n, n), F32)] * 3,
        compiler_params=PARAMS,
        name="leaf",
    )(flags, margin, cot, csc, coupling)


def sides(upper, own_ref, other_ref):
    return (
        lambda i: jnp.where(upper, other_ref[i], own_ref[i]),
        lambda i: jnp.where(upper, own_ref[i], other_ref[i]),
    )


def merge_refs(upper, own_ref, other_ref, depth, out_ref, d_ref, x_ref, after):
    left, right = sides(upper, own_ref, other_ref)

    def finish(x):
        combine(left, right, x, out_ref)
        after()

    merge_blocks(left(2) + right(0), depth, d_ref, x_ref, finish)


def core_kernel(flags_ref, own_ref, other_ref, out_ref, send_ref, d_ref, x_ref):
    core = flags_ref[2]
    merge_refs(core == 1, own_ref, other_ref, 1, out_ref, d_ref, x_ref, lambda: pack(core, out_ref, send_ref))


def core_merge(flags, own, other):
    n = own.shape[-1]
    return pl.pallas_call(
        core_kernel,
        out_shape=(jax.ShapeDtypeStruct((3, n, n), F32), jax.ShapeDtypeStruct((n + 8, n), F32)),
        in_specs=[SMEM, VMEM, VMEM],
        out_specs=(VMEM, VMEM),
        scratch_shapes=[pltpu.VMEM((n, n), F32)] * 2,
        compiler_params=PARAMS,
        name="core_merge",
    )(flags, own, other)


def unpack(core, came_ref, swapped_ref, other_ref):
    n = other_ref.shape[-1]
    row, column = grid_of(n)
    both = jnp.where(core == 0, came_ref[0:n], swapped_ref[0:n])
    diagonal = jnp.where(core == 0, came_ref[n : n + 1], swapped_ref[n : n + 1])
    turned = both.T
    other_ref[0] = jnp.where(row >= column, both, turned)
    other_ref[1] = jnp.where(core == 0, swapped_ref[0:n], came_ref[0:n])
    other_ref[2] = jnp.where(row == column, diagonal, jnp.where(row < column, both, turned))


def chip_kernel(level, flags_ref, own_ref, came_ref, swapped_ref, out_ref, send_ref, d_ref, x_ref, other_ref):
    core = flags_ref[2]
    active = flags_ref[4 + 2 * level] == 1

    @pl.when(active)
    def _():
        unpack(core, came_ref, swapped_ref, other_ref)
        merge_refs(
            flags_ref[5 + 2 * level] == 1, own_ref, other_ref, level + 2, out_ref, d_ref, x_ref,
            lambda: pack(core, out_ref, send_ref),
        )

    @pl.when(jnp.logical_not(active))
    def _():
        out_ref[...] = own_ref[...]
        send_ref[...] = jnp.zeros_like(send_ref)


def chip_merge(level, flags, own, came, swapped):
    n = own.shape[-1]
    return pl.pallas_call(
        functools.partial(chip_kernel, level),
        out_shape=(jax.ShapeDtypeStruct((3, n, n), F32), jax.ShapeDtypeStruct((n + 8, n), F32)),
        in_specs=[SMEM, VMEM, VMEM, VMEM],
        out_specs=(VMEM, VMEM),
        scratch_shapes=[pltpu.VMEM((n, n), F32)] * 2 + [pltpu.VMEM((3, n, n), F32)],
        compiler_params=PARAMS,
        name="chip_merge",
    )(flags, own, came, swapped)


def last_kernel(level, flags_ref, own_ref, came_ref, swapped_ref, mine_ref, next_ref, d_ref, x_ref, turned_ref, other_ref):
    n = d_ref.shape[0]
    core = flags_ref[2]
    wide, rows = mine_ref.shape[1:]
    active = flags_ref[4 + 2 * level] == 1
    upper = flags_ref[5 + 2 * level] == 1
    chip = flags_ref[0] // 2
    block = pl.ds(pl.multiple_of(chip // 2 * (4 * wide), 4 * wide), 4 * wide)

    def cut(wanted, array):
        moved = pltpu.roll(array, (n - flags_ref[3] * rows) % n, axis=1)[:, :rows]
        piece = moved[:wide]
        for i in range(1, 4):
            piece = jnp.where(wanted == i, moved[i * wide : (i + 1) * wide], piece)
        return piece

    @pl.when(active)
    def _():
        unpack(core, came_ref, swapped_ref, other_ref)
        left, right = sides(upper, own_ref, other_ref)
        turned_ref[...] = right(1).T

        def finish(x):
            x = parts(x)
            b1, b2 = parts(left(1)), parts(right(1))
            b1_rows = jnp.where(upper, other_ref[1, block, :], own_ref[1, block, :])
            w1, w2 = parts(dot6(parts(b1_rows), x)), parts(dot6(parts(turned_ref[block, :]), x))
            a_rows = jnp.where(upper, other_ref[0, block, :], own_ref[0, block, :])
            c_rows = jnp.where(upper, own_ref[2, block, :], other_ref[2, block, :])
            results = (a_rows - dot6(w1, b1, NT), dot6(w2, b1, NT), c_rows - dot6(w2, b2))
            for i, result in enumerate(results):
                mine_ref[i] = cut(chip % 2 * 2 + core, result)
                next_ref[i] = cut((1 - chip % 2) * 2 + core, result)

        merge_blocks(left(2) + right(0), level + 2, d_ref, x_ref, finish)

    @pl.when(jnp.logical_not(active))
    def _():
        mine_ref[...] = jnp.zeros_like(mine_ref)
        next_ref[...] = jnp.zeros_like(next_ref)


def last_merge(level, flags, own, came, swapped, wide, rows):
    n = own.shape[-1]
    return pl.pallas_call(
        functools.partial(last_kernel, level),
        out_shape=(jax.ShapeDtypeStruct((3, wide, rows), F32),) * 2,
        in_specs=[SMEM, VMEM, VMEM, VMEM],
        out_specs=(VMEM, VMEM),
        scratch_shapes=[pltpu.VMEM((n, n), F32)] * 3 + [pltpu.VMEM((3, n, n), F32)],
        compiler_params=PARAMS,
        name="last_merge",
    )(flags, own, came, swapped)


def pick_kernel(level, flags_ref, mine_ref, brought_ref, a_ref, b_ref, c_ref):
    for i, ref in enumerate((a_ref, b_ref, c_ref)):
        ref[...] = jnp.where(flags_ref[4 + 2 * level] == 1, mine_ref[i], brought_ref[i])


def pick(level, flags, mine, brought):
    return pl.pallas_call(
        functools.partial(pick_kernel, level),
        out_shape=(jax.ShapeDtypeStruct(mine.shape[1:], F32),) * 3,
        in_specs=[SMEM, VMEM, VMEM],
        out_specs=(VMEM,) * 3,
        compiler_params=pltpu.CompilerParams(vmem_limit_bytes=2**20),
        name="pick",
    )(flags, mine, brought)


def inner_kernel(own_ref, out_ref):
    shards, _, rows, depth = own_ref.shape
    n = shards * rows
    first = own_ref[:, 0].reshape(n, depth)
    second = own_ref[:, 1].reshape(n, depth)
    out_ref[...] = dot1(first, second, NT).reshape(shards, rows, n)


def margin_kernel(own_ref, before_ref, inner_ref, out_ref):
    shards, _, rows, depth = own_ref.shape
    n = shards * rows
    first = own_ref[:, 0].reshape(n, depth)
    out_ref[:, 0] = dot1(before_ref[...].reshape(n, depth), first, NT).reshape(shards, rows, n)
    out_ref[:, 1] = inner_ref[...]


def inner_parts(own):
    shards, _, rows, _ = own.shape
    return pl.pallas_call(
        inner_kernel,
        out_shape=jax.ShapeDtypeStruct((shards, rows, shards * rows), F32),
        in_specs=[VMEM],
        out_specs=VMEM,
        compiler_params=PARAMS,
        cost_estimate=WORK,
        name="inner_parts",
    )(own)


def margin_parts(own, before, inner):
    shards, sectors, rows, _ = own.shape
    return pl.pallas_call(
        margin_kernel,
        out_shape=jax.ShapeDtypeStruct((shards, sectors, rows, shards * rows), F32),
        in_specs=[VMEM, VMEM, VMEM],
        out_specs=VMEM,
        compiler_params=PARAMS,
        name="margin_parts",
    )(own, before, inner)


def total_kernel(points, partial_ref, out_ref):
    total = partial_ref[0]
    for shard in range(1, partial_ref.shape[0]):
        total = total + partial_ref[shard]
    total = total / points
    for shard in range(partial_ref.shape[0]):
        out_ref[shard] = total


def total_for_all(partial, points):
    return pl.pallas_call(
        functools.partial(total_kernel, points),
        out_shape=jax.ShapeDtypeStruct(partial.shape, F32),
        in_specs=[VMEM],
        out_specs=VMEM,
        compiler_params=PARAMS,
        name="total_for_all",
    )(partial)


def exchange(array):
    return lax.all_to_all(array, "chan", split_axis=0, concat_axis=0, tiled=True)


YS = 8
ENDS = (0, 3, 4, 7)


def place(position):
    return position // (2 * YS), position // 2 % YS, position % 2


def spot(x, y, core):
    return (x * YS + y) * 2 + core


def levels(xs):
    result = [
        (lambda x, y: (x, y ^ 1), range(YS), ("y", 0)),
        (lambda x, y: (x, y ^ 2), ENDS, ("y", 1)),
        (lambda x, y: (x, YS - 1 - y), ENDS, ("y", 2)),
    ]
    for bit in range(xs.bit_length() - 1):
        mask = 2 ** (bit + 1) - 1
        result.append((lambda x, y, mask=mask: (x ^ mask, y), ENDS, ("x", bit)))
    return result


def per_device(surface_functions, channel_rates, coupling):
    sectors, rows, points = surface_functions.shape
    n = channel_rates.shape[1]
    shards = lax.axis_size("chan")
    count = lax.axis_size("sector")
    position = lax.axis_index("sector")
    plan = levels(count // (2 * YS))
    cut = surface_functions.reshape(sectors, rows, shards, points // shards)
    own = exchange(jnp.transpose(cut, (2, 0, 1, 3)))
    own, position, channel_rates = lax.optimization_barrier((own, position, channel_rates))
    x, y, core = place(position)
    at_end = (y == ENDS[0]) | (y == ENDS[1]) | (y == ENDS[2]) | (y == ENDS[3])
    words = [position, jnp.int32(count), core, lax.axis_index("chan")]
    for _, takers, (axis, bit) in plan:
        words.append(jnp.int32(1) if len(takers) == YS else at_end.astype(jnp.int32))
        words.append((x if axis == "x" else y) >> bit & 1)
    flags = jnp.stack([jnp.asarray(word, jnp.int32) for word in words])

    step = 1.0 / (sectors * count)
    cot = channel_rates / jnp.tanh(channel_rates * step)
    csc = channel_rates / jnp.sinh(channel_rates * step)

    before = lax.ppermute(own[:, sectors - 1], "sector", [(i, i + 1) for i in range(count - 1)])
    inner, cot, csc, flags, before = lax.optimization_barrier((inner_parts(own), cot, csc, flags, before))
    partial = exchange(margin_parts(own, before, inner))
    margin = exchange(total_for_all(partial, points))

    packed = leaf(flags, margin, cot, csc, coupling)
    cores = [(i, i ^ 1) for i in range(count)]
    packed, send = core_merge(flags, packed, lax.ppermute(packed, "sector", cores))
    wide = n // count
    for level, (partner, takers, _) in enumerate(plan):
        pairs = []
        for i in range(count):
            xi, yi, ci = place(i)
            if yi in takers:
                pairs.append((spot(*partner(xi, yi), ci), i))
        came = lax.ppermute(send, "sector", pairs)
        swapped = lax.ppermute(came, "sector", cores)
        if level < len(plan) - 1:
            packed, send = chip_merge(level, flags, packed, came, swapped)
        else:
            mine, for_next = last_merge(level, flags, packed, came, swapped, wide, rows)
    pairs = []
    for i in range(count):
        xi, yi, ci = place(i)
        if yi not in ENDS:
            pairs.append((spot(xi, yi ^ 1, ci), i))
    brought = lax.ppermute(for_next, "sector", pairs)
    return tuple(block.T for block in pick(len(plan) - 1, flags, mine, brought))


def solution(mesh):
    placed = (P("sector", "chan", None), P("sector", None), P("sector", None, None))
    return jax.shard_map(
        per_device,
        mesh=mesh,
        in_specs=placed,
        out_specs=(P("chan", "sector"), P("chan", "sector"), P("chan", "sector")),
        check_vma=False,
    )
```

```python
import functools

import jax
import jax.numpy as jnp
from jax import lax
from jax.experimental import pallas as pl
from jax.experimental.pallas import tpu as pltpu
from jax.sharding import PartitionSpec as P

F32 = jnp.float32
BF16 = jnp.bfloat16
NN = (((1,), (0,)), ((), ()))
NT = (((1,), (1,)), ((), ()))
TN = (((0,), (0,)), ((), ()))
TOLERANCE = 1e-5
STEPS = 8
SQUARINGS = (3, 3, 4, 5, 6, 7, 7)
WORK = pl.CostEstimate(flops=10**9, bytes_accessed=2 * 10**6, transcendentals=0)
PARAMS = pltpu.CompilerParams(vmem_limit_bytes=32 * 2**20)
VMEM = pl.BlockSpec(memory_space=pltpu.VMEM)
SMEM = pl.BlockSpec(memory_space=pltpu.SMEM)


def parts(x):
    high = x.astype(BF16)
    rest = x - high.astype(F32)
    middle = rest.astype(BF16)
    return high, middle, (rest - middle.astype(F32)).astype(BF16)


def dot1(a, b, dims=NN):
    return lax.dot_general(a, b, dims, preferred_element_type=F32)


def dot3(a, b, dims=NN):
    return dot1(a[0], b[0], dims) + (dot1(a[0], b[1], dims) + dot1(a[1], b[0], dims))


def dot6(a, b, dims=NN):
    low = dot1(a[0], b[2], dims) + dot1(a[1], b[1], dims) + dot1(a[2], b[0], dims)
    return dot1(a[0], b[0], dims) + ((dot1(a[0], b[1], dims) + dot1(a[1], b[0], dims)) + low)


def grid_of(n):
    return (
        lax.broadcasted_iota(jnp.int32, (n, n), 0),
        lax.broadcasted_iota(jnp.int32, (n, n), 1),
    )


def unit(n):
    row, column = grid_of(n)
    return jnp.where(row == column, F32(1), F32(0))


def step_size(d):
    return 1.9 / jnp.max(jnp.sum(jnp.abs(d), axis=0, keepdims=True), axis=1, keepdims=True)


def first_inverse(d, squarings):
    n = d.shape[0]
    one = unit(n)
    alpha = step_size(d)
    e = one - alpha * d
    c = jnp.sum(jnp.sum(e * one, axis=0, keepdims=True), axis=1, keepdims=True) / n
    f = e - c * one
    p, y = 1 + c, f
    for _ in range(squarings):
        rounded = f.astype(BF16)
        f = 2 * c * f + dot1(rounded, rounded)
        c = c * c
        y = p * f + (1 + c) * y + dot1(y.astype(BF16), f.astype(BF16))
        p = p * (1 + c)
    return alpha * (p * one + y)


def newton(d_parts, x, dot):
    x_parts = parts(x)
    residual = unit(x.shape[0]) - dot(d_parts, x_parts)
    return x + (dot1(x_parts[0], residual.astype(BF16)) if dot is dot3 else dot3(x_parts, parts(residual))), residual


def combine(left, right, x, out_ref):
    b1, b2, x = parts(left(1)), parts(right(1)), parts(x)
    w1, w2 = parts(dot6(b1, x)), parts(dot6(x, b2))
    out_ref[0] = left(0) - dot6(w1, b1, NT)
    out_ref[1] = dot6(w1, b2)
    out_ref[2] = right(2) - dot6(b2, w2, TN)


def merge_blocks(d, depth, d_ref, x_ref, finish):
    d_ref[...] = d
    x_ref[...], _ = newton(parts(d), first_inverse(d, SQUARINGS[min(depth, len(SQUARINGS) - 1)]), dot3)

    def going(state):
        return jnp.logical_and(state[0] < 9 * STEPS, jnp.logical_not(state[1] < TOLERANCE))

    def again(state):
        @pl.when(state[0] == STEPS)
        def _():
            x_ref[...] = step_size(d_ref[...]) * unit(d_ref.shape[0])

        x, residual = newton(parts(d_ref[...]), x_ref[...], dot6)
        x_ref[...] = x
        finish(x)
        return state[0] + 1, jnp.sum(residual * residual)

    lax.while_loop(going, again, (0, F32(1)))


def pack(core, out_ref, send_ref):
    n = out_ref.shape[-1]
    row, column = grid_of(n)
    last = out_ref[2]
    both = jnp.where(row >= column, out_ref[0], last)
    send_ref[0:n] = jnp.where(core == 0, both, out_ref[1])
    diagonal = jnp.sum(jnp.where(row == column, last, F32(0)), axis=0, keepdims=True)
    send_ref[n : n + 8] = jnp.broadcast_to(diagonal, (8, n))


def leaf_kernel(flags_ref, margin_ref, cot_ref, csc_ref, coupling_ref, out_ref, d_ref, x_ref, a_ref, b_ref, c_ref):
    n = d_ref.shape[0]
    row, column = grid_of(n)
    half_step = 0.5 / (2 * flags_ref[1]).astype(F32)

    def sector(s):
        margin = margin_ref[:, s].reshape(n, n)
        if s == 0:
            margin = jnp.where(flags_ref[0] == 0, unit(n), margin)
        inner = jnp.where(row == column, cot_ref[s : s + 1, :], F32(0)) + half_step * coupling_ref[s].astype(F32)
        m = parts(margin)
        a_ref[s] = dot6(parts(dot6(m, parts(inner))), m, NT)
        b_ref[s] = margin * csc_ref[s : s + 1, :]
        c_ref[s] = inner

    sector(1)
    sector(0)
    blocks = (a_ref, b_ref, c_ref)
    merge_blocks(
        c_ref[0] + a_ref[1], 0, d_ref, x_ref,
        lambda x: combine(lambda i: blocks[i][0], lambda i: blocks[i][1], x, out_ref),
    )


def leaf(flags, margin, cot, csc, coupling):
    n = coupling.shape[-1]
    return pl.pallas_call(
        leaf_kernel,
        out_shape=jax.ShapeDtypeStruct((3, n, n), F32),
        in_specs=[SMEM, VMEM, VMEM, VMEM, VMEM],
        out_specs=VMEM,
        scratch_shapes=[pltpu.VMEM((n, n), F32)] * 2 + [pltpu.VMEM((2, n, n), F32)] * 3,
        compiler_params=PARAMS,
        name="leaf",
    )(flags, margin, cot, csc, coupling)


def sides(upper, own_ref, other_ref):
    return (
        lambda i: jnp.where(upper, other_ref[i], own_ref[i]),
        lambda i: jnp.where(upper, own_ref[i], other_ref[i]),
    )


def merge_refs(upper, own_ref, other_ref, depth, out_ref, d_ref, x_ref, after):
    left, right = sides(upper, own_ref, other_ref)

    def finish(x):
        combine(left, right, x, out_ref)
        after()

    merge_blocks(left(2) + right(0), depth, d_ref, x_ref, finish)


def core_kernel(flags_ref, own_ref, other_ref, out_ref, send_ref, d_ref, x_ref):
    core = flags_ref[2]
    merge_refs(core == 1, own_ref, other_ref, 1, out_ref, d_ref, x_ref, lambda: pack(core, out_ref, send_ref))


def core_merge(flags, own, other):
    n = own.shape[-1]
    return pl.pallas_call(
        core_kernel,
        out_shape=(jax.ShapeDtypeStruct((3, n, n), F32), jax.ShapeDtypeStruct((n + 8, n), F32)),
        in_specs=[SMEM, VMEM, VMEM],
        out_specs=(VMEM, VMEM),
        scratch_shapes=[pltpu.VMEM((n, n), F32)] * 2,
        compiler_params=PARAMS,
        name="core_merge",
    )(flags, own, other)


def unpack(core, came_ref, swapped_ref, other_ref):
    n = other_ref.shape[-1]
    row, column = grid_of(n)
    both = jnp.where(core == 0, came_ref[0:n], swapped_ref[0:n])
    diagonal = jnp.where(core == 0, came_ref[n : n + 1], swapped_ref[n : n + 1])
    turned = both.T
    other_ref[0] = jnp.where(row >= column, both, turned)
    other_ref[1] = jnp.where(core == 0, swapped_ref[0:n], came_ref[0:n])
    other_ref[2] = jnp.where(row == column, diagonal, jnp.where(row < column, both, turned))


def chip_kernel(level, flags_ref, own_ref, came_ref, swapped_ref, out_ref, send_ref, d_ref, x_ref, other_ref):
    core = flags_ref[2]
    active = flags_ref[4 + 2 * level] == 1

    @pl.when(active)
    def _():
        unpack(core, came_ref, swapped_ref, other_ref)
        merge_refs(
            flags_ref[5 + 2 * level] == 1, own_ref, other_ref, level + 2, out_ref, d_ref, x_ref,
            lambda: pack(core, out_ref, send_ref),
        )

    @pl.when(jnp.logical_not(active))
    def _():
        out_ref[...] = own_ref[...]
        send_ref[...] = jnp.zeros_like(send_ref)


def chip_merge(level, flags, own, came, swapped):
    n = own.shape[-1]
    return pl.pallas_call(
        functools.partial(chip_kernel, level),
        out_shape=(jax.ShapeDtypeStruct((3, n, n), F32), jax.ShapeDtypeStruct((n + 8, n), F32)),
        in_specs=[SMEM, VMEM, VMEM, VMEM],
        out_specs=(VMEM, VMEM),
        scratch_shapes=[pltpu.VMEM((n, n), F32)] * 2 + [pltpu.VMEM((3, n, n), F32)],
        compiler_params=PARAMS,
        name="chip_merge",
    )(flags, own, came, swapped)


def last_kernel(level, flags_ref, own_ref, came_ref, swapped_ref, mine_ref, next_ref, d_ref, x_ref, turned_ref, other_ref):
    n = d_ref.shape[0]
    core = flags_ref[2]
    wide, rows = mine_ref.shape[1:]
    active = flags_ref[4 + 2 * level] == 1
    upper = flags_ref[5 + 2 * level] == 1
    chip = flags_ref[0] // 2
    block = pl.ds(pl.multiple_of(chip // 2 * (4 * wide), 4 * wide), 4 * wide)

    def cut(wanted, array):
        moved = pltpu.roll(array, (n - flags_ref[3] * rows) % n, axis=1)[:, :rows]
        piece = moved[:wide]
        for i in range(1, 4):
            piece = jnp.where(wanted == i, moved[i * wide : (i + 1) * wide], piece)
        return piece

    @pl.when(active)
    def _():
        unpack(core, came_ref, swapped_ref, other_ref)
        left, right = sides(upper, own_ref, other_ref)
        turned_ref[...] = right(1).T

        def finish(x):
            x = parts(x)
            b1, b2 = parts(left(1)), parts(right(1))
            b1_rows = jnp.where(upper, other_ref[1, block, :], own_ref[1, block, :])
            w1, w2 = parts(dot6(parts(b1_rows), x)), parts(dot6(parts(turned_ref[block, :]), x))
            a_rows = jnp.where(upper, other_ref[0, block, :], own_ref[0, block, :])
            c_rows = jnp.where(upper, own_ref[2, block, :], other_ref[2, block, :])
            results = (a_rows - dot6(w1, b1, NT), dot6(w2, b1, NT), c_rows - dot6(w2, b2))
            for i, result in enumerate(results):
                mine_ref[i] = cut(chip % 2 * 2 + core, result)
                next_ref[i] = cut((1 - chip % 2) * 2 + core, result)

        merge_blocks(left(2) + right(0), level + 2, d_ref, x_ref, finish)

    @pl.when(jnp.logical_not(active))
    def _():
        mine_ref[...] = jnp.zeros_like(mine_ref)
        next_ref[...] = jnp.zeros_like(next_ref)


def last_merge(level, flags, own, came, swapped, wide, rows):
    n = own.shape[-1]
    return pl.pallas_call(
        functools.partial(last_kernel, level),
        out_shape=(jax.ShapeDtypeStruct((3, wide, rows), F32),) * 2,
        in_specs=[SMEM, VMEM, VMEM, VMEM],
        out_specs=(VMEM, VMEM),
        scratch_shapes=[pltpu.VMEM((n, n), F32)] * 3 + [pltpu.VMEM((3, n, n), F32)],
        compiler_params=PARAMS,
        name="last_merge",
    )(flags, own, came, swapped)


def pick_kernel(level, flags_ref, mine_ref, brought_ref, a_ref, b_ref, c_ref):
    for i, ref in enumerate((a_ref, b_ref, c_ref)):
        ref[...] = jnp.where(flags_ref[4 + 2 * level] == 1, mine_ref[i], brought_ref[i])


def pick(level, flags, mine, brought):
    return pl.pallas_call(
        functools.partial(pick_kernel, level),
        out_shape=(jax.ShapeDtypeStruct(mine.shape[1:], F32),) * 3,
        in_specs=[SMEM, VMEM, VMEM],
        out_specs=(VMEM,) * 3,
        compiler_params=pltpu.CompilerParams(vmem_limit_bytes=2**20),
        name="pick",
    )(flags, mine, brought)


def shares_kernel(whole_ref, out_ref):
    depth = out_ref.shape[-1]
    for shard in range(out_ref.shape[0]):
        out_ref[shard] = whole_ref[:, :, shard * depth : (shard + 1) * depth]


def shares(surface_functions, shards):
    sectors, rows, points = surface_functions.shape
    return pl.pallas_call(
        shares_kernel,
        out_shape=jax.ShapeDtypeStruct((shards, sectors, rows, points // shards), BF16),
        in_specs=[VMEM],
        out_specs=VMEM,
        compiler_params=PARAMS,
        name="shares",
    )(surface_functions)


def inner_kernel(own_ref, out_ref):
    shards, _, rows, depth = own_ref.shape
    n = shards * rows
    first = own_ref[:, 0].reshape(n, depth)
    second = own_ref[:, 1].reshape(n, depth)
    out_ref[...] = dot1(first, second, NT).reshape(shards, rows, n)


def margin_kernel(own_ref, before_ref, inner_ref, out_ref):
    shards, _, rows, depth = own_ref.shape
    n = shards * rows
    first = own_ref[:, 0].reshape(n, depth)
    out_ref[:, 0] = dot1(before_ref[...].reshape(n, depth), first, NT).reshape(shards, rows, n)
    out_ref[:, 1] = inner_ref[...]


def inner_parts(own):
    shards, _, rows, _ = own.shape
    return pl.pallas_call(
        inner_kernel,
        out_shape=jax.ShapeDtypeStruct((shards, rows, shards * rows), F32),
        in_specs=[VMEM],
        out_specs=VMEM,
        compiler_params=PARAMS,
        cost_estimate=WORK,
        name="inner_parts",
    )(own)


def margin_parts(own, before, inner):
    shards, sectors, rows, _ = own.shape
    return pl.pallas_call(
        margin_kernel,
        out_shape=jax.ShapeDtypeStruct((shards, sectors, rows, shards * rows), F32),
        in_specs=[VMEM, VMEM, VMEM],
        out_specs=VMEM,
        compiler_params=PARAMS,
        name="margin_parts",
    )(own, before, inner)


def total_kernel(points, partial_ref, out_ref):
    total = partial_ref[0]
    for shard in range(1, partial_ref.shape[0]):
        total = total + partial_ref[shard]
    total = total / points
    for shard in range(partial_ref.shape[0]):
        out_ref[shard] = total


def total_for_all(partial, points):
    return pl.pallas_call(
        functools.partial(total_kernel, points),
        out_shape=jax.ShapeDtypeStruct(partial.shape, F32),
        in_specs=[VMEM],
        out_specs=VMEM,
        compiler_params=PARAMS,
        name="total_for_all",
    )(partial)


def exchange(array):
    return lax.all_to_all(array, "chan", split_axis=0, concat_axis=0, tiled=True)


YS = 8
ENDS = (0, 3, 4, 7)


def place(position):
    return position // (2 * YS), position // 2 % YS, position % 2


def spot(x, y, core):
    return (x * YS + y) * 2 + core


def levels(xs):
    result = [
        (lambda x, y: (x, y ^ 1), range(YS), ("y", 0)),
        (lambda x, y: (x, y ^ 2), ENDS, ("y", 1)),
        (lambda x, y: (x, YS - 1 - y), ENDS, ("y", 2)),
    ]
    for bit in range(xs.bit_length() - 1):
        mask = 2 ** (bit + 1) - 1
        result.append((lambda x, y, mask=mask: (x ^ mask, y), ENDS, ("x", bit)))
    return result


def per_device(surface_functions, channel_rates, coupling):
    sectors, rows, points = surface_functions.shape
    n = channel_rates.shape[1]
    shards = lax.axis_size("chan")
    count = lax.axis_size("sector")
    position = lax.axis_index("sector")
    plan = levels(count // (2 * YS))
    own = exchange(shares(surface_functions, shards))
    own, position, shard, channel_rates = lax.optimization_barrier(
        (own, position, lax.axis_index("chan"), channel_rates)
    )
    x, y, core = place(position)
    at_end = (y == ENDS[0]) | (y == ENDS[1]) | (y == ENDS[2]) | (y == ENDS[3])
    words = [position, jnp.int32(count), core, shard]
    for _, takers, (axis, bit) in plan:
        words.append(jnp.int32(1) if len(takers) == YS else at_end.astype(jnp.int32))
        words.append((x if axis == "x" else y) >> bit & 1)
    flags = jnp.stack([jnp.asarray(word, jnp.int32) for word in words])

    step = 1.0 / (sectors * count)
    cot = channel_rates / jnp.tanh(channel_rates * step)
    csc = channel_rates / jnp.sinh(channel_rates * step)

    before = lax.ppermute(own[:, sectors - 1], "sector", [(i, i + 1) for i in range(count - 1)])
    inner, cot, csc, flags, before = lax.optimization_barrier((inner_parts(own), cot, csc, flags, before))
    partial = exchange(margin_parts(own, before, inner))
    margin = exchange(total_for_all(partial, points))

    packed = leaf(flags, margin, cot, csc, coupling)
    cores = [(i, i ^ 1) for i in range(count)]
    packed, send = core_merge(flags, packed, lax.ppermute(packed, "sector", cores))
    wide = n // count
    for level, (partner, takers, _) in enumerate(plan):
        pairs = []
        for i in range(count):
            xi, yi, ci = place(i)
            if yi in takers:
                pairs.append((spot(*partner(xi, yi), ci), i))
        came = lax.ppermute(send, "sector", pairs)
        swapped = lax.ppermute(came, "sector", cores)
        if level < len(plan) - 1:
            packed, send = chip_merge(level, flags, packed, came, swapped)
        else:
            mine, for_next = last_merge(level, flags, packed, came, swapped, wide, rows)
    pairs = []
    for i in range(count):
        xi, yi, ci = place(i)
        if yi not in ENDS:
            pairs.append((spot(xi, yi ^ 1, ci), i))
    brought = lax.ppermute(for_next, "sector", pairs)
    return tuple(block.T for block in pick(len(plan) - 1, flags, mine, brought))


def solution(mesh):
    placed = (P("sector", "chan", None), P("sector", None), P("sector", None, None))
    return jax.shard_map(
        per_device,
        mesh=mesh,
        in_specs=placed,
        out_specs=(P("chan", "sector"), P("chan", "sector"), P("chan", "sector")),
        check_vma=False,
    )
```

```python
import functools

import jax
import jax.numpy as jnp
from jax import lax
from jax.experimental import pallas as pl
from jax.experimental.pallas import tpu as pltpu
from jax.sharding import PartitionSpec as P

F32 = jnp.float32
BF16 = jnp.bfloat16
NN = (((1,), (0,)), ((), ()))
NT = (((1,), (1,)), ((), ()))
TN = (((0,), (0,)), ((), ()))
TOLERANCE = 1e-5
STEPS = 8
SQUARINGS = (3, 3, 4, 5, 6, 7, 7)
WORK = pl.CostEstimate(flops=10**9, bytes_accessed=2 * 10**6, transcendentals=0)
PARAMS = pltpu.CompilerParams(vmem_limit_bytes=32 * 2**20)
VMEM = pl.BlockSpec(memory_space=pltpu.VMEM)
SMEM = pl.BlockSpec(memory_space=pltpu.SMEM)


def parts(x):
    high = x.astype(BF16)
    rest = x - high.astype(F32)
    middle = rest.astype(BF16)
    return high, middle, (rest - middle.astype(F32)).astype(BF16)


def dot1(a, b, dims=NN):
    return lax.dot_general(a, b, dims, preferred_element_type=F32)


def dot3(a, b, dims=NN):
    return dot1(a[0], b[0], dims) + (dot1(a[0], b[1], dims) + dot1(a[1], b[0], dims))


def dot6(a, b, dims=NN):
    low = dot1(a[0], b[2], dims) + dot1(a[1], b[1], dims) + dot1(a[2], b[0], dims)
    return dot1(a[0], b[0], dims) + ((dot1(a[0], b[1], dims) + dot1(a[1], b[0], dims)) + low)


def grid_of(n):
    return (
        lax.broadcasted_iota(jnp.int32, (n, n), 0),
        lax.broadcasted_iota(jnp.int32, (n, n), 1),
    )


def unit(n):
    row, column = grid_of(n)
    return jnp.where(row == column, F32(1), F32(0))


def step_size(d):
    return 1.9 / jnp.max(jnp.sum(jnp.abs(d), axis=0, keepdims=True), axis=1, keepdims=True)


def first_inverse(d, squarings):
    n = d.shape[0]
    one = unit(n)
    alpha = step_size(d)
    e = one - alpha * d
    c = jnp.sum(jnp.sum(e * one, axis=0, keepdims=True), axis=1, keepdims=True) / n
    f = e - c * one
    p, y = 1 + c, f
    for _ in range(squarings):
        rounded = f.astype(BF16)
        f = 2 * c * f + dot1(rounded, rounded)
        c = c * c
        y = p * f + (1 + c) * y + dot1(y.astype(BF16), f.astype(BF16))
        p = p * (1 + c)
    return alpha * (p * one + y)


def newton(d_parts, x, dot):
    x_parts = parts(x)
    residual = unit(x.shape[0]) - dot(d_parts, x_parts)
    return x + (dot1(x_parts[0], residual.astype(BF16)) if dot is dot3 else dot3(x_parts, parts(residual))), residual


def combine(left, right, x, out_ref):
    b1, b2, x = parts(left(1)), parts(right(1)), parts(x)
    w1, w2 = parts(dot6(b1, x)), parts(dot6(x, b2))
    out_ref[0] = left(0) - dot6(w1, b1, NT)
    out_ref[1] = dot6(w1, b2)
    out_ref[2] = right(2) - dot6(b2, w2, TN)


def merge_blocks(d, depth, d_ref, x_ref, finish):
    d_ref[...] = d
    x_ref[...], _ = newton(parts(d), first_inverse(d, SQUARINGS[min(depth, len(SQUARINGS) - 1)]), dot3)

    def going(state):
        return jnp.logical_and(state[0] < 9 * STEPS, jnp.logical_not(state[1] < TOLERANCE))

    def again(state):
        @pl.when(state[0] == STEPS)
        def _():
            x_ref[...] = step_size(d_ref[...]) * unit(d_ref.shape[0])

        x, residual = newton(parts(d_ref[...]), x_ref[...], dot6)
        x_ref[...] = x
        finish(x)
        return state[0] + 1, jnp.sum(residual * residual)

    lax.while_loop(going, again, (0, F32(1)))


def pack(core, out_ref, send_ref):
    n = out_ref.shape[-1]
    row, column = grid_of(n)
    last = out_ref[2]
    both = jnp.where(row >= column, out_ref[0], last)
    send_ref[0:n] = jnp.where(core == 0, both, out_ref[1])
    diagonal = jnp.sum(jnp.where(row == column, last, F32(0)), axis=0, keepdims=True)
    send_ref[n : n + 8] = jnp.broadcast_to(diagonal, (8, n))


def leaf_kernel(flags_ref, margin_ref, cot_ref, csc_ref, coupling_ref, out_ref, d_ref, x_ref, a_ref, b_ref, c_ref):
    n = d_ref.shape[0]
    row, column = grid_of(n)
    half_step = 0.5 / (2 * flags_ref[1]).astype(F32)

    def sector(s):
        margin = margin_ref[:, s].reshape(n, n)
        if s == 0:
            margin = jnp.where(flags_ref[0] == 0, unit(n), margin)
        inner = jnp.where(row == column, cot_ref[s : s + 1, :], F32(0)) + half_step * coupling_ref[s].astype(F32)
        m = parts(margin)
        a_ref[s] = dot6(parts(dot6(m, parts(inner))), m, NT)
        b_ref[s] = margin * csc_ref[s : s + 1, :]
        c_ref[s] = inner

    sector(1)
    sector(0)
    blocks = (a_ref, b_ref, c_ref)
    merge_blocks(
        c_ref[0] + a_ref[1], 0, d_ref, x_ref,
        lambda x: combine(lambda i: blocks[i][0], lambda i: blocks[i][1], x, out_ref),
    )


def leaf(flags, margin, cot, csc, coupling):
    n = coupling.shape[-1]
    return pl.pallas_call(
        leaf_kernel,
        out_shape=jax.ShapeDtypeStruct((3, n, n), F32),
        in_specs=[SMEM, VMEM, VMEM, VMEM, VMEM],
        out_specs=VMEM,
        scratch_shapes=[pltpu.VMEM((n, n), F32)] * 2 + [pltpu.VMEM((2, n, n), F32)] * 3,
        compiler_params=PARAMS,
        name="leaf",
    )(flags, margin, cot, csc, coupling)


def sides(upper, own_ref, other_ref):
    return (
        lambda i: jnp.where(upper, other_ref[i], own_ref[i]),
        lambda i: jnp.where(upper, own_ref[i], other_ref[i]),
    )


def merge_refs(upper, own_ref, other_ref, depth, out_ref, d_ref, x_ref, after):
    left, right = sides(upper, own_ref, other_ref)

    def finish(x):
        combine(left, right, x, out_ref)
        after()

    merge_blocks(left(2) + right(0), depth, d_ref, x_ref, finish)


def core_kernel(flags_ref, own_ref, other_ref, out_ref, send_ref, d_ref, x_ref):
    core = flags_ref[2]
    merge_refs(core == 1, own_ref, other_ref, 1, out_ref, d_ref, x_ref, lambda: pack(core, out_ref, send_ref))


def core_merge(flags, own, other):
    n = own.shape[-1]
    return pl.pallas_call(
        core_kernel,
        out_shape=(jax.ShapeDtypeStruct((3, n, n), F32), jax.ShapeDtypeStruct((n + 8, n), F32)),
        in_specs=[SMEM, VMEM, VMEM],
        out_specs=(VMEM, VMEM),
        scratch_shapes=[pltpu.VMEM((n, n), F32)] * 2,
        compiler_params=PARAMS,
        name="core_merge",
    )(flags, own, other)


def unpack(core, came_ref, swapped_ref, other_ref):
    n = other_ref.shape[-1]
    row, column = grid_of(n)
    both = jnp.where(core == 0, came_ref[0:n], swapped_ref[0:n])
    diagonal = jnp.where(core == 0, came_ref[n : n + 1], swapped_ref[n : n + 1])
    turned = both.T
    other_ref[0] = jnp.where(row >= column, both, turned)
    other_ref[1] = jnp.where(core == 0, swapped_ref[0:n], came_ref[0:n])
    other_ref[2] = jnp.where(row == column, diagonal, jnp.where(row < column, both, turned))


def pack_for_last(flags_ref, level, rows, block, out_ref, send_ref, turned_ref):
    n = out_ref.shape[-1]
    half = n // 2
    row, column = grid_of(n)
    both = jnp.where(row >= column, out_ref[0], out_ref[2])
    send_ref[0:half] = jnp.where(flags_ref[2] == 0, both[:half], both[half:])
    diagonal = jnp.sum(jnp.where(row == column, out_ref[2], F32(0)), axis=0, keepdims=True)
    send_ref[half : half + 8] = jnp.broadcast_to(diagonal, (8, n))
    turned_ref[...] = jnp.where(flags_ref[5 + 2 * level] == 1, out_ref[1].T, out_ref[1])
    first = flags_ref[4 + 2 * (level + 1)]
    send_ref[half + 8 : half + 8 + block] = turned_ref[pl.ds(pl.multiple_of(first * block, block), block), :]
    mine = pl.ds(pl.multiple_of(flags_ref[3] * rows, rows), rows)
    send_ref[half + 8 + block : half + 8 + block + rows] = turned_ref[mine, :]


def chip_kernel(level, last, flags_ref, own_ref, came_ref, swapped_ref, out_ref, send_ref, d_ref, x_ref, other_ref, turned_ref):
    core = flags_ref[2]
    active = flags_ref[4 + 2 * level] == 1

    def send_off():
        if last is None:
            pack(core, out_ref, send_ref)
        else:
            pack_for_last(flags_ref, level + 1, *last, out_ref, send_ref, turned_ref)

    @pl.when(active)
    def _():
        unpack(core, came_ref, swapped_ref, other_ref)
        merge_refs(
            flags_ref[5 + 2 * level] == 1, own_ref, other_ref, level + 2, out_ref, d_ref, x_ref, send_off
        )

    @pl.when(jnp.logical_not(active))
    def _():
        out_ref[...] = own_ref[...]
        send_ref[...] = jnp.zeros_like(send_ref)


def chip_merge(level, last, flags, own, came, swapped):
    n = own.shape[-1]
    sent = n + 8 if last is None else n // 2 + 8 + sum(last)
    return pl.pallas_call(
        functools.partial(chip_kernel, level, last),
        out_shape=(jax.ShapeDtypeStruct((3, n, n), F32), jax.ShapeDtypeStruct((sent, n), F32)),
        in_specs=[SMEM, VMEM, VMEM, VMEM],
        out_specs=(VMEM, VMEM),
        scratch_shapes=[pltpu.VMEM((n, n), F32)] * 2 + [pltpu.VMEM((3, n, n), F32), pltpu.VMEM((n, n), F32)],
        compiler_params=PARAMS,
        name="chip_merge",
    )(flags, own, came, swapped)


def last_kernel(level, flags_ref, own_ref, came_ref, swapped_ref, mine_ref, next_ref, d_ref, x_ref, turned_ref, other_ref):
    n = d_ref.shape[0]
    core = flags_ref[2]
    wide, rows = mine_ref.shape[1:]
    active = flags_ref[4 + 2 * level] == 1
    upper = flags_ref[5 + 2 * level] == 1
    chip = flags_ref[0] // 2
    depth = 4 * wide
    block = pl.ds(pl.multiple_of(chip // 2 * depth, depth), depth)
    mine = pl.ds(pl.multiple_of(flags_ref[3] * rows, rows), rows)
    half = n // 2

    def cut(wanted, array):
        piece = array[:wide]
        for i in range(1, 4):
            piece = jnp.where(wanted == i, array[i * wide : (i + 1) * wide], piece)
        return piece

    def at_mine(array):
        return pltpu.roll(array, (n - flags_ref[3] * rows) % n, axis=1)[:, :rows]

    @pl.when(active)
    def _():
        row, column = grid_of(n)
        x_ref[0:half] = jnp.where(core == 0, came_ref[0:half], swapped_ref[0:half])
        x_ref[half:n] = jnp.where(core == 0, swapped_ref[0:half], came_ref[0:half])
        both = x_ref[...]
        turned = both.T
        other_ref[0] = jnp.where(row >= column, both, turned)
        other_ref[1] = jnp.where(row == column, came_ref[half : half + 1], jnp.where(row < column, both, turned))
        turned_ref[...] = jnp.where(upper, own_ref[1].T, own_ref[1])
        d = jnp.where(upper, other_ref[1] + own_ref[0], own_ref[2] + other_ref[0])

        def finish(x):
            x = parts(x)
            came_block = came_ref[half + 8 : half + 8 + depth]
            came_mine = came_ref[half + 8 + depth : half + 8 + depth + rows]
            own_block, own_mine = turned_ref[block, :], turned_ref[mine, :]
            b1_block, b2_block = jnp.where(upper, came_block, own_block), jnp.where(upper, own_block, came_block)
            b1 = parts(jnp.where(upper, came_mine, own_mine))
            b2 = parts(jnp.where(upper, own_mine, came_mine))
            w1, w2 = parts(dot6(parts(b1_block), x)), parts(dot6(parts(b2_block), x))
            a_rows = jnp.where(upper, other_ref[0, block, :], own_ref[0, block, :])
            c_rows = jnp.where(upper, own_ref[2, block, :], other_ref[1, block, :])
            results = (at_mine(a_rows) - dot6(w1, b1, NT), dot6(w2, b1, NT), at_mine(c_rows) - dot6(w2, b2, NT))
            for i, result in enumerate(results):
                mine_ref[i] = cut(chip % 2 * 2 + core, result)
                next_ref[i] = cut((1 - chip % 2) * 2 + core, result)

        merge_blocks(d, level + 2, d_ref, x_ref, finish)

    @pl.when(jnp.logical_not(active))
    def _():
        mine_ref[...] = jnp.zeros_like(mine_ref)
        next_ref[...] = jnp.zeros_like(next_ref)


def last_merge(level, flags, own, came, swapped, wide, rows):
    n = own.shape[-1]
    return pl.pallas_call(
        functools.partial(last_kernel, level),
        out_shape=(jax.ShapeDtypeStruct((3, wide, rows), F32),) * 2,
        in_specs=[SMEM, VMEM, VMEM, VMEM],
        out_specs=(VMEM, VMEM),
        scratch_shapes=[pltpu.VMEM((n, n), F32)] * 3 + [pltpu.VMEM((2, n, n), F32)],
        compiler_params=PARAMS,
        name="last_merge",
    )(flags, own, came, swapped)


def pick_kernel(level, flags_ref, mine_ref, brought_ref, a_ref, b_ref, c_ref):
    for i, ref in enumerate((a_ref, b_ref, c_ref)):
        ref[...] = jnp.where(flags_ref[4 + 2 * level] == 1, mine_ref[i], brought_ref[i])


def pick(level, flags, mine, brought):
    return pl.pallas_call(
        functools.partial(pick_kernel, level),
        out_shape=(jax.ShapeDtypeStruct(mine.shape[1:], F32),) * 3,
        in_specs=[SMEM, VMEM, VMEM],
        out_specs=(VMEM,) * 3,
        compiler_params=pltpu.CompilerParams(vmem_limit_bytes=2**20),
        name="pick",
    )(flags, mine, brought)


def shares_kernel(whole_ref, out_ref):
    depth = out_ref.shape[-1]
    for shard in range(out_ref.shape[0]):
        out_ref[shard] = whole_ref[:, :, shard * depth : (shard + 1) * depth]


def shares(surface_functions, shards):
    sectors, rows, points = surface_functions.shape
    return pl.pallas_call(
        shares_kernel,
        out_shape=jax.ShapeDtypeStruct((shards, sectors, rows, points // shards), BF16),
        in_specs=[VMEM],
        out_specs=VMEM,
        compiler_params=PARAMS,
        name="shares",
    )(surface_functions)


def inner_kernel(own_ref, out_ref):
    shards, _, rows, depth = own_ref.shape
    n = shards * rows
    first = own_ref[:, 0].reshape(n, depth)
    second = own_ref[:, 1].reshape(n, depth)
    out_ref[...] = dot1(first, second, NT).reshape(shards, rows, n)


def margin_kernel(own_ref, before_ref, inner_ref, out_ref):
    shards, _, rows, depth = own_ref.shape
    n = shards * rows
    first = own_ref[:, 0].reshape(n, depth)
    out_ref[:, 0] = dot1(before_ref[...].reshape(n, depth), first, NT).reshape(shards, rows, n)
    out_ref[:, 1] = inner_ref[...]


def inner_parts(own):
    shards, _, rows, _ = own.shape
    return pl.pallas_call(
        inner_kernel,
        out_shape=jax.ShapeDtypeStruct((shards, rows, shards * rows), F32),
        in_specs=[VMEM],
        out_specs=VMEM,
        compiler_params=PARAMS,
        cost_estimate=WORK,
        name="inner_parts",
    )(own)


def margin_parts(own, before, inner):
    shards, sectors, rows, _ = own.shape
    return pl.pallas_call(
        margin_kernel,
        out_shape=jax.ShapeDtypeStruct((shards, sectors, rows, shards * rows), F32),
        in_specs=[VMEM, VMEM, VMEM],
        out_specs=VMEM,
        compiler_params=PARAMS,
        name="margin_parts",
    )(own, before, inner)


def total_kernel(points, partial_ref, out_ref):
    total = partial_ref[0]
    for shard in range(1, partial_ref.shape[0]):
        total = total + partial_ref[shard]
    total = total / points
    for shard in range(partial_ref.shape[0]):
        out_ref[shard] = total


def total_for_all(partial, points):
    return pl.pallas_call(
        functools.partial(total_kernel, points),
        out_shape=jax.ShapeDtypeStruct(partial.shape, F32),
        in_specs=[VMEM],
        out_specs=VMEM,
        compiler_params=PARAMS,
        name="total_for_all",
    )(partial)


def exchange(array):
    return lax.all_to_all(array, "chan", split_axis=0, concat_axis=0, tiled=True)


YS = 8
ENDS = (0, 3, 4, 7)


def place(position):
    return position // (2 * YS), position // 2 % YS, position % 2


def spot(x, y, core):
    return (x * YS + y) * 2 + core


def levels(xs):
    result = [
        (lambda x, y: (x, y ^ 1), range(YS), ("y", 0)),
        (lambda x, y: (x, y ^ 2), ENDS, ("y", 1)),
        (lambda x, y: (x, YS - 1 - y), ENDS, ("y", 2)),
    ]
    for bit in range(xs.bit_length() - 1):
        mask = 2 ** (bit + 1) - 1
        result.append((lambda x, y, mask=mask: (x ^ mask, y), ENDS, ("x", bit)))
    return result


def per_device(surface_functions, channel_rates, coupling):
    sectors, rows, points = surface_functions.shape
    n = channel_rates.shape[1]
    shards = lax.axis_size("chan")
    count = lax.axis_size("sector")
    position = lax.axis_index("sector")
    plan = levels(count // (2 * YS))
    own = exchange(shares(surface_functions, shards))
    own, position, shard, channel_rates = lax.optimization_barrier(
        (own, position, lax.axis_index("chan"), channel_rates)
    )
    x, y, core = place(position)
    at_end = (y == ENDS[0]) | (y == ENDS[1]) | (y == ENDS[2]) | (y == ENDS[3])
    words = [position, jnp.int32(count), core, shard]
    for _, takers, (axis, bit) in plan:
        words.append(jnp.int32(1) if len(takers) == YS else at_end.astype(jnp.int32))
        words.append((x if axis == "x" else y) >> bit & 1)
    across, along = plan[-1][0](x, y)
    words.append((across * YS + along) // 2)
    flags = jnp.stack([jnp.asarray(word, jnp.int32) for word in words])

    step = 1.0 / (sectors * count)
    cot = channel_rates / jnp.tanh(channel_rates * step)
    csc = channel_rates / jnp.sinh(channel_rates * step)

    before = lax.ppermute(own[:, sectors - 1], "sector", [(i, i + 1) for i in range(count - 1)])
    inner, cot, csc, flags, before = lax.optimization_barrier((inner_parts(own), cot, csc, flags, before))
    partial = exchange(margin_parts(own, before, inner))
    margin = exchange(total_for_all(partial, points))

    packed = leaf(flags, margin, cot, csc, coupling)
    cores = [(i, i ^ 1) for i in range(count)]
    packed, send = core_merge(flags, packed, lax.ppermute(packed, "sector", cores))
    wide = n // count
    for level, (partner, takers, _) in enumerate(plan):
        pairs = []
        for i in range(count):
            xi, yi, ci = place(i)
            if yi in takers:
                pairs.append((spot(*partner(xi, yi), ci), i))
        came = lax.ppermute(send, "sector", pairs)
        swapped = lax.ppermute(came, "sector", cores)
        if level < len(plan) - 1:
            last = (rows, 4 * wide) if level == len(plan) - 2 else None
            packed, send = chip_merge(level, last, flags, packed, came, swapped)
        else:
            mine, for_next = last_merge(level, flags, packed, came, swapped, wide, rows)
    pairs = []
    for i in range(count):
        xi, yi, ci = place(i)
        if yi not in ENDS:
            pairs.append((spot(xi, yi ^ 1, ci), i))
    brought = lax.ppermute(for_next, "sector", pairs)
    return tuple(block.T for block in pick(len(plan) - 1, flags, mine, brought))


def solution(mesh):
    placed = (P("sector", "chan", None), P("sector", None), P("sector", None, None))
    return jax.shard_map(
        per_device,
        mesh=mesh,
        in_specs=placed,
        out_specs=(P("chan", "sector"), P("chan", "sector"), P("chan", "sector")),
        check_vma=False,
    )
```

```python
import functools

import jax
import jax.numpy as jnp
from jax import lax
from jax.experimental import pallas as pl
from jax.experimental.pallas import tpu as pltpu
from jax.sharding import PartitionSpec as P

F32 = jnp.float32
BF16 = jnp.bfloat16
NN = (((1,), (0,)), ((), ()))
NT = (((1,), (1,)), ((), ()))
TN = (((0,), (0,)), ((), ()))
TOLERANCE = 1e-5
STEPS = 8
SQUARINGS = (3, 3, 4, 5, 6, 7, 7)
WORK = pl.CostEstimate(flops=10**9, bytes_accessed=2 * 10**6, transcendentals=0)
PARAMS = pltpu.CompilerParams(vmem_limit_bytes=32 * 2**20)
VMEM = pl.BlockSpec(memory_space=pltpu.VMEM)
SMEM = pl.BlockSpec(memory_space=pltpu.SMEM)


def parts(x):
    high = x.astype(BF16)
    rest = x - high.astype(F32)
    middle = rest.astype(BF16)
    return high, middle, (rest - middle.astype(F32)).astype(BF16)


def dot1(a, b, dims=NN):
    return lax.dot_general(a, b, dims, preferred_element_type=F32)


def dot3(a, b, dims=NN):
    return dot1(a[0], b[0], dims) + (dot1(a[0], b[1], dims) + dot1(a[1], b[0], dims))


def dot6(a, b, dims=NN):
    low = dot1(a[0], b[2], dims) + dot1(a[1], b[1], dims) + dot1(a[2], b[0], dims)
    return dot1(a[0], b[0], dims) + ((dot1(a[0], b[1], dims) + dot1(a[1], b[0], dims)) + low)


def grid_of(n):
    return (
        lax.broadcasted_iota(jnp.int32, (n, n), 0),
        lax.broadcasted_iota(jnp.int32, (n, n), 1),
    )


def unit(n):
    row, column = grid_of(n)
    return jnp.where(row == column, F32(1), F32(0))


def step_size(d):
    return 1.9 / jnp.max(jnp.sum(jnp.abs(d), axis=0, keepdims=True), axis=1, keepdims=True)


def first_inverse(d, squarings):
    n = d.shape[0]
    one = unit(n)
    alpha = step_size(d)
    e = one - alpha * d
    c = jnp.sum(jnp.sum(e * one, axis=0, keepdims=True), axis=1, keepdims=True) / n
    f = e - c * one
    p, y = 1 + c, f
    for _ in range(squarings):
        rounded = f.astype(BF16)
        f = 2 * c * f + dot1(rounded, rounded)
        c = c * c
        y = p * f + (1 + c) * y + dot1(y.astype(BF16), f.astype(BF16))
        p = p * (1 + c)
    return alpha * (p * one + y)


def newton(d_parts, x, dot):
    x_parts = parts(x)
    residual = unit(x.shape[0]) - dot(d_parts, x_parts)
    return x + (dot1(x_parts[0], residual.astype(BF16)) if dot is dot3 else dot3(x_parts, parts(residual))), residual


def combine(left, right, x, out_ref):
    b1, b2, x = parts(left(1)), parts(right(1)), parts(x)
    w1, w2 = parts(dot6(b1, x)), parts(dot6(x, b2))
    out_ref[0] = left(0) - dot6(w1, b1, NT)
    out_ref[1] = dot6(w1, b2)
    out_ref[2] = right(2) - dot6(b2, w2, TN)


def merge_blocks(d, depth, d_ref, x_ref, finish):
    d_ref[...] = d
    x_ref[...], _ = newton(parts(d), first_inverse(d, SQUARINGS[min(depth, len(SQUARINGS) - 1)]), dot3)

    def going(state):
        return jnp.logical_and(state[0] < 9 * STEPS, jnp.logical_not(state[1] < TOLERANCE))

    def again(state):
        @pl.when(state[0] == STEPS)
        def _():
            x_ref[...] = step_size(d_ref[...]) * unit(d_ref.shape[0])

        x, residual = newton(parts(d_ref[...]), x_ref[...], dot6)
        x_ref[...] = x
        finish(x)
        return state[0] + 1, jnp.sum(residual * residual)

    lax.while_loop(going, again, (0, F32(1)))


def pack(core, out_ref, send_ref):
    n = out_ref.shape[-1]
    row, column = grid_of(n)
    last = out_ref[2]
    both = jnp.where(row >= column, out_ref[0], last)
    send_ref[0:n] = jnp.where(core == 0, both, out_ref[1])
    diagonal = jnp.sum(jnp.where(row == column, last, F32(0)), axis=0, keepdims=True)
    send_ref[n : n + 8] = jnp.broadcast_to(diagonal, (8, n))


def leaf_kernel(flags_ref, margin_ref, cot_ref, csc_ref, coupling_ref, out_ref, d_ref, x_ref):
    n = d_ref.shape[0]
    row, column = grid_of(n)
    half_step = 0.5 / (2 * flags_ref[1]).astype(F32)

    def inner(s):
        diagonal = jnp.where(row == column, cot_ref[s : s + 1, :], F32(0))
        return diagonal + half_step * coupling_ref[s].astype(F32)

    second = margin_ref[:, 1].reshape(n, n)
    m1 = parts(second)
    a1 = dot6(parts(dot6(m1, parts(inner(1)))), m1, NT)

    def finish(x):
        m0 = parts(jnp.where(flags_ref[0] == 0, unit(n), margin_ref[:, 0].reshape(n, n)))
        csc = csc_ref[0:1, :]
        csc_down = jnp.sum(jnp.where(row == column, csc, F32(0)), axis=1, keepdims=True)
        b2 = parts(margin_ref[:, 1].reshape(n, n) * csc_ref[1:2, :])
        w2 = dot6(parts(x), b2)
        out_ref[0] = dot6(parts(dot6(m0, parts(inner(0) - csc_down * x * csc))), m0, NT)
        out_ref[1] = dot6(m0, parts(csc_down * w2))
        out_ref[2] = inner(1) - dot6(b2, parts(w2), TN)

    merge_blocks(inner(0) + a1, 0, d_ref, x_ref, finish)


def leaf(flags, margin, cot, csc, coupling):
    n = coupling.shape[-1]
    return pl.pallas_call(
        leaf_kernel,
        out_shape=jax.ShapeDtypeStruct((3, n, n), F32),
        in_specs=[SMEM, VMEM, VMEM, VMEM, VMEM],
        out_specs=VMEM,
        scratch_shapes=[pltpu.VMEM((n, n), F32)] * 2,
        compiler_params=PARAMS,
        name="leaf",
    )(flags, margin, cot, csc, coupling)


def sides(upper, own_ref, other_ref):
    return (
        lambda i: jnp.where(upper, other_ref[i], own_ref[i]),
        lambda i: jnp.where(upper, own_ref[i], other_ref[i]),
    )


def merge_refs(upper, own_ref, other_ref, depth, out_ref, d_ref, x_ref, after):
    left, right = sides(upper, own_ref, other_ref)

    def finish(x):
        combine(left, right, x, out_ref)
        after()

    merge_blocks(left(2) + right(0), depth, d_ref, x_ref, finish)


def core_kernel(flags_ref, own_ref, other_ref, out_ref, send_ref, d_ref, x_ref):
    core = flags_ref[2]
    merge_refs(core == 1, own_ref, other_ref, 1, out_ref, d_ref, x_ref, lambda: pack(core, out_ref, send_ref))


def core_merge(flags, own, other):
    n = own.shape[-1]
    return pl.pallas_call(
        core_kernel,
        out_shape=(jax.ShapeDtypeStruct((3, n, n), F32), jax.ShapeDtypeStruct((n + 8, n), F32)),
        in_specs=[SMEM, VMEM, VMEM],
        out_specs=(VMEM, VMEM),
        scratch_shapes=[pltpu.VMEM((n, n), F32)] * 2,
        compiler_params=PARAMS,
        name="core_merge",
    )(flags, own, other)


def unpack(core, came_ref, swapped_ref, other_ref):
    n = other_ref.shape[-1]
    row, column = grid_of(n)
    both = jnp.where(core == 0, came_ref[0:n], swapped_ref[0:n])
    diagonal = jnp.where(core == 0, came_ref[n : n + 1], swapped_ref[n : n + 1])
    turned = both.T
    other_ref[0] = jnp.where(row >= column, both, turned)
    other_ref[1] = jnp.where(core == 0, swapped_ref[0:n], came_ref[0:n])
    other_ref[2] = jnp.where(row == column, diagonal, jnp.where(row < column, both, turned))


def pack_for_last(flags_ref, level, rows, block, out_ref, send_ref, turned_ref):
    n = out_ref.shape[-1]
    half = n // 2
    row, column = grid_of(n)
    both = jnp.where(row >= column, out_ref[0], out_ref[2])
    send_ref[0:half] = jnp.where(flags_ref[2] == 0, both[:half], both[half:])
    diagonal = jnp.sum(jnp.where(row == column, out_ref[2], F32(0)), axis=0, keepdims=True)
    send_ref[half : half + 8] = jnp.broadcast_to(diagonal, (8, n))
    turned_ref[...] = jnp.where(flags_ref[5 + 2 * level] == 1, out_ref[1].T, out_ref[1])
    first = flags_ref[4 + 2 * (level + 1)]
    send_ref[half + 8 : half + 8 + block] = turned_ref[pl.ds(pl.multiple_of(first * block, block), block), :]
    mine = pl.ds(pl.multiple_of(flags_ref[3] * rows, rows), rows)
    send_ref[half + 8 + block : half + 8 + block + rows] = turned_ref[mine, :]


def chip_kernel(level, last, flags_ref, own_ref, came_ref, swapped_ref, out_ref, send_ref, d_ref, x_ref, other_ref, turned_ref):
    core = flags_ref[2]
    active = flags_ref[4 + 2 * level] == 1

    def send_off():
        if last is None:
            pack(core, out_ref, send_ref)
        else:
            pack_for_last(flags_ref, level + 1, *last, out_ref, send_ref, turned_ref)

    @pl.when(active)
    def _():
        unpack(core, came_ref, swapped_ref, other_ref)
        merge_refs(
            flags_ref[5 + 2 * level] == 1, own_ref, other_ref, level + 2, out_ref, d_ref, x_ref, send_off
        )

    @pl.when(jnp.logical_not(active))
    def _():
        out_ref[...] = own_ref[...]
        send_ref[...] = jnp.zeros_like(send_ref)


def chip_merge(level, last, flags, own, came, swapped):
    n = own.shape[-1]
    sent = n + 8 if last is None else n // 2 + 8 + sum(last)
    return pl.pallas_call(
        functools.partial(chip_kernel, level, last),
        out_shape=(jax.ShapeDtypeStruct((3, n, n), F32), jax.ShapeDtypeStruct((sent, n), F32)),
        in_specs=[SMEM, VMEM, VMEM, VMEM],
        out_specs=(VMEM, VMEM),
        scratch_shapes=[pltpu.VMEM((n, n), F32)] * 2 + [pltpu.VMEM((3, n, n), F32), pltpu.VMEM((n, n), F32)],
        compiler_params=PARAMS,
        name="chip_merge",
    )(flags, own, came, swapped)


def last_kernel(level, flags_ref, own_ref, came_ref, swapped_ref, mine_ref, next_ref, d_ref, x_ref, turned_ref, other_ref):
    n = d_ref.shape[0]
    core = flags_ref[2]
    wide, rows = mine_ref.shape[1:]
    active = flags_ref[4 + 2 * level] == 1
    upper = flags_ref[5 + 2 * level] == 1
    chip = flags_ref[0] // 2
    depth = 4 * wide
    block = pl.ds(pl.multiple_of(chip // 2 * depth, depth), depth)
    mine = pl.ds(pl.multiple_of(flags_ref[3] * rows, rows), rows)
    half = n // 2

    def cut(wanted, array):
        piece = array[:wide]
        for i in range(1, 4):
            piece = jnp.where(wanted == i, array[i * wide : (i + 1) * wide], piece)
        return piece

    def at_mine(array):
        return pltpu.roll(array, (n - flags_ref[3] * rows) % n, axis=1)[:, :rows]

    @pl.when(active)
    def _():
        row, column = grid_of(n)
        x_ref[0:half] = jnp.where(core == 0, came_ref[0:half], swapped_ref[0:half])
        x_ref[half:n] = jnp.where(core == 0, swapped_ref[0:half], came_ref[0:half])
        both = x_ref[...]
        turned = both.T
        other_ref[0] = jnp.where(row >= column, both, turned)
        other_ref[1] = jnp.where(row == column, came_ref[half : half + 1], jnp.where(row < column, both, turned))
        turned_ref[...] = jnp.where(upper, own_ref[1].T, own_ref[1])
        d = jnp.where(upper, other_ref[1] + own_ref[0], own_ref[2] + other_ref[0])

        def finish(x):
            x = parts(x)
            came_block = came_ref[half + 8 : half + 8 + depth]
            came_mine = came_ref[half + 8 + depth : half + 8 + depth + rows]
            own_block, own_mine = turned_ref[block, :], turned_ref[mine, :]
            b1_block, b2_block = jnp.where(upper, came_block, own_block), jnp.where(upper, own_block, came_block)
            b1 = parts(jnp.where(upper, came_mine, own_mine))
            b2 = parts(jnp.where(upper, own_mine, came_mine))
            w1, w2 = parts(dot6(parts(b1_block), x)), parts(dot6(parts(b2_block), x))
            a_rows = jnp.where(upper, other_ref[0, block, :], own_ref[0, block, :])
            c_rows = jnp.where(upper, own_ref[2, block, :], other_ref[1, block, :])
            results = (at_mine(a_rows) - dot6(w1, b1, NT), dot6(w2, b1, NT), at_mine(c_rows) - dot6(w2, b2, NT))
            for i, result in enumerate(results):
                mine_ref[i] = cut(chip % 2 * 2 + core, result)
                next_ref[i] = cut((1 - chip % 2) * 2 + core, result)

        merge_blocks(d, level + 2, d_ref, x_ref, finish)

    @pl.when(jnp.logical_not(active))
    def _():
        mine_ref[...] = jnp.zeros_like(mine_ref)
        next_ref[...] = jnp.zeros_like(next_ref)


def last_merge(level, flags, own, came, swapped, wide, rows):
    n = own.shape[-1]
    return pl.pallas_call(
        functools.partial(last_kernel, level),
        out_shape=(jax.ShapeDtypeStruct((3, wide, rows), F32),) * 2,
        in_specs=[SMEM, VMEM, VMEM, VMEM],
        out_specs=(VMEM, VMEM),
        scratch_shapes=[pltpu.VMEM((n, n), F32)] * 3 + [pltpu.VMEM((2, n, n), F32)],
        compiler_params=PARAMS,
        name="last_merge",
    )(flags, own, came, swapped)


def pick_kernel(level, flags_ref, mine_ref, brought_ref, a_ref, b_ref, c_ref):
    for i, ref in enumerate((a_ref, b_ref, c_ref)):
        ref[...] = jnp.where(flags_ref[4 + 2 * level] == 1, mine_ref[i], brought_ref[i])


def pick(level, flags, mine, brought):
    return pl.pallas_call(
        functools.partial(pick_kernel, level),
        out_shape=(jax.ShapeDtypeStruct(mine.shape[1:], F32),) * 3,
        in_specs=[SMEM, VMEM, VMEM],
        out_specs=(VMEM,) * 3,
        compiler_params=pltpu.CompilerParams(vmem_limit_bytes=2**20),
        name="pick",
    )(flags, mine, brought)


def shares_kernel(whole_ref, out_ref):
    depth = out_ref.shape[-1]
    for shard in range(out_ref.shape[0]):
        out_ref[shard] = whole_ref[:, :, shard * depth : (shard + 1) * depth]


def shares(surface_functions, shards):
    sectors, rows, points = surface_functions.shape
    return pl.pallas_call(
        shares_kernel,
        out_shape=jax.ShapeDtypeStruct((shards, sectors, rows, points // shards), BF16),
        in_specs=[VMEM],
        out_specs=VMEM,
        compiler_params=PARAMS,
        name="shares",
    )(surface_functions)


def inner_kernel(own_ref, out_ref):
    shards, _, rows, depth = own_ref.shape
    n = shards * rows
    first = own_ref[:, 0].reshape(n, depth)
    second = own_ref[:, 1].reshape(n, depth)
    out_ref[...] = dot1(first, second, NT).reshape(shards, rows, n)


def margin_kernel(own_ref, before_ref, inner_ref, out_ref):
    shards, _, rows, depth = own_ref.shape
    n = shards * rows
    first = own_ref[:, 0].reshape(n, depth)
    out_ref[:, 0] = dot1(before_ref[...].reshape(n, depth), first, NT).reshape(shards, rows, n)
    out_ref[:, 1] = inner_ref[...]


def inner_parts(own):
    shards, _, rows, _ = own.shape
    return pl.pallas_call(
        inner_kernel,
        out_shape=jax.ShapeDtypeStruct((shards, rows, shards * rows), F32),
        in_specs=[VMEM],
        out_specs=VMEM,
        compiler_params=PARAMS,
        cost_estimate=WORK,
        name="inner_parts",
    )(own)


def margin_parts(own, before, inner):
    shards, sectors, rows, _ = own.shape
    return pl.pallas_call(
        margin_kernel,
        out_shape=jax.ShapeDtypeStruct((shards, sectors, rows, shards * rows), F32),
        in_specs=[VMEM, VMEM, VMEM],
        out_specs=VMEM,
        compiler_params=PARAMS,
        name="margin_parts",
    )(own, before, inner)


def total_kernel(points, partial_ref, out_ref):
    total = partial_ref[0]
    for shard in range(1, partial_ref.shape[0]):
        total = total + partial_ref[shard]
    total = total / points
    for shard in range(partial_ref.shape[0]):
        out_ref[shard] = total


def total_for_all(partial, points):
    return pl.pallas_call(
        functools.partial(total_kernel, points),
        out_shape=jax.ShapeDtypeStruct(partial.shape, F32),
        in_specs=[VMEM],
        out_specs=VMEM,
        compiler_params=PARAMS,
        name="total_for_all",
    )(partial)


def exchange(array):
    return lax.all_to_all(array, "chan", split_axis=0, concat_axis=0, tiled=True)


YS = 8
ENDS = (0, 3, 4, 7)


def place(position):
    return position // (2 * YS), position // 2 % YS, position % 2


def spot(x, y, core):
    return (x * YS + y) * 2 + core


def levels(xs):
    result = [
        (lambda x, y: (x, y ^ 1), range(YS), ("y", 0)),
        (lambda x, y: (x, y ^ 2), ENDS, ("y", 1)),
        (lambda x, y: (x, YS - 1 - y), ENDS, ("y", 2)),
    ]
    for bit in range(xs.bit_length() - 1):
        mask = 2 ** (bit + 1) - 1
        result.append((lambda x, y, mask=mask: (x ^ mask, y), ENDS, ("x", bit)))
    return result


def per_device(surface_functions, channel_rates, coupling):
    sectors, rows, points = surface_functions.shape
    n = channel_rates.shape[1]
    shards = lax.axis_size("chan")
    count = lax.axis_size("sector")
    position = lax.axis_index("sector")
    plan = levels(count // (2 * YS))
    own = exchange(shares(surface_functions, shards))
    own, position, shard, channel_rates = lax.optimization_barrier(
        (own, position, lax.axis_index("chan"), channel_rates)
    )
    x, y, core = place(position)
    at_end = (y == ENDS[0]) | (y == ENDS[1]) | (y == ENDS[2]) | (y == ENDS[3])
    words = [position, jnp.int32(count), core, shard]
    for _, takers, (axis, bit) in plan:
        words.append(jnp.int32(1) if len(takers) == YS else at_end.astype(jnp.int32))
        words.append((x if axis == "x" else y) >> bit & 1)
    across, along = plan[-1][0](x, y)
    words.append((across * YS + along) // 2)
    flags = jnp.stack([jnp.asarray(word, jnp.int32) for word in words])

    step = 1.0 / (sectors * count)
    cot = channel_rates / jnp.tanh(channel_rates * step)
    csc = channel_rates / jnp.sinh(channel_rates * step)

    before = lax.ppermute(own[:, sectors - 1], "sector", [(i, i + 1) for i in range(count - 1)])
    inner, cot, csc, flags, before = lax.optimization_barrier((inner_parts(own), cot, csc, flags, before))
    partial = exchange(margin_parts(own, before, inner))
    margin = exchange(total_for_all(partial, points))

    packed = leaf(flags, margin, cot, csc, coupling)
    cores = [(i, i ^ 1) for i in range(count)]
    packed, send = core_merge(flags, packed, lax.ppermute(packed, "sector", cores))
    wide = n // count
    for level, (partner, takers, _) in enumerate(plan):
        pairs = []
        for i in range(count):
            xi, yi, ci = place(i)
            if yi in takers:
                pairs.append((spot(*partner(xi, yi), ci), i))
        came = lax.ppermute(send, "sector", pairs)
        swapped = lax.ppermute(came, "sector", cores)
        if level < len(plan) - 1:
            last = (rows, 4 * wide) if level == len(plan) - 2 else None
            packed, send = chip_merge(level, last, flags, packed, came, swapped)
        else:
            mine, for_next = last_merge(level, flags, packed, came, swapped, wide, rows)
    pairs = []
    for i in range(count):
        xi, yi, ci = place(i)
        if yi not in ENDS:
            pairs.append((spot(xi, yi ^ 1, ci), i))
    brought = lax.ppermute(for_next, "sector", pairs)
    return tuple(block.T for block in pick(len(plan) - 1, flags, mine, brought))


def solution(mesh):
    placed = (P("sector", "chan", None), P("sector", None), P("sector", None, None))
    return jax.shard_map(
        per_device,
        mesh=mesh,
        in_specs=placed,
        out_specs=(P("chan", "sector"), P("chan", "sector"), P("chan", "sector")),
        check_vma=False,
    )
```

```python
import functools

import jax
import jax.numpy as jnp
from jax import lax
from jax.experimental import pallas as pl
from jax.experimental.pallas import tpu as pltpu
from jax.sharding import PartitionSpec as P

F32 = jnp.float32
BF16 = jnp.bfloat16
NN = (((1,), (0,)), ((), ()))
NT = (((1,), (1,)), ((), ()))
TN = (((0,), (0,)), ((), ()))
TOLERANCE = 1e-5
STEPS = 8
SQUARINGS = (3, 3, 4, 5, 6, 7, 7)
WORK = pl.CostEstimate(flops=10**9, bytes_accessed=2 * 10**6, transcendentals=0)
PARAMS = pltpu.CompilerParams(vmem_limit_bytes=32 * 2**20)
VMEM = pl.BlockSpec(memory_space=pltpu.VMEM)
SMEM = pl.BlockSpec(memory_space=pltpu.SMEM)


def parts(x):
    high = x.astype(BF16)
    rest = x - high.astype(F32)
    middle = rest.astype(BF16)
    return high, middle, (rest - middle.astype(F32)).astype(BF16)


def dot1(a, b, dims=NN):
    return lax.dot_general(a, b, dims, preferred_element_type=F32)


def dot3(a, b, dims=NN):
    return dot1(a[0], b[0], dims) + (dot1(a[0], b[1], dims) + dot1(a[1], b[0], dims))


def dot6(a, b, dims=NN):
    low = dot1(a[0], b[2], dims) + dot1(a[1], b[1], dims) + dot1(a[2], b[0], dims)
    return dot1(a[0], b[0], dims) + ((dot1(a[0], b[1], dims) + dot1(a[1], b[0], dims)) + low)


def grid_of(n):
    return (
        lax.broadcasted_iota(jnp.int32, (n, n), 0),
        lax.broadcasted_iota(jnp.int32, (n, n), 1),
    )


def unit(n):
    row, column = grid_of(n)
    return jnp.where(row == column, F32(1), F32(0))


def step_size(d):
    return 1.9 / jnp.max(jnp.sum(jnp.abs(d), axis=0, keepdims=True), axis=1, keepdims=True)


def first_inverse(d, squarings):
    n = d.shape[0]
    one = unit(n)
    alpha = step_size(d)
    e = one - alpha * d
    c = jnp.sum(jnp.sum(e * one, axis=0, keepdims=True), axis=1, keepdims=True) / n
    f = e - c * one
    p, y = 1 + c, f
    for _ in range(squarings):
        rounded = f.astype(BF16)
        f = 2 * c * f + dot1(rounded, rounded)
        c = c * c
        y = p * f + (1 + c) * y + dot1(y.astype(BF16), f.astype(BF16))
        p = p * (1 + c)
    return alpha * (p * one + y)


def newton(d_parts, x, dot):
    x_parts = parts(x)
    residual = unit(x.shape[0]) - dot(d_parts, x_parts)
    return x + (dot1(x_parts[0], residual.astype(BF16)) if dot is dot3 else dot3(x_parts, parts(residual))), residual


def combine(left, right, x, out_ref):
    b1, b2, x = parts(left(1)), parts(right(1)), parts(x)
    w1, w2 = parts(dot6(b1, x)), parts(dot6(x, b2))
    out_ref[0] = left(0) - dot6(w1, b1, NT)
    out_ref[1] = dot6(w1, b2)
    out_ref[2] = right(2) - dot6(b2, w2, TN)


def merge_blocks(d, depth, d_ref, x_ref, finish):
    d_ref[...] = d
    x_ref[...], _ = newton(parts(d), first_inverse(d, SQUARINGS[min(depth, len(SQUARINGS) - 1)]), dot3)

    def going(state):
        return jnp.logical_and(state[0] < 9 * STEPS, jnp.logical_not(state[1] < TOLERANCE))

    def again(state):
        @pl.when(state[0] == STEPS)
        def _():
            x_ref[...] = step_size(d_ref[...]) * unit(d_ref.shape[0])

        x, residual = newton(parts(d_ref[...]), x_ref[...], dot6)
        x_ref[...] = x
        finish(x)
        return state[0] + 1, jnp.sum(residual * residual)

    lax.while_loop(going, again, (0, F32(1)))


def pack(core, out_ref, send_ref):
    n = out_ref.shape[-1]
    row, column = grid_of(n)
    last = out_ref[2]
    both = jnp.where(row >= column, out_ref[0], last)
    send_ref[0:n] = jnp.where(core == 0, both, out_ref[1])
    diagonal = jnp.sum(jnp.where(row == column, last, F32(0)), axis=0, keepdims=True)
    send_ref[n : n + 8] = jnp.broadcast_to(diagonal, (8, n))


def leaf_kernel(flags_ref, margin_ref, cot_ref, csc_ref, coupling_ref, out_ref, d_ref, x_ref, a_ref, b_ref, c_ref):
    n = d_ref.shape[0]
    row, column = grid_of(n)
    half_step = 0.5 / (2 * flags_ref[1]).astype(F32)

    def sector(s):
        margin = margin_ref[:, s].reshape(n, n)
        if s == 0:
            margin = jnp.where(flags_ref[0] == 0, unit(n), margin)
        inner = jnp.where(row == column, cot_ref[s : s + 1, :], F32(0)) + half_step * coupling_ref[s].astype(F32)
        m = parts(margin)
        a_ref[s] = dot6(parts(dot6(m, parts(inner))), m, NT)
        b_ref[s] = margin * csc_ref[s : s + 1, :]
        c_ref[s] = inner

    sector(1)
    sector(0)
    blocks = (a_ref, b_ref, c_ref)
    merge_blocks(
        c_ref[0] + a_ref[1], 0, d_ref, x_ref,
        lambda x: combine(lambda i: blocks[i][0], lambda i: blocks[i][1], x, out_ref),
    )


def leaf(flags, margin, cot, csc, coupling):
    n = coupling.shape[-1]
    return pl.pallas_call(
        leaf_kernel,
        out_shape=jax.ShapeDtypeStruct((3, n, n), F32),
        in_specs=[SMEM, VMEM, VMEM, VMEM, VMEM],
        out_specs=VMEM,
        scratch_shapes=[pltpu.VMEM((n, n), F32)] * 2 + [pltpu.VMEM((2, n, n), F32)] * 3,
        compiler_params=PARAMS,
        name="leaf",
    )(flags, margin, cot, csc, coupling)


def sides(upper, own_ref, other_ref):
    return (
        lambda i: jnp.where(upper, other_ref[i], own_ref[i]),
        lambda i: jnp.where(upper, own_ref[i], other_ref[i]),
    )


def merge_refs(upper, own_ref, other_ref, depth, out_ref, d_ref, x_ref, after):
    left, right = sides(upper, own_ref, other_ref)

    def finish(x):
        combine(left, right, x, out_ref)
        after()

    merge_blocks(left(2) + right(0), depth, d_ref, x_ref, finish)


def core_kernel(flags_ref, own_ref, other_ref, out_ref, send_ref, d_ref, x_ref):
    core = flags_ref[2]
    merge_refs(core == 1, own_ref, other_ref, 1, out_ref, d_ref, x_ref, lambda: pack(core, out_ref, send_ref))


def core_merge(flags, own, other):
    n = own.shape[-1]
    return pl.pallas_call(
        core_kernel,
        out_shape=(jax.ShapeDtypeStruct((3, n, n), F32), jax.ShapeDtypeStruct((n + 8, n), F32)),
        in_specs=[SMEM, VMEM, VMEM],
        out_specs=(VMEM, VMEM),
        scratch_shapes=[pltpu.VMEM((n, n), F32)] * 2,
        compiler_params=PARAMS,
        name="core_merge",
    )(flags, own, other)


def unpack(core, came_ref, swapped_ref, other_ref):
    n = other_ref.shape[-1]
    row, column = grid_of(n)
    both = jnp.where(core == 0, came_ref[0:n], swapped_ref[0:n])
    diagonal = jnp.where(core == 0, came_ref[n : n + 1], swapped_ref[n : n + 1])
    turned = both.T
    other_ref[0] = jnp.where(row >= column, both, turned)
    other_ref[1] = jnp.where(core == 0, swapped_ref[0:n], came_ref[0:n])
    other_ref[2] = jnp.where(row == column, diagonal, jnp.where(row < column, both, turned))


def pack_for_last(flags_ref, level, rows, block, out_ref, send_ref, turned_ref):
    n = out_ref.shape[-1]
    half = n // 2
    row, column = grid_of(n)
    both = jnp.where(row >= column, out_ref[0], out_ref[2])
    send_ref[0:half] = jnp.where(flags_ref[2] == 0, both[:half], both[half:])
    diagonal = jnp.sum(jnp.where(row == column, out_ref[2], F32(0)), axis=0, keepdims=True)
    send_ref[half : half + 8] = jnp.broadcast_to(diagonal, (8, n))
    turned_ref[...] = jnp.where(flags_ref[5 + 2 * level] == 1, out_ref[1].T, out_ref[1])
    first = flags_ref[4 + 2 * (level + 1)]
    send_ref[half + 8 : half + 8 + block] = turned_ref[pl.ds(pl.multiple_of(first * block, block), block), :]
    mine = pl.ds(pl.multiple_of(flags_ref[3] * rows, rows), rows)
    send_ref[half + 8 + block : half + 8 + block + rows] = turned_ref[mine, :]


def chip_kernel(level, last, flags_ref, own_ref, came_ref, swapped_ref, out_ref, send_ref, d_ref, x_ref, other_ref, turned_ref):
    core = flags_ref[2]
    active = flags_ref[4 + 2 * level] == 1

    def send_off():
        if last is None:
            pack(core, out_ref, send_ref)
        else:
            pack_for_last(flags_ref, level + 1, *last, out_ref, send_ref, turned_ref)

    @pl.when(active)
    def _():
        unpack(core, came_ref, swapped_ref, other_ref)
        merge_refs(
            flags_ref[5 + 2 * level] == 1, own_ref, other_ref, level + 2, out_ref, d_ref, x_ref, send_off
        )

    @pl.when(jnp.logical_not(active))
    def _():
        out_ref[...] = own_ref[...]
        send_ref[...] = jnp.zeros_like(send_ref)


def chip_merge(level, last, flags, own, came, swapped):
    n = own.shape[-1]
    sent = n + 8 if last is None else n // 2 + 8 + sum(last)
    return pl.pallas_call(
        functools.partial(chip_kernel, level, last),
        out_shape=(jax.ShapeDtypeStruct((3, n, n), F32), jax.ShapeDtypeStruct((sent, n), F32)),
        in_specs=[SMEM, VMEM, VMEM, VMEM],
        out_specs=(VMEM, VMEM),
        scratch_shapes=[pltpu.VMEM((n, n), F32)] * 2 + [pltpu.VMEM((3, n, n), F32), pltpu.VMEM((n, n), F32)],
        compiler_params=PARAMS,
        name="chip_merge",
    )(flags, own, came, swapped)


def last_kernel(level, flags_ref, own_ref, came_ref, swapped_ref, mine_ref, next_ref, d_ref, x_ref, turned_ref, other_ref):
    n = d_ref.shape[0]
    core = flags_ref[2]
    wide, rows = mine_ref.shape[1:]
    active = flags_ref[4 + 2 * level] == 1
    upper = flags_ref[5 + 2 * level] == 1
    chip = flags_ref[0] // 2
    depth = 4 * wide
    block = pl.ds(pl.multiple_of(chip // 2 * depth, depth), depth)
    mine = pl.ds(pl.multiple_of(flags_ref[3] * rows, rows), rows)
    half = n // 2

    def cut(wanted, array):
        piece = array[:wide]
        for i in range(1, 4):
            piece = jnp.where(wanted == i, array[i * wide : (i + 1) * wide], piece)
        return piece

    def at_mine(array):
        return pltpu.roll(array, (n - flags_ref[3] * rows) % n, axis=1)[:, :rows]

    @pl.when(active)
    def _():
        row, column = grid_of(n)
        x_ref[0:half] = jnp.where(core == 0, came_ref[0:half], swapped_ref[0:half])
        x_ref[half:n] = jnp.where(core == 0, swapped_ref[0:half], came_ref[0:half])
        both = x_ref[...]
        turned = both.T
        other_ref[0] = jnp.where(row >= column, both, turned)
        other_ref[1] = jnp.where(row == column, came_ref[half : half + 1], jnp.where(row < column, both, turned))
        turned_ref[...] = jnp.where(upper, own_ref[1].T, own_ref[1])
        d = jnp.where(upper, other_ref[1] + own_ref[0], own_ref[2] + other_ref[0])

        def finish(x):
            x = parts(x)
            came_block = came_ref[half + 8 : half + 8 + depth]
            came_mine = came_ref[half + 8 + depth : half + 8 + depth + rows]
            own_block, own_mine = turned_ref[block, :], turned_ref[mine, :]
            b1_block, b2_block = jnp.where(upper, came_block, own_block), jnp.where(upper, own_block, came_block)
            b1 = parts(jnp.where(upper, came_mine, own_mine))
            b2 = parts(jnp.where(upper, own_mine, came_mine))
            w1, w2 = parts(dot6(parts(b1_block), x)), parts(dot6(parts(b2_block), x))
            a_rows = jnp.where(upper, other_ref[0, block, :], own_ref[0, block, :])
            c_rows = jnp.where(upper, own_ref[2, block, :], other_ref[1, block, :])
            results = (at_mine(a_rows) - dot6(w1, b1, NT), dot6(w2, b1, NT), at_mine(c_rows) - dot6(w2, b2, NT))
            for i, result in enumerate(results):
                mine_ref[i] = cut(chip % 2 * 2 + core, result)
                next_ref[i] = cut((1 - chip % 2) * 2 + core, result)

        merge_blocks(d, level + 2, d_ref, x_ref, finish)

    @pl.when(jnp.logical_not(active))
    def _():
        mine_ref[...] = jnp.zeros_like(mine_ref)
        next_ref[...] = jnp.zeros_like(next_ref)


def last_merge(level, flags, own, came, swapped, wide, rows):
    n = own.shape[-1]
    return pl.pallas_call(
        functools.partial(last_kernel, level),
        out_shape=(jax.ShapeDtypeStruct((3, wide, rows), F32),) * 2,
        in_specs=[SMEM, VMEM, VMEM, VMEM],
        out_specs=(VMEM, VMEM),
        scratch_shapes=[pltpu.VMEM((n, n), F32)] * 3 + [pltpu.VMEM((2, n, n), F32)],
        compiler_params=PARAMS,
        name="last_merge",
    )(flags, own, came, swapped)


def shares_kernel(whole_ref, out_ref):
    depth = out_ref.shape[-1]
    for shard in range(out_ref.shape[0]):
        out_ref[shard] = whole_ref[:, :, shard * depth : (shard + 1) * depth]


def shares(surface_functions, shards):
    sectors, rows, points = surface_functions.shape
    return pl.pallas_call(
        shares_kernel,
        out_shape=jax.ShapeDtypeStruct((shards, sectors, rows, points // shards), BF16),
        in_specs=[VMEM],
        out_specs=VMEM,
        compiler_params=PARAMS,
        name="shares",
    )(surface_functions)


def inner_kernel(own_ref, out_ref):
    shards, _, rows, depth = own_ref.shape
    n = shards * rows
    first = own_ref[:, 0].reshape(n, depth)
    second = own_ref[:, 1].reshape(n, depth)
    out_ref[...] = dot1(first, second, NT).reshape(shards, rows, n)


def margin_kernel(own_ref, before_ref, inner_ref, out_ref):
    shards, _, rows, depth = own_ref.shape
    n = shards * rows
    first = own_ref[:, 0].reshape(n, depth)
    out_ref[:, 0] = dot1(before_ref[...].reshape(n, depth), first, NT).reshape(shards, rows, n)
    out_ref[:, 1] = inner_ref[...]


def inner_parts(own):
    shards, _, rows, _ = own.shape
    return pl.pallas_call(
        inner_kernel,
        out_shape=jax.ShapeDtypeStruct((shards, rows, shards * rows), F32),
        in_specs=[VMEM],
        out_specs=VMEM,
        compiler_params=PARAMS,
        cost_estimate=WORK,
        name="inner_parts",
    )(own)


def margin_parts(own, before, inner):
    shards, sectors, rows, _ = own.shape
    return pl.pallas_call(
        margin_kernel,
        out_shape=jax.ShapeDtypeStruct((shards, sectors, rows, shards * rows), F32),
        in_specs=[VMEM, VMEM, VMEM],
        out_specs=VMEM,
        compiler_params=PARAMS,
        name="margin_parts",
    )(own, before, inner)


def total_kernel(points, partial_ref, out_ref):
    total = partial_ref[0]
    for shard in range(1, partial_ref.shape[0]):
        total = total + partial_ref[shard]
    total = total / points
    for shard in range(partial_ref.shape[0]):
        out_ref[shard] = total


def total_for_all(partial, points):
    return pl.pallas_call(
        functools.partial(total_kernel, points),
        out_shape=jax.ShapeDtypeStruct(partial.shape, F32),
        in_specs=[VMEM],
        out_specs=VMEM,
        compiler_params=PARAMS,
        name="total_for_all",
    )(partial)


def exchange(array):
    return lax.all_to_all(array, "chan", split_axis=0, concat_axis=0, tiled=True)


YS = 8
ENDS = (0, 3, 4, 7)


def place(position):
    return position // (2 * YS), position // 2 % YS, position % 2


def spot(x, y, core):
    return (x * YS + y) * 2 + core


def levels(xs):
    result = [
        (lambda x, y: (x, y ^ 1), range(YS), ("y", 0)),
        (lambda x, y: (x, y ^ 2), ENDS, ("y", 1)),
        (lambda x, y: (x, YS - 1 - y), ENDS, ("y", 2)),
    ]
    for bit in range(xs.bit_length() - 1):
        mask = 2 ** (bit + 1) - 1
        result.append((lambda x, y, mask=mask: (x ^ mask, y), ENDS, ("x", bit)))
    return result


def per_device(surface_functions, channel_rates, coupling):
    sectors, rows, points = surface_functions.shape
    n = channel_rates.shape[1]
    shards = lax.axis_size("chan")
    count = lax.axis_size("sector")
    position = lax.axis_index("sector")
    plan = levels(count // (2 * YS))
    own = exchange(shares(surface_functions, shards))
    own, position, shard, channel_rates = lax.optimization_barrier(
        (own, position, lax.axis_index("chan"), channel_rates)
    )
    x, y, core = place(position)
    at_end = (y == ENDS[0]) | (y == ENDS[1]) | (y == ENDS[2]) | (y == ENDS[3])
    words = [position, jnp.int32(count), core, shard]
    for _, takers, (axis, bit) in plan:
        words.append(jnp.int32(1) if len(takers) == YS else at_end.astype(jnp.int32))
        words.append((x if axis == "x" else y) >> bit & 1)
    across, along = plan[-1][0](x, y)
    words.append((across * YS + along) // 2)
    flags = jnp.stack([jnp.asarray(word, jnp.int32) for word in words])

    step = 1.0 / (sectors * count)
    cot = channel_rates / jnp.tanh(channel_rates * step)
    csc = channel_rates / jnp.sinh(channel_rates * step)

    before = lax.ppermute(own[:, sectors - 1], "sector", [(i, i + 1) for i in range(count - 1)])
    inner, cot, csc, flags, before = lax.optimization_barrier((inner_parts(own), cot, csc, flags, before))
    partial = exchange(margin_parts(own, before, inner))
    margin = exchange(total_for_all(partial, points))

    packed = leaf(flags, margin, cot, csc, coupling)
    cores = [(i, i ^ 1) for i in range(count)]
    packed, send = core_merge(flags, packed, lax.ppermute(packed, "sector", cores))
    wide = n // count
    for level, (partner, takers, _) in enumerate(plan):
        pairs = []
        for i in range(count):
            xi, yi, ci = place(i)
            if yi in takers:
                pairs.append((spot(*partner(xi, yi), ci), i))
        came = lax.ppermute(send, "sector", pairs)
        swapped = lax.ppermute(came, "sector", cores)
        if level < len(plan) - 1:
            last = (rows, 4 * wide) if level == len(plan) - 2 else None
            packed, send = chip_merge(level, last, flags, packed, came, swapped)
        else:
            mine, for_next = last_merge(level, flags, packed, came, swapped, wide, rows)
    pairs = []
    for i in range(count):
        xi, yi, ci = place(i)
        if yi not in ENDS:
            pairs.append((spot(xi, yi ^ 1, ci), i))
    brought = lax.ppermute(for_next, "sector", pairs)
    result = mine + brought
    return tuple(result[i].T for i in range(3))


def solution(mesh):
    placed = (P("sector", "chan", None), P("sector", None), P("sector", None, None))
    return jax.shard_map(
        per_device,
        mesh=mesh,
        in_specs=placed,
        out_specs=(P("chan", "sector"), P("chan", "sector"), P("chan", "sector")),
        check_vma=False,
    )
```

```python
import functools

import jax
import jax.numpy as jnp
from jax import lax
from jax.experimental import pallas as pl
from jax.experimental.pallas import tpu as pltpu
from jax.sharding import PartitionSpec as P

F32 = jnp.float32
BF16 = jnp.bfloat16
NN = (((1,), (0,)), ((), ()))
NT = (((1,), (1,)), ((), ()))
TN = (((0,), (0,)), ((), ()))
TOLERANCE = 1e-5
STEPS = 8
SQUARINGS = (3, 3, 4, 5, 6, 7, 7)
WORK = pl.CostEstimate(flops=10**9, bytes_accessed=2 * 10**6, transcendentals=0)
PARAMS = pltpu.CompilerParams(vmem_limit_bytes=32 * 2**20)
VMEM = pl.BlockSpec(memory_space=pltpu.VMEM)
SMEM = pl.BlockSpec(memory_space=pltpu.SMEM)


def parts(x):
    high = x.astype(BF16)
    rest = x - high.astype(F32)
    middle = rest.astype(BF16)
    return high, middle, (rest - middle.astype(F32)).astype(BF16)


def dot1(a, b, dims=NN):
    return lax.dot_general(a, b, dims, preferred_element_type=F32)


def dot3(a, b, dims=NN):
    return dot1(a[0], b[0], dims) + (dot1(a[0], b[1], dims) + dot1(a[1], b[0], dims))


def dot6(a, b, dims=NN):
    low = dot1(a[0], b[2], dims) + dot1(a[1], b[1], dims) + dot1(a[2], b[0], dims)
    return dot1(a[0], b[0], dims) + ((dot1(a[0], b[1], dims) + dot1(a[1], b[0], dims)) + low)


def grid_of(n):
    return (
        lax.broadcasted_iota(jnp.int32, (n, n), 0),
        lax.broadcasted_iota(jnp.int32, (n, n), 1),
    )


def unit(n):
    row, column = grid_of(n)
    return jnp.where(row == column, F32(1), F32(0))


def step_size(d):
    return 1.9 / jnp.max(jnp.sum(jnp.abs(d), axis=0, keepdims=True), axis=1, keepdims=True)


def first_inverse(d, squarings):
    n = d.shape[0]
    one = unit(n)
    alpha = step_size(d)
    e = one - alpha * d
    c = jnp.sum(jnp.sum(e * one, axis=0, keepdims=True), axis=1, keepdims=True) / n
    f = e - c * one
    p, y = 1 + c, f
    for _ in range(squarings):
        rounded = f.astype(BF16)
        f = 2 * c * f + dot1(rounded, rounded)
        c = c * c
        y = p * f + (1 + c) * y + dot1(y.astype(BF16), f.astype(BF16))
        p = p * (1 + c)
    return alpha * (p * one + y)


def newton(d_parts, x, dot):
    x_parts = parts(x)
    residual = unit(x.shape[0]) - dot(d_parts, x_parts)
    return x + (dot1(x_parts[0], residual.astype(BF16)) if dot is dot3 else dot3(x_parts, parts(residual))), residual


def combine(left, right, x, out_ref):
    b1, b2, x = parts(left(1)), parts(right(1)), parts(x)
    w1, w2 = parts(dot6(b1, x)), parts(dot6(x, b2))
    out_ref[0] = left(0) - dot6(w1, b1, NT)
    out_ref[1] = dot6(w1, b2)
    out_ref[2] = right(2) - dot6(b2, w2, TN)


def merge_blocks(d, depth, d_ref, x_ref, finish):
    d_ref[...] = d
    x_ref[...], _ = newton(parts(d), first_inverse(d, SQUARINGS[min(depth, len(SQUARINGS) - 1)]), dot3)

    def going(state):
        return jnp.logical_and(state[0] < 9 * STEPS, jnp.logical_not(state[1] < TOLERANCE))

    def again(state):
        @pl.when(state[0] == STEPS)
        def _():
            x_ref[...] = step_size(d_ref[...]) * unit(d_ref.shape[0])

        x_parts = parts(x_ref[...])
        residual = unit(d_ref.shape[0]) - dot6(parts(d_ref[...]), x_parts)
        rounded = residual.astype(BF16)
        x_ref[...] = x_ref[...] + dot1(x_parts[0], rounded)

        @pl.when(state[0] > 0)
        def _():
            rest = (residual - rounded.astype(F32)).astype(BF16)
            x_ref[...] = x_ref[...] + (dot1(x_parts[0], rest) + dot1(x_parts[1], rounded))

        finish(x_ref[...])
        return state[0] + 1, jnp.sum(residual * residual)

    lax.while_loop(going, again, (0, F32(1)))


def pack(core, out_ref, send_ref):
    n = out_ref.shape[-1]
    row, column = grid_of(n)
    last = out_ref[2]
    both = jnp.where(row >= column, out_ref[0], last)
    send_ref[0:n] = jnp.where(core == 0, both, out_ref[1])
    diagonal = jnp.sum(jnp.where(row == column, last, F32(0)), axis=0, keepdims=True)
    send_ref[n : n + 8] = jnp.broadcast_to(diagonal, (8, n))


def leaf_kernel(flags_ref, margin_ref, cot_ref, csc_ref, coupling_ref, out_ref, d_ref, x_ref, a_ref, b_ref, c_ref):
    n = d_ref.shape[0]
    row, column = grid_of(n)
    half_step = 0.5 / (2 * flags_ref[1]).astype(F32)

    def sector(s):
        margin = margin_ref[:, s].reshape(n, n)
        if s == 0:
            margin = jnp.where(flags_ref[0] == 0, unit(n), margin)
        inner = jnp.where(row == column, cot_ref[s : s + 1, :], F32(0)) + half_step * coupling_ref[s].astype(F32)
        m = parts(margin)
        a_ref[s] = dot6(parts(dot6(m, parts(inner))), m, NT)
        b_ref[s] = margin * csc_ref[s : s + 1, :]
        c_ref[s] = inner

    sector(1)
    sector(0)
    blocks = (a_ref, b_ref, c_ref)
    merge_blocks(
        c_ref[0] + a_ref[1], 0, d_ref, x_ref,
        lambda x: combine(lambda i: blocks[i][0], lambda i: blocks[i][1], x, out_ref),
    )


def leaf(flags, margin, cot, csc, coupling):
    n = coupling.shape[-1]
    return pl.pallas_call(
        leaf_kernel,
        out_shape=jax.ShapeDtypeStruct((3, n, n), F32),
        in_specs=[SMEM, VMEM, VMEM, VMEM, VMEM],
        out_specs=VMEM,
        scratch_shapes=[pltpu.VMEM((n, n), F32)] * 2 + [pltpu.VMEM((2, n, n), F32)] * 3,
        compiler_params=PARAMS,
        name="leaf",
    )(flags, margin, cot, csc, coupling)


def sides(upper, own_ref, other_ref):
    return (
        lambda i: jnp.where(upper, other_ref[i], own_ref[i]),
        lambda i: jnp.where(upper, own_ref[i], other_ref[i]),
    )


def merge_refs(upper, own_ref, other_ref, depth, out_ref, d_ref, x_ref, after):
    left, right = sides(upper, own_ref, other_ref)

    def finish(x):
        combine(left, right, x, out_ref)
        after()

    merge_blocks(left(2) + right(0), depth, d_ref, x_ref, finish)


def core_kernel(flags_ref, own_ref, other_ref, out_ref, send_ref, d_ref, x_ref):
    core = flags_ref[2]
    merge_refs(core == 1, own_ref, other_ref, 1, out_ref, d_ref, x_ref, lambda: pack(core, out_ref, send_ref))


def core_merge(flags, own, other):
    n = own.shape[-1]
    return pl.pallas_call(
        core_kernel,
        out_shape=(jax.ShapeDtypeStruct((3, n, n), F32), jax.ShapeDtypeStruct((n + 8, n), F32)),
        in_specs=[SMEM, VMEM, VMEM],
        out_specs=(VMEM, VMEM),
        scratch_shapes=[pltpu.VMEM((n, n), F32)] * 2,
        compiler_params=PARAMS,
        name="core_merge",
    )(flags, own, other)


def unpack(core, came_ref, swapped_ref, other_ref):
    n = other_ref.shape[-1]
    row, column = grid_of(n)
    both = jnp.where(core == 0, came_ref[0:n], swapped_ref[0:n])
    diagonal = jnp.where(core == 0, came_ref[n : n + 1], swapped_ref[n : n + 1])
    turned = both.T
    other_ref[0] = jnp.where(row >= column, both, turned)
    other_ref[1] = jnp.where(core == 0, swapped_ref[0:n], came_ref[0:n])
    other_ref[2] = jnp.where(row == column, diagonal, jnp.where(row < column, both, turned))


def pack_for_last(flags_ref, level, rows, block, out_ref, send_ref, turned_ref):
    n = out_ref.shape[-1]
    half = n // 2
    row, column = grid_of(n)
    both = jnp.where(row >= column, out_ref[0], out_ref[2])
    send_ref[0:half] = jnp.where(flags_ref[2] == 0, both[:half], both[half:])
    diagonal = jnp.sum(jnp.where(row == column, out_ref[2], F32(0)), axis=0, keepdims=True)
    send_ref[half : half + 8] = jnp.broadcast_to(diagonal, (8, n))
    turned_ref[...] = jnp.where(flags_ref[5 + 2 * level] == 1, out_ref[1].T, out_ref[1])
    first = flags_ref[4 + 2 * (level + 1)]
    send_ref[half + 8 : half + 8 + block] = turned_ref[pl.ds(pl.multiple_of(first * block, block), block), :]
    mine = pl.ds(pl.multiple_of(flags_ref[3] * rows, rows), rows)
    send_ref[half + 8 + block : half + 8 + block + rows] = turned_ref[mine, :]


def chip_kernel(level, last, flags_ref, own_ref, came_ref, swapped_ref, out_ref, send_ref, d_ref, x_ref, other_ref, turned_ref):
    core = flags_ref[2]
    active = flags_ref[4 + 2 * level] == 1

    def send_off():
        if last is None:
            pack(core, out_ref, send_ref)
        else:
            pack_for_last(flags_ref, level + 1, *last, out_ref, send_ref, turned_ref)

    @pl.when(active)
    def _():
        unpack(core, came_ref, swapped_ref, other_ref)
        merge_refs(
            flags_ref[5 + 2 * level] == 1, own_ref, other_ref, level + 2, out_ref, d_ref, x_ref, send_off
        )

    @pl.when(jnp.logical_not(active))
    def _():
        out_ref[...] = own_ref[...]
        send_ref[...] = jnp.zeros_like(send_ref)


def chip_merge(level, last, flags, own, came, swapped):
    n = own.shape[-1]
    sent = n + 8 if last is None else n // 2 + 8 + sum(last)
    return pl.pallas_call(
        functools.partial(chip_kernel, level, last),
        out_shape=(jax.ShapeDtypeStruct((3, n, n), F32), jax.ShapeDtypeStruct((sent, n), F32)),
        in_specs=[SMEM, VMEM, VMEM, VMEM],
        out_specs=(VMEM, VMEM),
        scratch_shapes=[pltpu.VMEM((n, n), F32)] * 2 + [pltpu.VMEM((3, n, n), F32), pltpu.VMEM((n, n), F32)],
        compiler_params=PARAMS,
        name="chip_merge",
    )(flags, own, came, swapped)


def last_kernel(level, flags_ref, own_ref, came_ref, swapped_ref, mine_ref, next_ref, d_ref, x_ref, turned_ref, other_ref):
    n = d_ref.shape[0]
    core = flags_ref[2]
    wide, rows = mine_ref.shape[1:]
    active = flags_ref[4 + 2 * level] == 1
    upper = flags_ref[5 + 2 * level] == 1
    chip = flags_ref[0] // 2
    depth = 4 * wide
    block = pl.ds(pl.multiple_of(chip // 2 * depth, depth), depth)
    mine = pl.ds(pl.multiple_of(flags_ref[3] * rows, rows), rows)
    half = n // 2

    def cut(wanted, array):
        piece = array[:wide]
        for i in range(1, 4):
            piece = jnp.where(wanted == i, array[i * wide : (i + 1) * wide], piece)
        return piece

    def at_mine(array):
        return pltpu.roll(array, (n - flags_ref[3] * rows) % n, axis=1)[:, :rows]

    @pl.when(active)
    def _():
        row, column = grid_of(n)
        x_ref[0:half] = jnp.where(core == 0, came_ref[0:half], swapped_ref[0:half])
        x_ref[half:n] = jnp.where(core == 0, swapped_ref[0:half], came_ref[0:half])
        both = x_ref[...]
        turned = both.T
        other_ref[0] = jnp.where(row >= column, both, turned)
        other_ref[1] = jnp.where(row == column, came_ref[half : half + 1], jnp.where(row < column, both, turned))
        turned_ref[...] = jnp.where(upper, own_ref[1].T, own_ref[1])
        d = jnp.where(upper, other_ref[1] + own_ref[0], own_ref[2] + other_ref[0])

        def finish(x):
            x = parts(x)
            came_block = came_ref[half + 8 : half + 8 + depth]
            came_mine = came_ref[half + 8 + depth : half + 8 + depth + rows]
            own_block, own_mine = turned_ref[block, :], turned_ref[mine, :]
            b1_block, b2_block = jnp.where(upper, came_block, own_block), jnp.where(upper, own_block, came_block)
            b1 = parts(jnp.where(upper, came_mine, own_mine))
            b2 = parts(jnp.where(upper, own_mine, came_mine))
            w1, w2 = parts(dot6(parts(b1_block), x)), parts(dot6(parts(b2_block), x))
            a_rows = jnp.where(upper, other_ref[0, block, :], own_ref[0, block, :])
            c_rows = jnp.where(upper, own_ref[2, block, :], other_ref[1, block, :])
            results = (at_mine(a_rows) - dot6(w1, b1, NT), dot6(w2, b1, NT), at_mine(c_rows) - dot6(w2, b2, NT))
            for i, result in enumerate(results):
                mine_ref[i] = cut(chip % 2 * 2 + core, result)
                next_ref[i] = cut((1 - chip % 2) * 2 + core, result)

        merge_blocks(d, level + 2, d_ref, x_ref, finish)

    @pl.when(jnp.logical_not(active))
    def _():
        mine_ref[...] = jnp.zeros_like(mine_ref)
        next_ref[...] = jnp.zeros_like(next_ref)


def last_merge(level, flags, own, came, swapped, wide, rows):
    n = own.shape[-1]
    return pl.pallas_call(
        functools.partial(last_kernel, level),
        out_shape=(jax.ShapeDtypeStruct((3, wide, rows), F32),) * 2,
        in_specs=[SMEM, VMEM, VMEM, VMEM],
        out_specs=(VMEM, VMEM),
        scratch_shapes=[pltpu.VMEM((n, n), F32)] * 3 + [pltpu.VMEM((2, n, n), F32)],
        compiler_params=PARAMS,
        name="last_merge",
    )(flags, own, came, swapped)


def shares_kernel(whole_ref, out_ref):
    depth = out_ref.shape[-1]
    for shard in range(out_ref.shape[0]):
        out_ref[shard] = whole_ref[:, :, shard * depth : (shard + 1) * depth]


def shares(surface_functions, shards):
    sectors, rows, points = surface_functions.shape
    return pl.pallas_call(
        shares_kernel,
        out_shape=jax.ShapeDtypeStruct((shards, sectors, rows, points // shards), BF16),
        in_specs=[VMEM],
        out_specs=VMEM,
        compiler_params=PARAMS,
        name="shares",
    )(surface_functions)


def inner_kernel(own_ref, out_ref):
    shards, _, rows, depth = own_ref.shape
    n = shards * rows
    first = own_ref[:, 0].reshape(n, depth)
    second = own_ref[:, 1].reshape(n, depth)
    out_ref[...] = dot1(first, second, NT).reshape(shards, rows, n)


def margin_kernel(own_ref, before_ref, inner_ref, out_ref):
    shards, _, rows, depth = own_ref.shape
    n = shards * rows
    first = own_ref[:, 0].reshape(n, depth)
    out_ref[:, 0] = dot1(before_ref[...].reshape(n, depth), first, NT).reshape(shards, rows, n)
    out_ref[:, 1] = inner_ref[...]


def inner_parts(own):
    shards, _, rows, _ = own.shape
    return pl.pallas_call(
        inner_kernel,
        out_shape=jax.ShapeDtypeStruct((shards, rows, shards * rows), F32),
        in_specs=[VMEM],
        out_specs=VMEM,
        compiler_params=PARAMS,
        cost_estimate=WORK,
        name="inner_parts",
    )(own)


def margin_parts(own, before, inner):
    shards, sectors, rows, _ = own.shape
    return pl.pallas_call(
        margin_kernel,
        out_shape=jax.ShapeDtypeStruct((shards, sectors, rows, shards * rows), F32),
        in_specs=[VMEM, VMEM, VMEM],
        out_specs=VMEM,
        compiler_params=PARAMS,
        name="margin_parts",
    )(own, before, inner)


def total_kernel(points, partial_ref, out_ref):
    total = partial_ref[0]
    for shard in range(1, partial_ref.shape[0]):
        total = total + partial_ref[shard]
    total = total / points
    for shard in range(partial_ref.shape[0]):
        out_ref[shard] = total


def total_for_all(partial, points):
    return pl.pallas_call(
        functools.partial(total_kernel, points),
        out_shape=jax.ShapeDtypeStruct(partial.shape, F32),
        in_specs=[VMEM],
        out_specs=VMEM,
        compiler_params=PARAMS,
        name="total_for_all",
    )(partial)


def exchange(array):
    return lax.all_to_all(array, "chan", split_axis=0, concat_axis=0, tiled=True)


YS = 8
ENDS = (0, 3, 4, 7)


def place(position):
    return position // (2 * YS), position // 2 % YS, position % 2


def spot(x, y, core):
    return (x * YS + y) * 2 + core


def levels(xs):
    result = [
        (lambda x, y: (x, y ^ 1), range(YS), ("y", 0)),
        (lambda x, y: (x, y ^ 2), ENDS, ("y", 1)),
        (lambda x, y: (x, YS - 1 - y), ENDS, ("y", 2)),
    ]
    for bit in range(xs.bit_length() - 1):
        mask = 2 ** (bit + 1) - 1
        result.append((lambda x, y, mask=mask: (x ^ mask, y), ENDS, ("x", bit)))
    return result


def per_device(surface_functions, channel_rates, coupling):
    sectors, rows, points = surface_functions.shape
    n = channel_rates.shape[1]
    shards = lax.axis_size("chan")
    count = lax.axis_size("sector")
    position = lax.axis_index("sector")
    plan = levels(count // (2 * YS))
    own = exchange(shares(surface_functions, shards))
    own, position, shard, channel_rates = lax.optimization_barrier(
        (own, position, lax.axis_index("chan"), channel_rates)
    )
    x, y, core = place(position)
    at_end = (y == ENDS[0]) | (y == ENDS[1]) | (y == ENDS[2]) | (y == ENDS[3])
    words = [position, jnp.int32(count), core, shard]
    for _, takers, (axis, bit) in plan:
        words.append(jnp.int32(1) if len(takers) == YS else at_end.astype(jnp.int32))
        words.append((x if axis == "x" else y) >> bit & 1)
    across, along = plan[-1][0](x, y)
    words.append((across * YS + along) // 2)
    flags = jnp.stack([jnp.asarray(word, jnp.int32) for word in words])

    step = 1.0 / (sectors * count)
    cot = channel_rates / jnp.tanh(channel_rates * step)
    csc = channel_rates / jnp.sinh(channel_rates * step)

    before = lax.ppermute(own[:, sectors - 1], "sector", [(i, i + 1) for i in range(count - 1)])
    inner, cot, csc, flags, before = lax.optimization_barrier((inner_parts(own), cot, csc, flags, before))
    partial = exchange(margin_parts(own, before, inner))
    margin = exchange(total_for_all(partial, points))

    packed = leaf(flags, margin, cot, csc, coupling)
    cores = [(i, i ^ 1) for i in range(count)]
    packed, send = core_merge(flags, packed, lax.ppermute(packed, "sector", cores))
    wide = n // count
    for level, (partner, takers, _) in enumerate(plan):
        pairs = []
        for i in range(count):
            xi, yi, ci = place(i)
            if yi in takers:
                pairs.append((spot(*partner(xi, yi), ci), i))
        came = lax.ppermute(send, "sector", pairs)
        swapped = lax.ppermute(came, "sector", cores)
        if level < len(plan) - 1:
            last = (rows, 4 * wide) if level == len(plan) - 2 else None
            packed, send = chip_merge(level, last, flags, packed, came, swapped)
        else:
            mine, for_next = last_merge(level, flags, packed, came, swapped, wide, rows)
    pairs = []
    for i in range(count):
        xi, yi, ci = place(i)
        if yi not in ENDS:
            pairs.append((spot(xi, yi ^ 1, ci), i))
    brought = lax.ppermute(for_next, "sector", pairs)
    result = mine + brought
    return tuple(result[i].T for i in range(3))


def solution(mesh):
    placed = (P("sector", "chan", None), P("sector", None), P("sector", None, None))
    return jax.shard_map(
        per_device,
        mesh=mesh,
        in_specs=placed,
        out_specs=(P("chan", "sector"), P("chan", "sector"), P("chan", "sector")),
        check_vma=False,
    )
```
